256 devices in a mesh: gx: 8 (over z), gy: 32 (over x, y, core).
Axes of the slice: x: 4, y: 4, z: 8, core: 2. Of those that a mesh axis runs over, the one named last changes fastest.
Arguments:
- starting_heat_state: float32 [128, 1024, 128], P('gx', 'gy'), may hold values from -5 to 5
- material_zone_ids: int32 [64, 512, 64], P('gx', 'gy'), may hold values from 0 to 15
- zone_diffusivity_lookup: float32 [16], replicated, may hold values from 1 to 10
Outputs:
- new_temperature: float32 [128, 1024, 128], P('gx', 'gy')
The draws below stay inside these ranges and needn't reach their ends.
All inputs are finite; a program needn't handle non-finite values.
Results may differ from the reference program's by a relative error of at most 0.017.
Values sent between devices are 32-bit elements; how exact they have to be, the bound alone decides.
No kernel may reach another device: no remote copies, remote signals or barrier semaphores. Data moves between devices by JAX's collectives and lax.ppermute only.
A program may use at most 64 MiB of HBM per device.

```python
import math
import jax
import jax.numpy as jnp
from jax import lax

STEPS = 1
REGIONS = 16
NX = 128
NY = 1024
NZ = 128


def smooth_field(key, amplitude_one):
    phase_key, freq_key = jax.random.split(jax.random.fold_in(key, 7))
    phases = jax.random.uniform(phase_key, (4,), jnp.float32, 0.0, 2.0 * math.pi)
    freqs = jax.random.randint(freq_key, (2,), 3, 6).astype(jnp.float32)
    along_x = jnp.arange(NX, dtype=jnp.float32) / NX
    along_y = jnp.arange(NY, dtype=jnp.float32) / NY
    along_z = jnp.arange(NZ, dtype=jnp.float32) / NZ
    wave_x = jnp.sin(2.0 * math.pi * along_x + phases[0])
    wave_y = jnp.cos(2.0 * math.pi * freqs[0] * along_y + phases[1])
    wave_y2 = jnp.sin(2.0 * math.pi * freqs[1] * along_y + phases[2])
    wave_z = jnp.cos(2.0 * math.pi * along_z + phases[3])
    first_term = amplitude_one * wave_x[:, None, None] * wave_y[None, :, None] * jnp.ones((1, 1, NZ), jnp.float32)
    second_term = jnp.ones((NX, 1, 1), jnp.float32) * wave_y2[None, :, None] * wave_z[None, None, :]
    return first_term + second_term


def draw_starting_heat_state(key, part):
    grid_shape = (NX, NY, NZ)
    rough_key = jax.random.fold_in(key, 3)
    rough = jnp.clip(jax.random.normal(rough_key, grid_shape, jnp.float32), -2.0, 2.0)
    values = rough + smooth_field(key, 1.5)
    return jnp.clip(values, -5.0, 5.0)


def touch_ends(values, key, smallest, largest):
    index_at = [jax.random.randint(jax.random.fold_in(key, axis), (), 0, length) for axis, length in enumerate(values.shape)]
    widest = values.shape.index(max(values.shape))
    next_to = index_at[:widest] + [(index_at[widest] + 1) % values.shape[widest]] + index_at[widest + 1:]
    return values.at[tuple(index_at)].set(smallest).at[tuple(next_to)].set(largest)


def setup_inputs(seed: int = 0) -> dict:
    key_of = jax.random.split(jax.random.key(seed), 4)
    starting_heat_state = draw_starting_heat_state(jax.random.fold_in(key_of[3], 71), 0)
    material_zone_ids = touch_ends(jax.random.randint(key_of[1], (NX // 2, NY // 2, NZ // 2), 0, REGIONS), jax.random.fold_in(key_of[1], 1), 0, REGIONS - 1).astype(jnp.int32)
    zone_diffusivity_lookup = jnp.clip(jnp.exp(jax.random.uniform(key_of[2], (REGIONS,), jnp.float32, math.log(1.0), math.log(10.0))), 1.0, 10.0)
    return {"starting_heat_state": starting_heat_state, "material_zone_ids": material_zone_ids, "zone_diffusivity_lookup": zone_diffusivity_lookup}


face_scale = 2000.0
vertical_scale = 0.5


def thomas(lower, diagonal, upper, right_side):
    def forward(previous, entries):
        c_prev, d_prev = previous
        low_row, diag_row, up_row, side_row = entries
        divisor = diag_row - low_row * c_prev
        c_new = up_row / divisor
        d_new = (side_row - low_row * d_prev) / divisor
        return (c_new, d_new), (c_new, d_new)

    zeroes = jnp.zeros_like(right_side[0])
    _, (c_all, d_all) = lax.scan(forward, (zeroes, zeroes), (lower, diagonal, upper, right_side))

    def backward(x_next, entries):
        c_row, d_row = entries
        x_row = d_row - c_row * x_next
        return x_row, x_row

    _, solved = lax.scan(backward, zeroes, (c_all, d_all), reverse=True)
    return solved


def face_pair(thermal_diffusivity_map, solve_direction_index):
    scale_here = face_scale if solve_direction_index < 2 else vertical_scale
    border_amounts = [(0, 0), (0, 0), (0, 0)]
    border_amounts[solve_direction_index] = (1, 1)
    bordered_array = jnp.pad(thermal_diffusivity_map, border_amounts)
    domain_span = thermal_diffusivity_map.shape[solve_direction_index]
    leftward_neighbour = scale_here * (lax.slice_in_dim(bordered_array, 0, domain_span, axis=solve_direction_index) + thermal_diffusivity_map)
    rightward_neighbour = scale_here * (lax.slice_in_dim(bordered_array, 2, domain_span + 2, axis=solve_direction_index) + thermal_diffusivity_map)
    return leftward_neighbour, rightward_neighbour


def directional_operator_part(current_heat_state, thermal_diffusivity_map, solve_direction_index):
    leftward_neighbour, rightward_neighbour = face_pair(thermal_diffusivity_map, solve_direction_index)
    border_amounts = [(0, 0), (0, 0), (0, 0)]
    border_amounts[solve_direction_index] = (1, 1)
    bordered_array = jnp.pad(current_heat_state, border_amounts)
    domain_span = current_heat_state.shape[solve_direction_index]
    beneath_neighbour_plane = lax.slice_in_dim(bordered_array, 0, domain_span, axis=solve_direction_index)
    higher_neighbour_plane = lax.slice_in_dim(bordered_array, 2, domain_span + 2, axis=solve_direction_index)
    return rightward_neighbour * (higher_neighbour_plane - current_heat_state) - leftward_neighbour * (current_heat_state - beneath_neighbour_plane)


def solve_lines(thermal_diffusivity_map, right_side, solve_direction_index):
    leftward_neighbour, rightward_neighbour = face_pair(thermal_diffusivity_map, solve_direction_index)
    leftward_neighbour = jnp.moveaxis(leftward_neighbour, solve_direction_index, 0)
    rightward_neighbour = jnp.moveaxis(rightward_neighbour, solve_direction_index, 0)
    moved_side = jnp.moveaxis(right_side, solve_direction_index, 0)
    lower = -0.5 * leftward_neighbour
    upper = -0.5 * rightward_neighbour
    diagonal = 1.0 + 0.5 * (leftward_neighbour + rightward_neighbour)
    return jnp.moveaxis(thomas(lower, diagonal, upper, moved_side), 0, solve_direction_index)


def reference(starting_heat_state, material_zone_ids, zone_diffusivity_lookup):
    block_cond = zone_diffusivity_lookup[material_zone_ids]
    thermal_diffusivity_map = jnp.repeat(jnp.repeat(jnp.repeat(block_cond, 2, 0), 2, 1), 2, 2)
    current_heat_state = starting_heat_state
    for region_portion in range(STEPS):
        increment_update = directional_operator_part(current_heat_state, thermal_diffusivity_map, 0)
        increment_update = increment_update + directional_operator_part(current_heat_state, thermal_diffusivity_map, 1)
        increment_update = increment_update + directional_operator_part(current_heat_state, thermal_diffusivity_map, 2)
        increment_update = solve_lines(thermal_diffusivity_map, increment_update, 0)
        increment_update = solve_lines(thermal_diffusivity_map, increment_update, 1)
        increment_update = solve_lines(thermal_diffusivity_map, increment_update, 2)
        current_heat_state = current_heat_state + increment_update
    return current_heat_state
```

```python
import jax
import jax.numpy as jnp
from jax import lax
from jax.experimental import pallas as pl
from jax.experimental.pallas import tpu as pltpu
from jax.sharding import PartitionSpec as P

NX, NY, NZ = 16, 32, 128
MX, MY = NX // 2, NY // 2
XROWS = 104
YROWS = 48
f32 = jnp.float32


def lanes(shape):
    return lax.broadcasted_iota(jnp.int32, shape, 1)


def rows_of(shape):
    return lax.broadcasted_iota(jnp.int32, shape, 0)


def pack(first, second):
    return jnp.where(lanes(first.shape) % 2 == 0, first, second)


def unpack(both):
    even = lanes(both.shape) % 2 == 0
    first = jnp.where(even, both, pltpu.roll(both, 1, 1))
    second = jnp.where(even, pltpu.roll(both, NZ - 1, 1), both)
    return first, second


def through(near, far, link, beyond, leak, near_src, far_src, src):
    total = far + leak
    q = total + link
    cross = total * link
    f = beyond / ((near + beyond) * q + cross)
    new_leak = f * (near * q + cross)
    new_src = [f * (n * q + (e + s) * link) for n, e, s in zip(near_src, far_src, src)]
    return new_leak, new_src


def two_nodes(first, last, link, first_src, last_src):
    inv = 1.0 / (first * last + link * (first + last))
    low = [((last + link) * a + link * b) * inv for a, b in zip(first_src, last_src)]
    high = [((first + link) * b + link * a) * inv for a, b in zip(first_src, last_src)]
    return low, high


def eliminate(conduct, put):
    alpha = jnp.ones_like(conduct[0])
    beta = jnp.ones_like(conduct[0])
    link = conduct[0]
    for t in range(1, len(conduct)):
        g = conduct[t]
        inv = 1.0 / (link + beta + g)
        hd = link * inv
        gd = g * inv
        put(t - 1, gd, hd, inv)
        alpha = alpha + beta * hd
        link = link * gd
        beta = 1.0 + beta * gd
    return alpha, beta, link


def prepare_kernel(ids_ref, table_ref, heat_ref, k_ref, low_ref, high_ref, wide):
    ids = ids_ref[...]
    k = jnp.zeros(ids.shape, f32)
    for region in range(table_ref.shape[0]):
        k = jnp.where(ids == region, table_ref[region], k)
    wide[...] = jnp.zeros(wide.shape, f32)
    wide[:, : NZ // 2] = k
    index = lanes(wide.shape) // 2
    k_ref[...] = jnp.take_along_axis(wide[...], index, axis=1, mode="promise_in_bounds")
    low_ref[:NX] = heat_ref[pl.ds(0, NX, stride=NY), :]
    high_ref[:NX] = heat_ref[pl.ds(NY - 1, NX, stride=NY), :]
    low_ref[NX:] = k_ref[pl.ds(0, MX, stride=MY), :]
    high_ref[NX:] = k_ref[pl.ds(MY - 1, MX, stride=MY), :]


def matrix_kernel(
    k_ref, gx_ref, hx_ref, ix_ref, px_ref, gy_ref, hy_ref, iy_ref, my_ref, za_ref, zc_ref, zi_ref
):
    at_x, at_y = lax.axis_index("gx"), lax.axis_index("gy")
    last_x, last_y = lax.axis_size("gx") - 1, lax.axis_size("gy") - 1

    def chain(k):
        joints = []
        for m in range(len(k)):
            joints.append(2000.0 * k[m])
            if m + 1 < len(k):
                joints.append(1000.0 * (k[m] + k[m + 1]))
        return joints

    kx = [k_ref[m * MY : (m + 1) * MY, :] for m in range(MX)]

    def put_x(t, gd, hd, inv):
        gx_ref[t * MY : (t + 1) * MY, :] = gd
        hx_ref[t * MY : (t + 1) * MY, :] = hd
        ix_ref[t * MY : (t + 1) * MY, :] = inv

    alpha, beta, link = eliminate(chain(kx), put_x)
    alpha = alpha + jnp.where(at_x == 0, 1000.0, 0.0) * kx[0]
    beta = beta + jnp.where(at_x == last_x, 1000.0, 0.0) * kx[-1]
    px_ref[0:16, :] = pack(alpha, beta)
    px_ref[16:32, :] = pack(link, kx[0])
    px_ref[32:40, :] = pack(kx[-1][:8], kx[-1][8:])

    ky = [k_ref[pl.ds(n, MX, stride=MY), :] for n in range(MY)]

    def put_y(t, gd, hd, inv):
        gy_ref[t * MX : (t + 1) * MX, :] = gd
        hy_ref[t * MX : (t + 1) * MX, :] = hd
        iy_ref[t * MX : (t + 1) * MX, :] = inv

    alpha, beta, link = eliminate(chain(ky), put_y)
    my_ref[0:8, :] = alpha + jnp.where(at_y == 0, 1000.0, 0.0) * ky[0]
    my_ref[8:16, :] = beta + jnp.where(at_y == last_y, 1000.0, 0.0) * ky[-1]
    my_ref[16:24, :] = link

    group = 4
    for start in range(0, MY, group):
        k = jnp.concatenate(ky[start : start + group], 0)
        lane = lanes(k.shape)
        west = 0.25 * (k + jnp.where(lane == 0, 0.0, pltpu.roll(k, 1, 1)))
        east = 0.25 * (k + jnp.where(lane == NZ - 1, 0.0, pltpu.roll(k, NZ - 1, 1)))
        diag = 1.0 + (west + east)
        a = jnp.where(lane == 0, 0.0, west)
        c = jnp.where(lane == NZ - 1, 0.0, east)
        size = MX * group
        for s in range(7):
            step = 1 << s
            inv = 1.0 / diag
            low = a * pltpu.roll(inv, step, 1)
            high = c * pltpu.roll(inv, NZ - step, 1)
            at = s * MX * MY + start * MX
            za_ref[at : at + size, :] = low
            zc_ref[at : at + size, :] = high
            diag = diag - (low * pltpu.roll(c, step, 1) + high * pltpu.roll(a, NZ - step, 1))
            a = low * pltpu.roll(a, step, 1)
            c = high * pltpu.roll(c, NZ - step, 1)
        zi_ref[start * MX : start * MX + size, :] = 1.0 / diag


def right_side_kernel(heat_ref, k_ref, low_ref, high_ref, gx_ref, hx_ref, px_ref, send_ref, rb_ref):
    at_y = lax.axis_index("gy")
    inside_low = jnp.where(at_y == 0, 0.0, 1.0)
    inside_high = jnp.where(at_y == lax.axis_size("gy") - 1, 0.0, 1.0)
    shape = (MY, NZ)
    lane, row = lanes(shape), rows_of(shape)
    ra = None
    rb = None
    for m in range(MX):
        k = k_ref[m * MY : (m + 1) * MY, :]
        k_low = inside_low * low_ref[NX + m : NX + m + 1, :]
        k_high = inside_high * high_ref[NX + m : NX + m + 1, :]
        face_low = 2000.0 * (k + jnp.where(row == 0, k_low, pltpu.roll(k, 1, 0)))
        face_high = 2000.0 * (k + jnp.where(row == MY - 1, k_high, pltpu.roll(k, MY - 1, 0)))
        face_mid = 4000.0 * k
        west = 0.5 * (k + jnp.where(lane == 0, 0.0, pltpu.roll(k, 1, 1)))
        east = 0.5 * (k + jnp.where(lane == NZ - 1, 0.0, pltpu.roll(k, NZ - 1, 1)))
        middle = 2.0 - (west + east)
        west = jnp.where(lane == 0, 0.0, west)
        east = jnp.where(lane == NZ - 1, 0.0, east)
        for x in (2 * m, 2 * m + 1):
            even = heat_ref[pl.ds(x * NY, MY, stride=2), :]
            odd = heat_ref[pl.ds(x * NY + 1, MY, stride=2), :]
            before = jnp.where(row == 0, inside_low * low_ref[x : x + 1, :], pltpu.roll(odd, 1, 0))
            after = jnp.where(
                row == MY - 1, inside_high * high_ref[x : x + 1, :], pltpu.roll(even, MY - 1, 0)
            )
            flow = face_mid * (odd - even)
            r = []
            for v, along_y in (
                (even, flow - face_low * (even - before)),
                (odd, face_high * (after - odd) - flow),
            ):
                along_z = west * pltpu.roll(v, 1, 1) + east * pltpu.roll(v, NZ - 1, 1)
                r.append(along_y + (along_z + middle * v))
            if x == 0:
                ra = r
            elif x == 1:
                rb = r
            else:
                t = x - 2
                gd = gx_ref[t * MY : (t + 1) * MY, :]
                hd = hx_ref[t * MY : (t + 1) * MY, :]
                for q in range(2):
                    rb_ref[t * NY + q * MY : t * NY + (q + 1) * MY, :] = rb[q]
                ra = [a + b * hd for a, b in zip(ra, rb)]
                rb = [n + b * gd for n, b in zip(r, rb)]
    p = px_ref[...]
    for d in range(send_ref.shape[0]):
        send_ref[d, 0:16, :] = ra[0]
        send_ref[d, 16:32, :] = ra[1]
        send_ref[d, 32:48, :] = rb[0]
        send_ref[d, 48:64, :] = rb[1]
        send_ref[d, 64:104, :] = p


def x_solve_kernel(
    recv_ref, heat_ref, k_ref, low_ref, high_ref, rb_ref, gx_ref, hx_ref, ix_ref, gy_ref, hy_ref, my_ref,
    core_ref, mid_ref, rby_ref, first,
):
    at = lax.axis_index("gx")
    count = recv_ref.shape[0]

    def segment(d):
        alpha, beta = unpack(recv_ref[d, 64:80, :])
        link, k_first = unpack(recv_ref[d, 80:96, :])
        k_last = jnp.concatenate(unpack(recv_ref[d, 96:104, :]), 0)
        ra = [recv_ref[d, 0:16, :], recv_ref[d, 16:32, :]]
        rb = [recv_ref[d, 32:48, :], recv_ref[d, 48:64, :]]
        return alpha, beta, link, k_first, k_last, ra, rb

    segments = [segment(d) for d in range(count)]
    joints = [1000.0 * (segments[d][4] + segments[d + 1][3]) for d in range(count - 1)]
    zero = jnp.zeros((MY, NZ), f32)
    left, left_src = zero, [zero, zero]
    right, right_src = zero, [zero, zero]
    for step in range(count - 1):
        d = step
        alpha, beta, link, _, _, ra, rb = segments[d]
        new, new_src = through(beta, alpha, link, joints[d], left, rb, ra, left_src)
        left = jnp.where(d < at, new, left)
        left_src = [jnp.where(d < at, n, o) for n, o in zip(new_src, left_src)]
        d = count - 1 - step
        alpha, beta, link, _, _, ra, rb = segments[d]
        new, new_src = through(alpha, beta, link, joints[d - 1], right, ra, rb, right_src)
        right = jnp.where(d > at, new, right)
        right_src = [jnp.where(d > at, n, o) for n, o in zip(new_src, right_src)]
    alpha, beta, link, _, _, ra, rb = segment(at)
    u_first, u_next = two_nodes(
        alpha + left,
        beta + right,
        link,
        [a + s for a, s in zip(ra, left_src)],
        [b + s for b, s in zip(rb, right_src)],
    )

    def keep(x, u):
        for q in range(2):
            heat = heat_ref[pl.ds(x * NY + q, MY, stride=2), :]
            first[x * NY + q * MY : x * NY + (q + 1) * MY, :] = u[q] - 2.0 * heat

    keep(0, u_first)
    keep(NX - 1, u_next)
    for x in range(NX - 2, 0, -1):
        t = x - 1
        gd = gx_ref[t * MY : (t + 1) * MY, :]
        hd = hx_ref[t * MY : (t + 1) * MY, :]
        inv = ix_ref[t * MY : (t + 1) * MY, :]
        b = [rb_ref[t * NY + q * MY : t * NY + (q + 1) * MY, :] for q in range(2)]
        u_next = [(inv * b[q] + hd * u_first[q]) + gd * u_next[q] for q in range(2)]
        keep(x, u_next)

    def side(y):
        start = (y % 2) * MY + y // 2
        return [first[pl.ds(p * NY + start, MX, stride=2 * NY), :] for p in range(2)]

    ra = side(0)
    rb = side(1)
    for t in range(NY - 2):
        gd = gy_ref[t * MX : (t + 1) * MX, :]
        hd = hy_ref[t * MX : (t + 1) * MX, :]
        for p in range(2):
            rby_ref[t * NX + p * MX : t * NX + (p + 1) * MX, :] = rb[p]
        new = side(t + 2)
        ra = [a + b * hd for a, b in zip(ra, rb)]
        rb = [n + b * gd for n, b in zip(new, rb)]
    core = lax.rem(lax.axis_index("gy"), 2)
    joint_low = 1000.0 * (low_ref[NX:, :] + k_ref[pl.ds(0, MX, stride=MY), :])
    joint_high = 1000.0 * (high_ref[NX:, :] + k_ref[pl.ds(MY - 1, MX, stride=MY), :])
    mid_ref[...] = jnp.where(core == 0, joint_high, joint_low)
    outer = jnp.where(core == 0, joint_low, joint_high)
    core_ref[0:8, :] = ra[0]
    core_ref[8:16, :] = ra[1]
    core_ref[16:24, :] = rb[0]
    core_ref[24:32, :] = rb[1]
    core_ref[32:40, :] = pack(my_ref[0:8, :], my_ref[8:16, :])
    core_ref[40:48, :] = pack(my_ref[16:24, :], outer)


def y_segment(rows):
    alpha, beta = unpack(rows(32))
    link, joint = unpack(rows(40))
    return alpha, beta, link, joint, [rows(0), rows(8)], [rows(16), rows(24)]


def chip_kernel(own_ref, other_ref, mid_ref, send_ref):
    core = lax.rem(lax.axis_index("gy"), 2)
    own = y_segment(lambda r: own_ref[r : r + 8, :])
    other = y_segment(lambda r: other_ref[r : r + 8, :])

    def choose(a, b):
        return jnp.where(core == 0, a, b)

    a0, b0, h0, joint, ra0, rb0 = jax.tree.map(choose, own, other)
    a1, b1, h1, _, ra1, rb1 = jax.tree.map(choose, other, own)
    mid = mid_ref[...]
    inv = 1.0 / (h0 + b0 + mid)
    hd, gd = h0 * inv, mid * inv
    alpha = a0 + b0 * hd
    link = h0 * gd
    between = a1 + b0 * gd
    ra = [a + b * hd for a, b in zip(ra0, rb0)]
    rm = [a + b * gd for a, b in zip(ra1, rb0)]
    inv = 1.0 / (link + between + h1)
    hd, gd = link * inv, h1 * inv
    alpha = alpha + between * hd
    beta = b1 + between * gd
    ra = [a + m * hd for a, m in zip(ra, rm)]
    rb = [b + m * gd for b, m in zip(rb1, rm)]
    out = jnp.concatenate([*ra, *rb, pack(alpha, beta), pack(link * gd, joint)], 0)
    for d in range(send_ref.shape[0]):
        send_ref[d] = out


def y_solve_kernel(
    recv_ref, own_ref, other_ref, mid_ref, rb_ref, gy_ref, hy_ref, iy_ref, za_ref, zc_ref, zi_ref, heat_ref,
    out_ref, second,
):
    at_y = lax.axis_index("gy")
    core, chip = lax.rem(at_y, 2), lax.div(at_y, 2)
    count = recv_ref.shape[0]
    segments = [y_segment(lambda r, d=d: recv_ref[d, r : r + 8, :]) for d in range(count)]
    zero = jnp.zeros((MX, NZ), f32)
    left, left_src = zero, [zero, zero]
    right, right_src = zero, [zero, zero]
    for step in range(count - 1):
        d = step
        alpha, beta, link, _, ra, rb = segments[d]
        new, new_src = through(beta, alpha, link, segments[d + 1][3], left, rb, ra, left_src)
        left = jnp.where(d < chip, new, left)
        left_src = [jnp.where(d < chip, n, o) for n, o in zip(new_src, left_src)]
        d = count - 1 - step
        alpha, beta, link, joint, ra, rb = segments[d]
        new, new_src = through(alpha, beta, link, joint, right, ra, rb, right_src)
        right = jnp.where(d > chip, new, right)
        right_src = [jnp.where(d > chip, n, o) for n, o in zip(new_src, right_src)]

    def choose(a, b):
        return jnp.where(core == 0, a, b)

    alpha, beta, link, _, ra, rb = y_segment(lambda r: other_ref[r : r + 8, :])
    near, far = choose(alpha, beta), choose(beta, alpha)
    near_src = [choose(a, b) for a, b in zip(ra, rb)]
    far_src = [choose(b, a) for a, b in zip(ra, rb)]
    leak = choose(right, left)
    src = [choose(r, l) for r, l in zip(right_src, left_src)]
    new, new_src = through(near, far, link, mid_ref[...], leak, near_src, far_src, src)
    left, right = choose(left, new), choose(new, right)
    left_src, right_src = (
        [choose(l, n) for l, n in zip(left_src, new_src)],
        [choose(n, r) for n, r in zip(new_src, right_src)],
    )
    alpha, beta, link, _, ra, rb = y_segment(lambda r: own_ref[r : r + 8, :])
    u_first, u_next = two_nodes(
        alpha + left,
        beta + right,
        link,
        [a + s for a, s in zip(ra, left_src)],
        [b + s for b, s in zip(rb, right_src)],
    )

    def keep(y, u):
        for p in range(2):
            second[y * NX + p * MX : y * NX + (p + 1) * MX, :] = u[p]

    keep(0, u_first)
    keep(NY - 1, u_next)
    for y in range(NY - 2, 0, -1):
        t = y - 1
        gd = gy_ref[t * MX : (t + 1) * MX, :]
        hd = hy_ref[t * MX : (t + 1) * MX, :]
        inv = iy_ref[t * MX : (t + 1) * MX, :]
        b = [rb_ref[t * NX + p * MX : t * NX + (p + 1) * MX, :] for p in range(2)]
        u_next = [(inv * b[p] + hd * u_first[p]) + gd * u_next[p] for p in range(2)]
        keep(y, u_next)

    for n in range(MY):
        cells = [(2 * n + q, p) for q in range(2) for p in range(2)]
        v = [second[y * NX + p * MX : y * NX + (p + 1) * MX, :] for y, p in cells]
        for s in range(7):
            step = 1 << s
            at = s * MX * MY + n * MX
            low, high = za_ref[at : at + MX, :], zc_ref[at : at + MX, :]
            v = [w + (low * pltpu.roll(w, step, 1) + high * pltpu.roll(w, NZ - step, 1)) for w in v]
        inv = zi_ref[n * MX : (n + 1) * MX, :]
        for (y, p), w in zip(cells, v):
            where = pl.ds(p * NY + y, MX, stride=2 * NY)
            out_ref[where, :] = heat_ref[where, :] + inv * w


def call(kernel, ins, outs, scratch=(), smem=(), cost=20000):
    vm = pl.BlockSpec(memory_space=pltpu.VMEM)
    sm = pl.BlockSpec(memory_space=pltpu.SMEM)
    return pl.pallas_call(
        kernel,
        out_shape=tuple(jax.ShapeDtypeStruct(s, f32) for s in outs),
        in_specs=[sm if i in smem else vm for i in range(len(ins))],
        out_specs=tuple(vm for _ in outs),
        scratch_shapes=[pltpu.VMEM(s, f32) for s in scratch],
        cost_estimate=pl.CostEstimate(flops=cost, bytes_accessed=cost, transcendentals=0),
    )(*ins)


def on_device(starting_heat_state, material_zone_ids, zone_diffusivity_lookup):
    heat = starting_heat_state.reshape(NX * NY, NZ)
    ids = material_zone_ids.reshape(MX * MY, NZ // 2)
    nx, ny = lax.axis_size("gx"), lax.axis_size("gy")
    k, low_row, high_row = call(
        prepare_kernel,
        (ids, zone_diffusivity_lookup, heat),
        [(MX * MY, NZ), (NX + MX, NZ), (NX + MX, NZ)],
        scratch=[(MX * MY, NZ)],
        smem=(1,),
    )
    low = lax.ppermute(high_row, "gy", [(i, (i + 1) % ny) for i in range(ny)])
    high = lax.ppermute(low_row, "gy", [((i + 1) % ny, i) for i in range(ny)])
    tx, ty = NX - 2, NY - 2
    gx, hx, ix, px, gy, hy, iy, my, za, zc, zi = call(
        matrix_kernel,
        (k,),
        [(tx * MY, NZ)] * 3
        + [(40, NZ)]
        + [(ty * MX, NZ)] * 3
        + [(24, NZ)]
        + [(7 * MX * MY, NZ)] * 2
        + [(MX * MY, NZ)],
        cost=4000000,
    )
    send, rbx = call(
        right_side_kernel,
        (heat, k, low, high, gx, hx, px),
        [(nx, XROWS, NZ), (tx * NY, NZ)],
    )
    recv = lax.all_to_all(send, "gx", 0, 0)
    own, mid, rby = call(
        x_solve_kernel,
        (recv, heat, k, low, high, rbx, gx, hx, ix, gy, hy, my),
        [(YROWS, NZ), (MX, NZ), (ty * NX, NZ)],
        scratch=[(NX * NY, NZ)],
    )
    other = lax.ppermute(own, "gy", [(i, i ^ 1) for i in range(ny)])
    (send,) = call(chip_kernel, (own, other, mid), [(ny // 2, YROWS, NZ)])
    groups = [list(range(c, ny, 2)) for c in range(2)]
    recv = lax.all_to_all(send, "gy", 0, 0, axis_index_groups=groups)
    (out,) = call(
        y_solve_kernel,
        (recv, own, other, mid, rby, gy, hy, iy, za, zc, zi, heat),
        [(NX * NY, NZ)],
        scratch=[(NX * NY, NZ)],
    )
    return out.reshape(starting_heat_state.shape)


def solution(mesh):
    return jax.shard_map(
        on_device,
        mesh=mesh,
        in_specs=(P("gx", "gy", None), P("gx", "gy", None), P()),
        out_specs=P("gx", "gy", None),
        check_vma=False,
    )
```

```python
import jax
import jax.numpy as jnp
from jax import lax
from jax.experimental import pallas as pl
from jax.experimental.pallas import tpu as pltpu
from jax.sharding import PartitionSpec as P

NX, NY, NZ = 16, 32, 128
MX, MY = NX // 2, NY // 2
XROWS = 104
YROWS = 48
f32 = jnp.float32


def lanes(shape):
    return lax.broadcasted_iota(jnp.int32, shape, 1)


def rows_of(shape):
    return lax.broadcasted_iota(jnp.int32, shape, 0)


def pack(first, second):
    return jnp.where(lanes(first.shape) % 2 == 0, first, second)


def unpack(both):
    even = lanes(both.shape) % 2 == 0
    first = jnp.where(even, both, pltpu.roll(both, 1, 1))
    second = jnp.where(even, pltpu.roll(both, NZ - 1, 1), both)
    return first, second


def through(near, far, link, beyond, leak, near_src, far_src, src):
    total = far + leak
    q = total + link
    cross = total * link
    f = beyond / ((near + beyond) * q + cross)
    new_leak = f * (near * q + cross)
    new_src = [f * (n * q + (e + s) * link) for n, e, s in zip(near_src, far_src, src)]
    return new_leak, new_src


def two_nodes(first, last, link, first_src, last_src):
    inv = 1.0 / (first * last + link * (first + last))
    low = [((last + link) * a + link * b) * inv for a, b in zip(first_src, last_src)]
    high = [((first + link) * b + link * a) * inv for a, b in zip(first_src, last_src)]
    return low, high


def eliminate(conduct, put):
    alpha = jnp.ones_like(conduct[0])
    beta = jnp.ones_like(conduct[0])
    link = conduct[0]
    for t in range(1, len(conduct)):
        g = conduct[t]
        inv = 1.0 / (link + beta + g)
        hd = link * inv
        gd = g * inv
        put(t - 1, gd, hd, inv)
        alpha = alpha + beta * hd
        link = link * gd
        beta = 1.0 + beta * gd
    return alpha, beta, link


def prepare_kernel(ids_ref, table_ref, heat_ref, k_ref, low_ref, high_ref, wide):
    ids = ids_ref[...]
    k = jnp.zeros(ids.shape, f32)
    for region in range(table_ref.shape[0]):
        k = jnp.where(ids == region, table_ref[region], k)
    wide[...] = jnp.zeros(wide.shape, f32)
    wide[:, : NZ // 2] = k
    index = lanes(wide.shape) // 2
    k_ref[...] = jnp.take_along_axis(wide[...], index, axis=1, mode="promise_in_bounds")
    low_ref[:NX] = heat_ref[pl.ds(0, NX, stride=NY), :]
    high_ref[:NX] = heat_ref[pl.ds(NY - 1, NX, stride=NY), :]
    low_ref[NX:] = k_ref[pl.ds(0, MX, stride=MY), :]
    high_ref[NX:] = k_ref[pl.ds(MY - 1, MX, stride=MY), :]


def matrix_kernel(
    k_ref, gx_ref, hx_ref, ix_ref, px_ref, gy_ref, hy_ref, iy_ref, my_ref, za_ref, zc_ref, zi_ref
):
    at_x, at_y = lax.axis_index("gx"), lax.axis_index("gy")
    last_x, last_y = lax.axis_size("gx") - 1, lax.axis_size("gy") - 1

    def chain(k):
        joints = []
        for m in range(len(k)):
            joints.append(2000.0 * k[m])
            if m + 1 < len(k):
                joints.append(1000.0 * (k[m] + k[m + 1]))
        return joints

    kx = [k_ref[m * MY : (m + 1) * MY, :] for m in range(MX)]

    def put_x(t, gd, hd, inv):
        gx_ref[t * MY : (t + 1) * MY, :] = gd
        hx_ref[t * MY : (t + 1) * MY, :] = hd
        ix_ref[t * MY : (t + 1) * MY, :] = inv

    alpha, beta, link = eliminate(chain(kx), put_x)
    alpha = alpha + jnp.where(at_x == 0, 1000.0, 0.0) * kx[0]
    beta = beta + jnp.where(at_x == last_x, 1000.0, 0.0) * kx[-1]
    px_ref[0:16, :] = pack(alpha, beta)
    px_ref[16:32, :] = pack(link, kx[0])
    px_ref[32:40, :] = pack(kx[-1][:8], kx[-1][8:])

    ky = [k_ref[pl.ds(n, MX, stride=MY), :] for n in range(MY)]

    def put_y(t, gd, hd, inv):
        gy_ref[t * MX : (t + 1) * MX, :] = gd
        hy_ref[t * MX : (t + 1) * MX, :] = hd
        iy_ref[t * MX : (t + 1) * MX, :] = inv

    alpha, beta, link = eliminate(chain(ky), put_y)
    my_ref[0:8, :] = alpha + jnp.where(at_y == 0, 1000.0, 0.0) * ky[0]
    my_ref[8:16, :] = beta + jnp.where(at_y == last_y, 1000.0, 0.0) * ky[-1]
    my_ref[16:24, :] = link

    group = 4
    for start in range(0, MY, group):
        k = jnp.concatenate(ky[start : start + group], 0)
        lane = lanes(k.shape)
        west = 0.25 * (k + jnp.where(lane == 0, 0.0, pltpu.roll(k, 1, 1)))
        east = 0.25 * (k + jnp.where(lane == NZ - 1, 0.0, pltpu.roll(k, NZ - 1, 1)))
        diag = 1.0 + (west + east)
        a = jnp.where(lane == 0, 0.0, west)
        c = jnp.where(lane == NZ - 1, 0.0, east)
        size = MX * group
        for s in range(7):
            step = 1 << s
            inv = 1.0 / diag
            low = a * pltpu.roll(inv, step, 1)
            high = c * pltpu.roll(inv, NZ - step, 1)
            at = s * MX * MY + start * MX
            za_ref[at : at + size, :] = low
            zc_ref[at : at + size, :] = high
            diag = diag - (low * pltpu.roll(c, step, 1) + high * pltpu.roll(a, NZ - step, 1))
            a = low * pltpu.roll(a, step, 1)
            c = high * pltpu.roll(c, NZ - step, 1)
        zi_ref[start * MX : start * MX + size, :] = 1.0 / diag


def right_side_kernel(heat_ref, k_ref, low_ref, high_ref, gx_ref, hx_ref, px_ref, send_ref, rb_ref):
    at_y = lax.axis_index("gy")
    inside_low = jnp.where(at_y == 0, 0.0, 1.0)
    inside_high = jnp.where(at_y == lax.axis_size("gy") - 1, 0.0, 1.0)
    shape = (MY, NZ)
    lane, row = lanes(shape), rows_of(shape)
    ra = None
    rb = None
    for m in range(MX):
        k = k_ref[m * MY : (m + 1) * MY, :]
        k_low = inside_low * low_ref[NX + m : NX + m + 1, :]
        k_high = inside_high * high_ref[NX + m : NX + m + 1, :]
        face_low = 2000.0 * (k + jnp.where(row == 0, k_low, pltpu.roll(k, 1, 0)))
        face_high = 2000.0 * (k + jnp.where(row == MY - 1, k_high, pltpu.roll(k, MY - 1, 0)))
        face_mid = 4000.0 * k
        west = 0.5 * (k + jnp.where(lane == 0, 0.0, pltpu.roll(k, 1, 1)))
        east = 0.5 * (k + jnp.where(lane == NZ - 1, 0.0, pltpu.roll(k, NZ - 1, 1)))
        middle = 2.0 - (west + east)
        west = jnp.where(lane == 0, 0.0, west)
        east = jnp.where(lane == NZ - 1, 0.0, east)
        for x in (2 * m, 2 * m + 1):
            even = heat_ref[pl.ds(x * NY, MY, stride=2), :]
            odd = heat_ref[pl.ds(x * NY + 1, MY, stride=2), :]
            before = jnp.where(row == 0, inside_low * low_ref[x : x + 1, :], pltpu.roll(odd, 1, 0))
            after = jnp.where(
                row == MY - 1, inside_high * high_ref[x : x + 1, :], pltpu.roll(even, MY - 1, 0)
            )
            flow = face_mid * (odd - even)
            r = []
            for v, along_y in (
                (even, flow - face_low * (even - before)),
                (odd, face_high * (after - odd) - flow),
            ):
                along_z = west * pltpu.roll(v, 1, 1) + east * pltpu.roll(v, NZ - 1, 1)
                r.append(along_y + (along_z + middle * v))
            if x == 0:
                ra = r
            elif x == 1:
                rb = r
            else:
                t = x - 2
                gd = gx_ref[t * MY : (t + 1) * MY, :]
                hd = hx_ref[t * MY : (t + 1) * MY, :]
                for q in range(2):
                    rb_ref[t * NY + q * MY : t * NY + (q + 1) * MY, :] = rb[q]
                ra = [a + b * hd for a, b in zip(ra, rb)]
                rb = [n + b * gd for n, b in zip(r, rb)]
    p = px_ref[...]
    for d in range(send_ref.shape[0]):
        send_ref[d, 0:16, :] = ra[0]
        send_ref[d, 16:32, :] = ra[1]
        send_ref[d, 32:48, :] = rb[0]
        send_ref[d, 48:64, :] = rb[1]
        send_ref[d, 64:104, :] = p


def x_solve_kernel(
    recv_ref, heat_ref, k_ref, low_ref, high_ref, rb_ref, gx_ref, hx_ref, ix_ref, gy_ref, hy_ref, my_ref,
    core_ref, mid_ref, rby_ref, first,
):
    at = lax.axis_index("gx")
    count = recv_ref.shape[0]

    def segment(d):
        alpha, beta = unpack(recv_ref[d, 64:80, :])
        link, k_first = unpack(recv_ref[d, 80:96, :])
        k_last = jnp.concatenate(unpack(recv_ref[d, 96:104, :]), 0)
        ra = [recv_ref[d, 0:16, :], recv_ref[d, 16:32, :]]
        rb = [recv_ref[d, 32:48, :], recv_ref[d, 48:64, :]]
        return alpha, beta, link, k_first, k_last, ra, rb

    segments = [segment(d) for d in range(count)]
    joints = [1000.0 * (segments[d][4] + segments[d + 1][3]) for d in range(count - 1)]
    zero = jnp.zeros((MY, NZ), f32)
    left, left_src = zero, [zero, zero]
    right, right_src = zero, [zero, zero]
    for step in range(count - 1):
        d = step
        alpha, beta, link, _, _, ra, rb = segments[d]
        new, new_src = through(beta, alpha, link, joints[d], left, rb, ra, left_src)
        left = jnp.where(d < at, new, left)
        left_src = [jnp.where(d < at, n, o) for n, o in zip(new_src, left_src)]
        d = count - 1 - step
        alpha, beta, link, _, _, ra, rb = segments[d]
        new, new_src = through(alpha, beta, link, joints[d - 1], right, ra, rb, right_src)
        right = jnp.where(d > at, new, right)
        right_src = [jnp.where(d > at, n, o) for n, o in zip(new_src, right_src)]
    alpha, beta, link, _, _, ra, rb = segment(at)
    u_first, u_next = two_nodes(
        alpha + left,
        beta + right,
        link,
        [a + s for a, s in zip(ra, left_src)],
        [b + s for b, s in zip(rb, right_src)],
    )

    def keep(x, u):
        for q in range(2):
            heat = heat_ref[pl.ds(x * NY + q, MY, stride=2), :]
            first[x * NY + q * MY : x * NY + (q + 1) * MY, :] = u[q] - 2.0 * heat

    keep(0, u_first)
    keep(NX - 1, u_next)
    for x in range(NX - 2, 0, -1):
        t = x - 1
        gd = gx_ref[t * MY : (t + 1) * MY, :]
        hd = hx_ref[t * MY : (t + 1) * MY, :]
        inv = ix_ref[t * MY : (t + 1) * MY, :]
        b = [rb_ref[t * NY + q * MY : t * NY + (q + 1) * MY, :] for q in range(2)]
        u_next = [(inv * b[q] + hd * u_first[q]) + gd * u_next[q] for q in range(2)]
        keep(x, u_next)

    def side(y):
        start = (y % 2) * MY + y // 2
        return [first[pl.ds(p * NY + start, MX, stride=2 * NY), :] for p in range(2)]

    ra = side(0)
    rb = side(1)
    for t in range(NY - 2):
        gd = gy_ref[t * MX : (t + 1) * MX, :]
        hd = hy_ref[t * MX : (t + 1) * MX, :]
        for p in range(2):
            rby_ref[t * NX + p * MX : t * NX + (p + 1) * MX, :] = rb[p]
        new = side(t + 2)
        ra = [a + b * hd for a, b in zip(ra, rb)]
        rb = [n + b * gd for n, b in zip(new, rb)]
    core = lax.rem(lax.axis_index("gy"), 2)
    joint_low = 1000.0 * (low_ref[NX:, :] + k_ref[pl.ds(0, MX, stride=MY), :])
    joint_high = 1000.0 * (high_ref[NX:, :] + k_ref[pl.ds(MY - 1, MX, stride=MY), :])
    mid_ref[...] = jnp.where(core == 0, joint_high, joint_low)
    outer = jnp.where(core == 0, joint_low, joint_high)
    core_ref[0:8, :] = ra[0]
    core_ref[8:16, :] = ra[1]
    core_ref[16:24, :] = rb[0]
    core_ref[24:32, :] = rb[1]
    core_ref[32:40, :] = pack(my_ref[0:8, :], my_ref[8:16, :])
    core_ref[40:48, :] = pack(my_ref[16:24, :], outer)


def y_segment(rows):
    alpha, beta = unpack(rows(32))
    link, joint = unpack(rows(40))
    return alpha, beta, link, joint, [rows(0), rows(8)], [rows(16), rows(24)]


def chip_kernel(own_ref, other_ref, mid_ref, send_ref):
    core = lax.rem(lax.axis_index("gy"), 2)
    own = y_segment(lambda r: own_ref[r : r + 8, :])
    other = y_segment(lambda r: other_ref[r : r + 8, :])

    def choose(a, b):
        return jnp.where(core == 0, a, b)

    a0, b0, h0, joint, ra0, rb0 = jax.tree.map(choose, own, other)
    a1, b1, h1, _, ra1, rb1 = jax.tree.map(choose, other, own)
    mid = mid_ref[...]
    inv = 1.0 / (h0 + b0 + mid)
    hd, gd = h0 * inv, mid * inv
    alpha = a0 + b0 * hd
    link = h0 * gd
    between = a1 + b0 * gd
    ra = [a + b * hd for a, b in zip(ra0, rb0)]
    rm = [a + b * gd for a, b in zip(ra1, rb0)]
    inv = 1.0 / (link + between + h1)
    hd, gd = link * inv, h1 * inv
    alpha = alpha + between * hd
    beta = b1 + between * gd
    ra = [a + m * hd for a, m in zip(ra, rm)]
    rb = [b + m * gd for b, m in zip(rb1, rm)]
    out = jnp.concatenate([*ra, *rb, pack(alpha, beta), pack(link * gd, joint)], 0)
    for d in range(send_ref.shape[0]):
        send_ref[d] = out


def y_solve_kernel(
    recv_ref, own_ref, other_ref, mid_ref, rb_ref, gy_ref, hy_ref, iy_ref, za_ref, zc_ref, zi_ref, heat_ref,
    out_ref, second,
):
    at_y = lax.axis_index("gy")
    core, chip = lax.rem(at_y, 2), lax.div(at_y, 2)
    count = recv_ref.shape[0]
    segments = [y_segment(lambda r, d=d: recv_ref[d, r : r + 8, :]) for d in range(count)]
    zero = jnp.zeros((MX, NZ), f32)
    left, left_src = zero, [zero, zero]
    right, right_src = zero, [zero, zero]
    for step in range(count - 1):
        d = step
        alpha, beta, link, _, ra, rb = segments[d]
        new, new_src = through(beta, alpha, link, segments[d + 1][3], left, rb, ra, left_src)
        left = jnp.where(d < chip, new, left)
        left_src = [jnp.where(d < chip, n, o) for n, o in zip(new_src, left_src)]
        d = count - 1 - step
        alpha, beta, link, joint, ra, rb = segments[d]
        new, new_src = through(alpha, beta, link, joint, right, ra, rb, right_src)
        right = jnp.where(d > chip, new, right)
        right_src = [jnp.where(d > chip, n, o) for n, o in zip(new_src, right_src)]

    def choose(a, b):
        return jnp.where(core == 0, a, b)

    alpha, beta, link, _, ra, rb = y_segment(lambda r: other_ref[r : r + 8, :])
    near, far = choose(alpha, beta), choose(beta, alpha)
    near_src = [choose(a, b) for a, b in zip(ra, rb)]
    far_src = [choose(b, a) for a, b in zip(ra, rb)]
    leak = choose(right, left)
    src = [choose(r, l) for r, l in zip(right_src, left_src)]
    new, new_src = through(near, far, link, mid_ref[...], leak, near_src, far_src, src)
    left, right = choose(left, new), choose(new, right)
    left_src, right_src = (
        [choose(l, n) for l, n in zip(left_src, new_src)],
        [choose(n, r) for n, r in zip(new_src, right_src)],
    )
    alpha, beta, link, _, ra, rb = y_segment(lambda r: own_ref[r : r + 8, :])
    u_first, u_next = two_nodes(
        alpha + left,
        beta + right,
        link,
        [a + s for a, s in zip(ra, left_src)],
        [b + s for b, s in zip(rb, right_src)],
    )

    def keep(y, u):
        for p in range(2):
            second[y * NX + p * MX : y * NX + (p + 1) * MX, :] = u[p]

    keep(0, u_first)
    keep(NY - 1, u_next)
    for y in range(NY - 2, 0, -1):
        t = y - 1
        gd = gy_ref[t * MX : (t + 1) * MX, :]
        hd = hy_ref[t * MX : (t + 1) * MX, :]
        inv = iy_ref[t * MX : (t + 1) * MX, :]
        b = [rb_ref[t * NX + p * MX : t * NX + (p + 1) * MX, :] for p in range(2)]
        u_next = [(inv * b[p] + hd * u_first[p]) + gd * u_next[p] for p in range(2)]
        keep(y, u_next)

    for n in range(MY):
        cells = [(2 * n + q, p) for q in range(2) for p in range(2)]
        v = [second[y * NX + p * MX : y * NX + (p + 1) * MX, :] for y, p in cells]
        for s in range(7):
            step = 1 << s
            at = s * MX * MY + n * MX
            low, high = za_ref[at : at + MX, :], zc_ref[at : at + MX, :]
            v = [w + (low * pltpu.roll(w, step, 1) + high * pltpu.roll(w, NZ - step, 1)) for w in v]
        inv = zi_ref[n * MX : (n + 1) * MX, :]
        for (y, p), w in zip(cells, v):
            where = pl.ds(p * NY + y, MX, stride=2 * NY)
            out_ref[where, :] = heat_ref[where, :] + inv * w


def call(kernel, ins, outs, scratch=(), smem=(), cost=20000):
    vm = pl.BlockSpec(memory_space=pltpu.VMEM)
    sm = pl.BlockSpec(memory_space=pltpu.SMEM)
    return pl.pallas_call(
        kernel,
        out_shape=tuple(jax.ShapeDtypeStruct(s, f32) for s in outs),
        in_specs=[sm if i in smem else vm for i in range(len(ins))],
        out_specs=tuple(vm for _ in outs),
        scratch_shapes=[pltpu.VMEM(s, f32) for s in scratch],
        compiler_params=pltpu.CompilerParams(vmem_limit_bytes=8 << 20),
        cost_estimate=pl.CostEstimate(flops=cost, bytes_accessed=cost, transcendentals=0),
    )(*ins)


def on_device(starting_heat_state, material_zone_ids, zone_diffusivity_lookup):
    heat = starting_heat_state.reshape(NX * NY, NZ)
    ids = material_zone_ids.reshape(MX * MY, NZ // 2)
    nx, ny = lax.axis_size("gx"), lax.axis_size("gy")
    k, low_row, high_row = call(
        prepare_kernel,
        (ids, zone_diffusivity_lookup, heat),
        [(MX * MY, NZ), (NX + MX, NZ), (NX + MX, NZ)],
        scratch=[(MX * MY, NZ)],
        smem=(1,),
    )
    low = lax.ppermute(high_row, "gy", [(i, (i + 1) % ny) for i in range(ny)])
    high = lax.ppermute(low_row, "gy", [((i + 1) % ny, i) for i in range(ny)])
    tx, ty = NX - 2, NY - 2
    gx, hx, ix, px, gy, hy, iy, my, za, zc, zi = call(
        matrix_kernel,
        (k,),
        [(tx * MY, NZ)] * 3
        + [(40, NZ)]
        + [(ty * MX, NZ)] * 3
        + [(24, NZ)]
        + [(7 * MX * MY, NZ)] * 2
        + [(MX * MY, NZ)],
        cost=4000000,
    )
    send, rbx = call(
        right_side_kernel,
        (heat, k, low, high, gx, hx, px),
        [(nx, XROWS, NZ), (tx * NY, NZ)],
    )
    recv = lax.all_to_all(send, "gx", 0, 0)
    own, mid, rby = call(
        x_solve_kernel,
        (recv, heat, k, low, high, rbx, gx, hx, ix, gy, hy, my),
        [(YROWS, NZ), (MX, NZ), (ty * NX, NZ)],
        scratch=[(NX * NY, NZ)],
    )
    other = lax.ppermute(own, "gy", [(i, i ^ 1) for i in range(ny)])
    (send,) = call(chip_kernel, (own, other, mid), [(ny // 2, YROWS, NZ)])
    groups = [list(range(c, ny, 2)) for c in range(2)]
    recv = lax.all_to_all(send, "gy", 0, 0, axis_index_groups=groups)
    (out,) = call(
        y_solve_kernel,
        (recv, own, other, mid, rby, gy, hy, iy, za, zc, zi, heat),
        [(NX * NY, NZ)],
        scratch=[(NX * NY, NZ)],
    )
    return out.reshape(starting_heat_state.shape)


def solution(mesh):
    return jax.shard_map(
        on_device,
        mesh=mesh,
        in_specs=(P("gx", "gy", None), P("gx", "gy", None), P()),
        out_specs=P("gx", "gy", None),
        check_vma=False,
    )
```

```python
import jax
import jax.numpy as jnp
from jax import lax
from jax.experimental import pallas as pl
from jax.experimental.pallas import tpu as pltpu
from jax.sharding import PartitionSpec as P

NX, NY, NZ = 16, 32, 128
MX, MY = NX // 2, NY // 2
XROWS = 104
YROWS = 48
f32 = jnp.float32


def lanes(shape):
    return lax.broadcasted_iota(jnp.int32, shape, 1)


def rows_of(shape):
    return lax.broadcasted_iota(jnp.int32, shape, 0)


def pack(first, second):
    return jnp.where(lanes(first.shape) % 2 == 0, first, second)


def unpack(both):
    even = lanes(both.shape) % 2 == 0
    first = jnp.where(even, both, pltpu.roll(both, 1, 1))
    second = jnp.where(even, pltpu.roll(both, NZ - 1, 1), both)
    return first, second


def through(near, far, link, beyond, leak, near_src, far_src, src):
    total = far + leak
    q = total + link
    cross = total * link
    f = beyond / ((near + beyond) * q + cross)
    new_leak = f * (near * q + cross)
    new_src = [f * (n * q + (e + s) * link) for n, e, s in zip(near_src, far_src, src)]
    return new_leak, new_src


def two_nodes(first, last, link, first_src, last_src):
    inv = 1.0 / (first * last + link * (first + last))
    low = [((last + link) * a + link * b) * inv for a, b in zip(first_src, last_src)]
    high = [((first + link) * b + link * a) * inv for a, b in zip(first_src, last_src)]
    return low, high


def eliminate(conduct, put):
    alpha = jnp.ones_like(conduct[0])
    beta = jnp.ones_like(conduct[0])
    link = conduct[0]
    for t in range(1, len(conduct)):
        g = conduct[t]
        inv = 1.0 / (link + beta + g)
        hd = link * inv
        gd = g * inv
        put(t - 1, gd, hd, inv)
        alpha = alpha + beta * hd
        link = link * gd
        beta = 1.0 + beta * gd
    return alpha, beta, link


def prepare_kernel(
    ids_hbm, table_hbm, heat_hbm, k_ref, inner_ref, outer_ref, heat_ref, ids_ref, table_ref, wide, sems
):
    copies = [
        pltpu.make_async_copy(table_hbm, table_ref, sems.at[0]),
        pltpu.make_async_copy(ids_hbm, ids_ref, sems.at[1]),
        pltpu.make_async_copy(heat_hbm, heat_ref, sems.at[2]),
    ]
    for copy in copies:
        copy.start()
    wide[...] = jnp.zeros(wide.shape, f32)
    copies[0].wait()
    copies[1].wait()
    ids = ids_ref[...]
    k = jnp.zeros(ids.shape, f32)
    for region in range(table_ref.shape[0]):
        k = jnp.where(ids == region, table_ref[region], k)
    wide[:, : NZ // 2] = k
    index = lanes(wide.shape) // 2
    k_ref[...] = jnp.take_along_axis(wide[...], index, axis=1, mode="promise_in_bounds")
    copies[2].wait()
    low = [heat_ref[pl.ds(0, NX, stride=NY), :], k_ref[pl.ds(0, MX, stride=MY), :]]
    high = [heat_ref[pl.ds(NY - 1, NX, stride=NY), :], k_ref[pl.ds(MY - 1, MX, stride=MY), :]]
    core = lax.rem(lax.axis_index("gy"), 2)
    low, high = jnp.concatenate(low, 0), jnp.concatenate(high, 0)
    inner_ref[...] = jnp.where(core == 0, high, low)
    outer_ref[...] = jnp.where(core == 0, low, high)


def matrix_kernel(
    k_ref, gx_ref, hx_ref, ix_ref, px_ref, gy_ref, hy_ref, iy_ref, my_ref, za_ref, zc_ref, zi_ref
):
    at_x, at_y = lax.axis_index("gx"), lax.axis_index("gy")
    last_x, last_y = lax.axis_size("gx") - 1, lax.axis_size("gy") - 1

    def chain(k):
        joints = []
        for m in range(len(k)):
            joints.append(2000.0 * k[m])
            if m + 1 < len(k):
                joints.append(1000.0 * (k[m] + k[m + 1]))
        return joints

    kx = [k_ref[m * MY : (m + 1) * MY, :] for m in range(MX)]

    def put_x(t, gd, hd, inv):
        gx_ref[t * MY : (t + 1) * MY, :] = gd
        hx_ref[t * MY : (t + 1) * MY, :] = hd
        ix_ref[t * MY : (t + 1) * MY, :] = inv

    alpha, beta, link = eliminate(chain(kx), put_x)
    alpha = alpha + jnp.where(at_x == 0, 1000.0, 0.0) * kx[0]
    beta = beta + jnp.where(at_x == last_x, 1000.0, 0.0) * kx[-1]
    px_ref[0:16, :] = pack(alpha, beta)
    px_ref[16:32, :] = pack(link, kx[0])
    px_ref[32:40, :] = pack(kx[-1][:8], kx[-1][8:])

    ky = [k_ref[pl.ds(n, MX, stride=MY), :] for n in range(MY)]

    def put_y(t, gd, hd, inv):
        gy_ref[t * MX : (t + 1) * MX, :] = gd
        hy_ref[t * MX : (t + 1) * MX, :] = hd
        iy_ref[t * MX : (t + 1) * MX, :] = inv

    alpha, beta, link = eliminate(chain(ky), put_y)
    my_ref[0:8, :] = alpha + jnp.where(at_y == 0, 1000.0, 0.0) * ky[0]
    my_ref[8:16, :] = beta + jnp.where(at_y == last_y, 1000.0, 0.0) * ky[-1]
    my_ref[16:24, :] = link

    group = 4
    for start in range(0, MY, group):
        k = jnp.concatenate(ky[start : start + group], 0)
        lane = lanes(k.shape)
        west = 0.25 * (k + jnp.where(lane == 0, 0.0, pltpu.roll(k, 1, 1)))
        east = 0.25 * (k + jnp.where(lane == NZ - 1, 0.0, pltpu.roll(k, NZ - 1, 1)))
        diag = 1.0 + (west + east)
        a = jnp.where(lane == 0, 0.0, west)
        c = jnp.where(lane == NZ - 1, 0.0, east)
        size = MX * group
        for s in range(7):
            step = 1 << s
            inv = 1.0 / diag
            low = a * pltpu.roll(inv, step, 1)
            high = c * pltpu.roll(inv, NZ - step, 1)
            at = s * MX * MY + start * MX
            za_ref[at : at + size, :] = low
            zc_ref[at : at + size, :] = high
            diag = diag - (low * pltpu.roll(c, step, 1) + high * pltpu.roll(a, NZ - step, 1))
            a = low * pltpu.roll(a, step, 1)
            c = high * pltpu.roll(c, NZ - step, 1)
        zi_ref[start * MX : start * MX + size, :] = 1.0 / diag


def right_side_kernel(heat_ref, k_ref, inner_ref, outer_ref, gx_ref, hx_ref, px_ref, send_ref, rb_ref):
    at_y = lax.axis_index("gy")
    core = lax.rem(at_y, 2)
    inner, outer = inner_ref[...], outer_ref[...]
    low = jnp.where(at_y == 0, 0.0, jnp.where(core == 0, outer, inner))
    high = jnp.where(at_y == lax.axis_size("gy") - 1, 0.0, jnp.where(core == 0, inner, outer))
    shape = (MY, NZ)
    lane, row = lanes(shape), rows_of(shape)
    ra = None
    rb = None
    for m in range(MX):
        k = k_ref[m * MY : (m + 1) * MY, :]
        k_low = low[NX + m : NX + m + 1]
        k_high = high[NX + m : NX + m + 1]
        face_low = 2000.0 * (k + jnp.where(row == 0, k_low, pltpu.roll(k, 1, 0)))
        face_high = 2000.0 * (k + jnp.where(row == MY - 1, k_high, pltpu.roll(k, MY - 1, 0)))
        face_mid = 4000.0 * k
        west = 0.5 * (k + jnp.where(lane == 0, 0.0, pltpu.roll(k, 1, 1)))
        east = 0.5 * (k + jnp.where(lane == NZ - 1, 0.0, pltpu.roll(k, NZ - 1, 1)))
        middle = 2.0 - (west + east)
        west = jnp.where(lane == 0, 0.0, west)
        east = jnp.where(lane == NZ - 1, 0.0, east)
        for x in (2 * m, 2 * m + 1):
            even = heat_ref[pl.ds(x * NY, MY, stride=2), :]
            odd = heat_ref[pl.ds(x * NY + 1, MY, stride=2), :]
            before = jnp.where(row == 0, low[x : x + 1], pltpu.roll(odd, 1, 0))
            after = jnp.where(row == MY - 1, high[x : x + 1], pltpu.roll(even, MY - 1, 0))
            flow = face_mid * (odd - even)
            r = []
            for v, along_y in (
                (even, flow - face_low * (even - before)),
                (odd, face_high * (after - odd) - flow),
            ):
                along_z = west * pltpu.roll(v, 1, 1) + east * pltpu.roll(v, NZ - 1, 1)
                r.append(along_y + (along_z + middle * v))
            if x == 0:
                ra = r
            elif x == 1:
                rb = r
            else:
                t = x - 2
                gd = gx_ref[t * MY : (t + 1) * MY, :]
                hd = hx_ref[t * MY : (t + 1) * MY, :]
                for q in range(2):
                    rb_ref[t * NY + q * MY : t * NY + (q + 1) * MY, :] = rb[q]
                ra = [a + b * hd for a, b in zip(ra, rb)]
                rb = [n + b * gd for n, b in zip(r, rb)]
    send_ref[0:16, :] = ra[0]
    send_ref[16:32, :] = ra[1]
    send_ref[32:48, :] = rb[0]
    send_ref[48:64, :] = rb[1]
    send_ref[64:104, :] = px_ref[...]


def x_segment(rows):
    alpha, beta = unpack(rows[64:80])
    link, k_first = unpack(rows[80:96])
    k_last = jnp.concatenate(unpack(rows[96:104]), 0)
    return alpha, beta, link, k_first, k_last, [rows[0:16], rows[16:32]], [rows[32:48], rows[48:64]]


def x_quarter(place, refs):
    held = [r[...] for r in refs]
    segments = []
    for d in range(4):
        rows = held[0]
        for j in range(1, 4):
            rows = jnp.where(place == d ^ j, held[j], rows)
        segments.append(x_segment(rows))
    return segments


def x_half_kernel(own_ref, one_ref, two_ref, three_ref, send_ref):
    at = lax.axis_index("gx")
    upper = at >= 4
    place = lax.rem(at, 4)
    place = jnp.where(upper, 3 - place, place)

    def turn(segment):
        alpha, beta, link, k_first, k_last, ra, rb = segment

        def pick(a, b):
            return jnp.where(upper, a, b)

        near, far = pick(alpha, beta), pick(beta, alpha)
        k_near, k_far = pick(k_first, k_last), pick(k_last, k_first)
        near_src = [pick(a, b) for a, b in zip(ra, rb)]
        far_src = [pick(b, a) for a, b in zip(ra, rb)]
        return near, far, link, k_near, k_far, near_src, far_src

    segments = [turn(g) for g in x_quarter(place, (own_ref, one_ref, two_ref, three_ref))]
    zero = jnp.zeros((MY, NZ), f32)
    leak, src = zero, [zero, zero]
    for d in range(3):
        near, far, link, k_near, _, near_src, far_src = segments[d]
        joint = 1000.0 * (k_near + segments[d + 1][4])
        leak, src = through(near, far, link, joint, leak, near_src, far_src, src)
    near, far, link, k_near, _, near_src, far_src = segments[3]
    total = far + leak
    part = link / (total + link)
    send_ref[0:16, :] = near_src[0] + (far_src[0] + src[0]) * part
    send_ref[16:32, :] = near_src[1] + (far_src[1] + src[1]) * part
    send_ref[32:48, :] = pack(near + total * part, k_near)


def x_solve_kernel(
    own_ref, one_ref, two_ref, three_ref, half_ref, heat_ref, k_ref, inner_ref, outer_ref, rb_ref, gx_ref,
    hx_ref, ix_ref, gy_ref, hy_ref, my_ref, core_ref, mid_ref, rby_ref, first,
):
    at = lax.axis_index("gx")
    place = lax.rem(at, 4)
    segments = x_quarter(place, (own_ref, one_ref, two_ref, three_ref))
    half_leak, half_k = unpack(half_ref[32:48, :])
    upper = at >= 4
    joint = 1000.0 * (half_k + jnp.where(upper, segments[0][3], segments[3][4]))
    part = joint / (half_leak + joint)
    half_leak = half_leak * part
    half_src = [half_ref[0:16, :] * part, half_ref[16:32, :] * part]
    left = jnp.where(upper, half_leak, 0.0)
    left_src = [jnp.where(upper, v, 0.0) for v in half_src]
    right = jnp.where(upper, 0.0, half_leak)
    right_src = [jnp.where(upper, 0.0, v) for v in half_src]
    joints = [1000.0 * (segments[d][4] + segments[d + 1][3]) for d in range(3)]
    for step in range(3):
        d = step
        alpha, beta, link, _, _, ra, rb = segments[d]
        new, new_src = through(beta, alpha, link, joints[d], left, rb, ra, left_src)
        left = jnp.where(d < place, new, left)
        left_src = [jnp.where(d < place, n, o) for n, o in zip(new_src, left_src)]
        d = 3 - step
        alpha, beta, link, _, _, ra, rb = segments[d]
        new, new_src = through(alpha, beta, link, joints[d - 1], right, ra, rb, right_src)
        right = jnp.where(d > place, new, right)
        right_src = [jnp.where(d > place, n, o) for n, o in zip(new_src, right_src)]
    alpha, beta, link, _, _, ra, rb = x_segment(own_ref[...])
    u_first, u_next = two_nodes(
        alpha + left,
        beta + right,
        link,
        [a + s for a, s in zip(ra, left_src)],
        [b + s for b, s in zip(rb, right_src)],
    )

    def keep(x, u):
        for q in range(2):
            heat = heat_ref[pl.ds(x * NY + q, MY, stride=2), :]
            first[x * NY + q * MY : x * NY + (q + 1) * MY, :] = u[q] - 2.0 * heat

    keep(0, u_first)
    keep(NX - 1, u_next)
    for x in range(NX - 2, 0, -1):
        t = x - 1
        gd = gx_ref[t * MY : (t + 1) * MY, :]
        hd = hx_ref[t * MY : (t + 1) * MY, :]
        inv = ix_ref[t * MY : (t + 1) * MY, :]
        b = [rb_ref[t * NY + q * MY : t * NY + (q + 1) * MY, :] for q in range(2)]
        u_next = [(inv * b[q] + hd * u_first[q]) + gd * u_next[q] for q in range(2)]
        keep(x, u_next)

    def side(y):
        start = (y % 2) * MY + y // 2
        return [first[pl.ds(p * NY + start, MX, stride=2 * NY), :] for p in range(2)]

    ra = side(0)
    rb = side(1)
    for t in range(NY - 2):
        gd = gy_ref[t * MX : (t + 1) * MX, :]
        hd = hy_ref[t * MX : (t + 1) * MX, :]
        for p in range(2):
            rby_ref[t * NX + p * MX : t * NX + (p + 1) * MX, :] = rb[p]
        new = side(t + 2)
        ra = [a + b * hd for a, b in zip(ra, rb)]
        rb = [n + b * gd for n, b in zip(new, rb)]
    core = lax.rem(lax.axis_index("gy"), 2)
    k_low = k_ref[pl.ds(0, MX, stride=MY), :]
    k_high = k_ref[pl.ds(MY - 1, MX, stride=MY), :]
    mid_ref[...] = 1000.0 * (inner_ref[NX:, :] + jnp.where(core == 0, k_high, k_low))
    outer = 1000.0 * (outer_ref[NX:, :] + jnp.where(core == 0, k_low, k_high))
    core_ref[0:8, :] = ra[0]
    core_ref[8:16, :] = ra[1]
    core_ref[16:24, :] = rb[0]
    core_ref[24:32, :] = rb[1]
    core_ref[32:40, :] = pack(my_ref[0:8, :], my_ref[8:16, :])
    core_ref[40:48, :] = pack(my_ref[16:24, :], outer)


def y_segment(rows):
    alpha, beta = unpack(rows(32))
    link, joint = unpack(rows(40))
    return alpha, beta, link, joint, [rows(0), rows(8)], [rows(16), rows(24)]


def chip_kernel(own_ref, other_ref, mid_ref, send_ref):
    core = lax.rem(lax.axis_index("gy"), 2)
    own = y_segment(lambda r: own_ref[r : r + 8, :])
    other = y_segment(lambda r: other_ref[r : r + 8, :])

    def choose(a, b):
        return jnp.where(core == 0, a, b)

    a0, b0, h0, joint, ra0, rb0 = jax.tree.map(choose, own, other)
    a1, b1, h1, _, ra1, rb1 = jax.tree.map(choose, other, own)
    mid = mid_ref[...]
    inv = 1.0 / (h0 + b0 + mid)
    hd, gd = h0 * inv, mid * inv
    alpha = a0 + b0 * hd
    link = h0 * gd
    between = a1 + b0 * gd
    ra = [a + b * hd for a, b in zip(ra0, rb0)]
    rm = [a + b * gd for a, b in zip(ra1, rb0)]
    inv = 1.0 / (link + between + h1)
    hd, gd = link * inv, h1 * inv
    alpha = alpha + between * hd
    beta = b1 + between * gd
    ra = [a + m * hd for a, m in zip(ra, rm)]
    rb = [b + m * gd for b, m in zip(rb1, rm)]
    out = jnp.concatenate([*ra, *rb, pack(alpha, beta), pack(link * gd, joint)], 0)
    for d in range(send_ref.shape[0]):
        send_ref[d] = out


def y_solve_kernel(
    recv_ref, own_ref, other_ref, mid_ref, rb_ref, gy_ref, hy_ref, iy_ref, za_ref, zc_ref, zi_ref, heat_ref,
    out_ref, second,
):
    at_y = lax.axis_index("gy")
    core, chip = lax.rem(at_y, 2), lax.div(at_y, 2)
    count = recv_ref.shape[0]
    segments = [y_segment(lambda r, d=d: recv_ref[d, r : r + 8, :]) for d in range(count)]
    zero = jnp.zeros((MX, NZ), f32)
    left, left_src = zero, [zero, zero]
    right, right_src = zero, [zero, zero]
    for step in range(count - 1):
        d = step
        alpha, beta, link, _, ra, rb = segments[d]
        new, new_src = through(beta, alpha, link, segments[d + 1][3], left, rb, ra, left_src)
        left = jnp.where(d < chip, new, left)
        left_src = [jnp.where(d < chip, n, o) for n, o in zip(new_src, left_src)]
        d = count - 1 - step
        alpha, beta, link, joint, ra, rb = segments[d]
        new, new_src = through(alpha, beta, link, joint, right, ra, rb, right_src)
        right = jnp.where(d > chip, new, right)
        right_src = [jnp.where(d > chip, n, o) for n, o in zip(new_src, right_src)]

    def choose(a, b):
        return jnp.where(core == 0, a, b)

    alpha, beta, link, _, ra, rb = y_segment(lambda r: other_ref[r : r + 8, :])
    near, far = choose(alpha, beta), choose(beta, alpha)
    near_src = [choose(a, b) for a, b in zip(ra, rb)]
    far_src = [choose(b, a) for a, b in zip(ra, rb)]
    leak = choose(right, left)
    src = [choose(r, l) for r, l in zip(right_src, left_src)]
    new, new_src = through(near, far, link, mid_ref[...], leak, near_src, far_src, src)
    left, right = choose(left, new), choose(new, right)
    left_src, right_src = (
        [choose(l, n) for l, n in zip(left_src, new_src)],
        [choose(n, r) for n, r in zip(new_src, right_src)],
    )
    alpha, beta, link, _, ra, rb = y_segment(lambda r: own_ref[r : r + 8, :])
    u_first, u_next = two_nodes(
        alpha + left,
        beta + right,
        link,
        [a + s for a, s in zip(ra, left_src)],
        [b + s for b, s in zip(rb, right_src)],
    )

    def keep(y, u):
        for p in range(2):
            second[y * NX + p * MX : y * NX + (p + 1) * MX, :] = u[p]

    keep(0, u_first)
    keep(NY - 1, u_next)
    for y in range(NY - 2, 0, -1):
        t = y - 1
        gd = gy_ref[t * MX : (t + 1) * MX, :]
        hd = hy_ref[t * MX : (t + 1) * MX, :]
        inv = iy_ref[t * MX : (t + 1) * MX, :]
        b = [rb_ref[t * NX + p * MX : t * NX + (p + 1) * MX, :] for p in range(2)]
        u_next = [(inv * b[p] + hd * u_first[p]) + gd * u_next[p] for p in range(2)]
        keep(y, u_next)

    for n in range(MY):
        cells = [(2 * n + q, p) for q in range(2) for p in range(2)]
        v = [second[y * NX + p * MX : y * NX + (p + 1) * MX, :] for y, p in cells]
        for s in range(7):
            step = 1 << s
            at = s * MX * MY + n * MX
            low, high = za_ref[at : at + MX, :], zc_ref[at : at + MX, :]
            v = [w + (low * pltpu.roll(w, step, 1) + high * pltpu.roll(w, NZ - step, 1)) for w in v]
        inv = zi_ref[n * MX : (n + 1) * MX, :]
        for (y, p), w in zip(cells, v):
            where = pl.ds(p * NY + y, MX, stride=2 * NY)
            out_ref[where, :] = heat_ref[where, :] + inv * w


def call(kernel, ins, outs, scratch=(), outside=False, cost=20000):
    space = pltpu.HBM if outside else pltpu.VMEM
    return pl.pallas_call(
        kernel,
        out_shape=tuple(jax.ShapeDtypeStruct(s, f32) for s in outs),
        in_specs=[pl.BlockSpec(memory_space=space) for _ in ins],
        out_specs=tuple(pl.BlockSpec(memory_space=pltpu.VMEM) for _ in outs),
        scratch_shapes=scratch,
        compiler_params=pltpu.CompilerParams(vmem_limit_bytes=8 << 20),
        cost_estimate=pl.CostEstimate(flops=cost, bytes_accessed=cost, transcendentals=0),
    )(*ins)


def on_device(starting_heat_state, material_zone_ids, zone_diffusivity_lookup):
    heat = starting_heat_state.reshape(NX * NY, NZ)
    ids = material_zone_ids.reshape(MX * MY, NZ // 2)
    nx, ny = lax.axis_size("gx"), lax.axis_size("gy")
    k, inner, outer, heat = call(
        prepare_kernel,
        (ids, zone_diffusivity_lookup, heat),
        [(MX * MY, NZ), (NX + MX, NZ), (NX + MX, NZ), (NX * NY, NZ)],
        scratch=[
            pltpu.VMEM(ids.shape, jnp.int32),
            pltpu.SMEM(zone_diffusivity_lookup.shape, f32),
            pltpu.VMEM((MX * MY, NZ), f32),
            pltpu.SemaphoreType.DMA((3,)),
        ],
        outside=True,
    )
    cores = [(i, i ^ 1) for i in range(ny)]
    outer = lax.ppermute(outer, "gy", [(i, (i + (1 if i % 2 else -1)) % ny) for i in range(ny)])
    inner = lax.ppermute(inner, "gy", cores)
    tx, ty = NX - 2, NY - 2
    gx, hx, ix, px, gy, hy, iy, my, za, zc, zi = call(
        matrix_kernel,
        (k,),
        [(tx * MY, NZ)] * 3
        + [(40, NZ)]
        + [(ty * MX, NZ)] * 3
        + [(24, NZ)]
        + [(7 * MX * MY, NZ)] * 2
        + [(MX * MY, NZ)],
        cost=4000000,
    )
    send, rbx = call(
        right_side_kernel,
        (heat, k, inner, outer, gx, hx, px),
        [(XROWS, NZ), (tx * NY, NZ)],
    )
    quarter = [send] + [lax.ppermute(send, "gx", [(i, i ^ d) for i in range(nx)]) for d in (1, 2, 3)]
    (half,) = call(x_half_kernel, quarter, [(48, NZ)])
    half = lax.ppermute(half, "gx", [(i, nx - 1 - i) for i in range(nx)])
    own, mid, rby = call(
        x_solve_kernel,
        (*quarter, half, heat, k, inner, outer, rbx, gx, hx, ix, gy, hy, my),
        [(YROWS, NZ), (MX, NZ), (ty * MX * 2, NZ)],
        scratch=[pltpu.VMEM((NX * NY, NZ), f32)],
    )
    other = lax.ppermute(own, "gy", cores)
    (send,) = call(chip_kernel, (own, other, mid), [(ny // 2, YROWS, NZ)])
    groups = [list(range(c, ny, 2)) for c in range(2)]
    recv = lax.all_to_all(send, "gy", 0, 0, axis_index_groups=groups)
    (out,) = call(
        y_solve_kernel,
        (recv, own, other, mid, rby, gy, hy, iy, za, zc, zi, heat),
        [(NX * NY, NZ)],
        scratch=[pltpu.VMEM((NX * NY, NZ), f32)],
    )
    return out.reshape(starting_heat_state.shape)


def solution(mesh):
    return jax.shard_map(
        on_device,
        mesh=mesh,
        in_specs=(P("gx", "gy", None), P("gx", "gy", None), P()),
        out_specs=P("gx", "gy", None),
        check_vma=False,
    )
```

```python
import jax
import jax.numpy as jnp
from jax import lax
from jax.experimental import pallas as pl
from jax.experimental.pallas import tpu as pltpu
from jax.sharding import PartitionSpec as P

NX, NY, NZ = 16, 32, 128
MX, MY = NX // 2, NY // 2
XROWS = 104
YROWS = 48
f32 = jnp.float32


def lanes(shape):
    return lax.broadcasted_iota(jnp.int32, shape, 1)


def rows_of(shape):
    return lax.broadcasted_iota(jnp.int32, shape, 0)


def pack(first, second):
    return jnp.where(lanes(first.shape) % 2 == 0, first, second)


def unpack(both):
    even = lanes(both.shape) % 2 == 0
    first = jnp.where(even, both, pltpu.roll(both, 1, 1))
    second = jnp.where(even, pltpu.roll(both, NZ - 1, 1), both)
    return first, second


def through(near, far, link, beyond, leak, near_src, far_src, src):
    total = far + leak
    q = total + link
    cross = total * link
    f = beyond / ((near + beyond) * q + cross)
    new_leak = f * (near * q + cross)
    new_src = [f * (n * q + (e + s) * link) for n, e, s in zip(near_src, far_src, src)]
    return new_leak, new_src


def two_nodes(first, last, link, first_src, last_src):
    inv = 1.0 / (first * last + link * (first + last))
    low = [((last + link) * a + link * b) * inv for a, b in zip(first_src, last_src)]
    high = [((first + link) * b + link * a) * inv for a, b in zip(first_src, last_src)]
    return low, high


def eliminate(conduct, put):
    alpha = jnp.ones_like(conduct[0])
    beta = jnp.ones_like(conduct[0])
    link = conduct[0]
    for t in range(1, len(conduct)):
        g = conduct[t]
        inv = 1.0 / (link + beta + g)
        hd = link * inv
        gd = g * inv
        put(t - 1, gd, hd, inv)
        alpha = alpha + beta * hd
        link = link * gd
        beta = 1.0 + beta * gd
    return alpha, beta, link


def prepare_kernel(
    ids_hbm, table_hbm, heat_hbm, k_ref, inner_ref, outer_ref, ids_ref, table_ref, low_ref, high_ref, wide, sems
):
    copies = [
        pltpu.make_async_copy(table_hbm, table_ref, sems.at[0]),
        pltpu.make_async_copy(ids_hbm, ids_ref, sems.at[1]),
        pltpu.make_async_copy(heat_hbm.at[:, 0:8, :], low_ref, sems.at[2]),
        pltpu.make_async_copy(heat_hbm.at[:, NY - 8 : NY, :], high_ref, sems.at[3]),
    ]
    for copy in copies:
        copy.start()
    wide[...] = jnp.zeros(wide.shape, f32)
    copies[0].wait()
    copies[1].wait()
    ids = ids_ref[...]
    k = jnp.zeros(ids.shape, f32)
    for region in range(table_ref.shape[0]):
        k = jnp.where(ids == region, table_ref[region], k)
    wide[:, : NZ // 2] = k
    index = lanes(wide.shape) // 2
    k_ref[...] = jnp.take_along_axis(wide[...], index, axis=1, mode="promise_in_bounds")
    copies[2].wait()
    copies[3].wait()
    low = jnp.concatenate([low_ref[:, 0, :], k_ref[pl.ds(0, MX, stride=MY), :]], 0)
    high = jnp.concatenate([high_ref[:, 7, :], k_ref[pl.ds(MY - 1, MX, stride=MY), :]], 0)
    core = lax.rem(lax.axis_index("gy"), 2)
    inner_ref[...] = jnp.where(core == 0, high, low)
    outer_ref[...] = jnp.where(core == 0, low, high)


def matrix_kernel(
    k_ref, gx_ref, hx_ref, ix_ref, px_ref, gy_ref, hy_ref, iy_ref, my_ref, za_ref, zc_ref, zi_ref
):
    at_x, at_y = lax.axis_index("gx"), lax.axis_index("gy")
    last_x, last_y = lax.axis_size("gx") - 1, lax.axis_size("gy") - 1

    def chain(k):
        joints = []
        for m in range(len(k)):
            joints.append(2000.0 * k[m])
            if m + 1 < len(k):
                joints.append(1000.0 * (k[m] + k[m + 1]))
        return joints

    kx = [k_ref[m * MY : (m + 1) * MY, :] for m in range(MX)]

    def put_x(t, gd, hd, inv):
        gx_ref[t * MY : (t + 1) * MY, :] = gd
        hx_ref[t * MY : (t + 1) * MY, :] = hd
        ix_ref[t * MY : (t + 1) * MY, :] = inv

    alpha, beta, link = eliminate(chain(kx), put_x)
    alpha = alpha + jnp.where(at_x == 0, 1000.0, 0.0) * kx[0]
    beta = beta + jnp.where(at_x == last_x, 1000.0, 0.0) * kx[-1]
    px_ref[0:16, :] = pack(alpha, beta)
    px_ref[16:32, :] = pack(link, kx[0])
    px_ref[32:40, :] = pack(kx[-1][:8], kx[-1][8:])

    ky = [k_ref[pl.ds(n, MX, stride=MY), :] for n in range(MY)]

    def put_y(t, gd, hd, inv):
        gy_ref[t * MX : (t + 1) * MX, :] = gd
        hy_ref[t * MX : (t + 1) * MX, :] = hd
        iy_ref[t * MX : (t + 1) * MX, :] = inv

    alpha, beta, link = eliminate(chain(ky), put_y)
    my_ref[0:8, :] = alpha + jnp.where(at_y == 0, 1000.0, 0.0) * ky[0]
    my_ref[8:16, :] = beta + jnp.where(at_y == last_y, 1000.0, 0.0) * ky[-1]
    my_ref[16:24, :] = link

    group = 4
    for start in range(0, MY, group):
        k = jnp.concatenate(ky[start : start + group], 0)
        lane = lanes(k.shape)
        west = 0.25 * (k + jnp.where(lane == 0, 0.0, pltpu.roll(k, 1, 1)))
        east = 0.25 * (k + jnp.where(lane == NZ - 1, 0.0, pltpu.roll(k, NZ - 1, 1)))
        diag = 1.0 + (west + east)
        a = jnp.where(lane == 0, 0.0, west)
        c = jnp.where(lane == NZ - 1, 0.0, east)
        size = MX * group
        for s in range(7):
            step = 1 << s
            inv = 1.0 / diag
            low = a * pltpu.roll(inv, step, 1)
            high = c * pltpu.roll(inv, NZ - step, 1)
            at = s * MX * MY + start * MX
            za_ref[at : at + size, :] = low
            zc_ref[at : at + size, :] = high
            diag = diag - (low * pltpu.roll(c, step, 1) + high * pltpu.roll(a, NZ - step, 1))
            a = low * pltpu.roll(a, step, 1)
            c = high * pltpu.roll(c, NZ - step, 1)
        zi_ref[start * MX : start * MX + size, :] = 1.0 / diag


def right_side_kernel(heat_ref, k_ref, inner_ref, outer_ref, gx_ref, hx_ref, px_ref, send_ref, rb_ref):
    at_y = lax.axis_index("gy")
    core = lax.rem(at_y, 2)
    inner, outer = inner_ref[...], outer_ref[...]
    low = jnp.where(at_y == 0, 0.0, jnp.where(core == 0, outer, inner))
    high = jnp.where(at_y == lax.axis_size("gy") - 1, 0.0, jnp.where(core == 0, inner, outer))
    shape = (MY, NZ)
    lane, row = lanes(shape), rows_of(shape)
    ra = None
    rb = None
    for m in range(MX):
        k = k_ref[m * MY : (m + 1) * MY, :]
        k_low = low[NX + m : NX + m + 1]
        k_high = high[NX + m : NX + m + 1]
        face_low = 2000.0 * (k + jnp.where(row == 0, k_low, pltpu.roll(k, 1, 0)))
        face_high = 2000.0 * (k + jnp.where(row == MY - 1, k_high, pltpu.roll(k, MY - 1, 0)))
        face_mid = 4000.0 * k
        west = 0.5 * (k + jnp.where(lane == 0, 0.0, pltpu.roll(k, 1, 1)))
        east = 0.5 * (k + jnp.where(lane == NZ - 1, 0.0, pltpu.roll(k, NZ - 1, 1)))
        middle = 2.0 - (west + east)
        west = jnp.where(lane == 0, 0.0, west)
        east = jnp.where(lane == NZ - 1, 0.0, east)
        for x in (2 * m, 2 * m + 1):
            even = heat_ref[pl.ds(x * NY, MY, stride=2), :]
            odd = heat_ref[pl.ds(x * NY + 1, MY, stride=2), :]
            before = jnp.where(row == 0, low[x : x + 1], pltpu.roll(odd, 1, 0))
            after = jnp.where(row == MY - 1, high[x : x + 1], pltpu.roll(even, MY - 1, 0))
            flow = face_mid * (odd - even)
            r = []
            for v, along_y in (
                (even, flow - face_low * (even - before)),
                (odd, face_high * (after - odd) - flow),
            ):
                along_z = west * pltpu.roll(v, 1, 1) + east * pltpu.roll(v, NZ - 1, 1)
                r.append(along_y + (along_z + middle * v))
            if x == 0:
                ra = r
            elif x == 1:
                rb = r
            else:
                t = x - 2
                gd = gx_ref[t * MY : (t + 1) * MY, :]
                hd = hx_ref[t * MY : (t + 1) * MY, :]
                for q in range(2):
                    rb_ref[t * NY + q * MY : t * NY + (q + 1) * MY, :] = rb[q]
                ra = [a + b * hd for a, b in zip(ra, rb)]
                rb = [n + b * gd for n, b in zip(r, rb)]
    send_ref[0:16, :] = ra[0]
    send_ref[16:32, :] = ra[1]
    send_ref[32:48, :] = rb[0]
    send_ref[48:64, :] = rb[1]
    send_ref[64:104, :] = px_ref[...]


def x_segment(rows):
    alpha, beta = unpack(rows[64:80])
    link, k_first = unpack(rows[80:96])
    k_last = jnp.concatenate(unpack(rows[96:104]), 0)
    return alpha, beta, link, k_first, k_last, [rows[0:16], rows[16:32]], [rows[32:48], rows[48:64]]


def quarter(place, refs, segment):
    held = [r[...] for r in refs]
    segments = []
    for d in range(4):
        rows = held[0]
        for j in range(1, 4):
            rows = jnp.where(place == d ^ j, held[j], rows)
        segments.append(segment(rows))
    return segments


def x_half_kernel(own_ref, one_ref, two_ref, three_ref, send_ref):
    at = lax.axis_index("gx")
    upper = at >= 4
    place = lax.rem(at, 4)
    place = jnp.where(upper, 3 - place, place)

    def turn(segment):
        alpha, beta, link, k_first, k_last, ra, rb = segment

        def pick(a, b):
            return jnp.where(upper, a, b)

        near, far = pick(alpha, beta), pick(beta, alpha)
        k_near, k_far = pick(k_first, k_last), pick(k_last, k_first)
        near_src = [pick(a, b) for a, b in zip(ra, rb)]
        far_src = [pick(b, a) for a, b in zip(ra, rb)]
        return near, far, link, k_near, k_far, near_src, far_src

    segments = [turn(g) for g in quarter(place, (own_ref, one_ref, two_ref, three_ref), x_segment)]
    zero = jnp.zeros((MY, NZ), f32)
    leak, src = zero, [zero, zero]
    for d in range(3):
        near, far, link, k_near, _, near_src, far_src = segments[d]
        joint = 1000.0 * (k_near + segments[d + 1][4])
        leak, src = through(near, far, link, joint, leak, near_src, far_src, src)
    near, far, link, k_near, _, near_src, far_src = segments[3]
    total = far + leak
    part = link / (total + link)
    send_ref[0:16, :] = near_src[0] + (far_src[0] + src[0]) * part
    send_ref[16:32, :] = near_src[1] + (far_src[1] + src[1]) * part
    send_ref[32:48, :] = pack(near + total * part, k_near)


def x_solve_kernel(
    own_ref, one_ref, two_ref, three_ref, half_ref, heat_ref, k_ref, inner_ref, outer_ref, rb_ref, gx_ref,
    hx_ref, ix_ref, gy_ref, hy_ref, my_ref, core_ref, mid_ref, rby_ref, first,
):
    at = lax.axis_index("gx")
    place = lax.rem(at, 4)
    segments = quarter(place, (own_ref, one_ref, two_ref, three_ref), x_segment)
    half_leak, half_k = unpack(half_ref[32:48, :])
    upper = at >= 4
    joint = 1000.0 * (half_k + jnp.where(upper, segments[0][3], segments[3][4]))
    part = joint / (half_leak + joint)
    half_leak = half_leak * part
    half_src = [half_ref[0:16, :] * part, half_ref[16:32, :] * part]
    left = jnp.where(upper, half_leak, 0.0)
    left_src = [jnp.where(upper, v, 0.0) for v in half_src]
    right = jnp.where(upper, 0.0, half_leak)
    right_src = [jnp.where(upper, 0.0, v) for v in half_src]
    joints = [1000.0 * (segments[d][4] + segments[d + 1][3]) for d in range(3)]
    for step in range(3):
        d = step
        alpha, beta, link, _, _, ra, rb = segments[d]
        new, new_src = through(beta, alpha, link, joints[d], left, rb, ra, left_src)
        left = jnp.where(d < place, new, left)
        left_src = [jnp.where(d < place, n, o) for n, o in zip(new_src, left_src)]
        d = 3 - step
        alpha, beta, link, _, _, ra, rb = segments[d]
        new, new_src = through(alpha, beta, link, joints[d - 1], right, ra, rb, right_src)
        right = jnp.where(d > place, new, right)
        right_src = [jnp.where(d > place, n, o) for n, o in zip(new_src, right_src)]
    alpha, beta, link, _, _, ra, rb = x_segment(own_ref[...])
    u_first, u_next = two_nodes(
        alpha + left,
        beta + right,
        link,
        [a + s for a, s in zip(ra, left_src)],
        [b + s for b, s in zip(rb, right_src)],
    )

    def keep(x, u):
        for q in range(2):
            heat = heat_ref[pl.ds(x * NY + q, MY, stride=2), :]
            first[x * NY + q * MY : x * NY + (q + 1) * MY, :] = u[q] - 2.0 * heat

    keep(0, u_first)
    keep(NX - 1, u_next)
    for x in range(NX - 2, 0, -1):
        t = x - 1
        gd = gx_ref[t * MY : (t + 1) * MY, :]
        hd = hx_ref[t * MY : (t + 1) * MY, :]
        inv = ix_ref[t * MY : (t + 1) * MY, :]
        b = [rb_ref[t * NY + q * MY : t * NY + (q + 1) * MY, :] for q in range(2)]
        u_next = [(inv * b[q] + hd * u_first[q]) + gd * u_next[q] for q in range(2)]
        keep(x, u_next)

    def side(y):
        start = (y % 2) * MY + y // 2
        return [first[pl.ds(p * NY + start, MX, stride=2 * NY), :] for p in range(2)]

    ra = side(0)
    rb = side(1)
    for t in range(NY - 2):
        gd = gy_ref[t * MX : (t + 1) * MX, :]
        hd = hy_ref[t * MX : (t + 1) * MX, :]
        for p in range(2):
            rby_ref[t * NX + p * MX : t * NX + (p + 1) * MX, :] = rb[p]
        new = side(t + 2)
        ra = [a + b * hd for a, b in zip(ra, rb)]
        rb = [n + b * gd for n, b in zip(new, rb)]
    core = lax.rem(lax.axis_index("gy"), 2)
    k_low = k_ref[pl.ds(0, MX, stride=MY), :]
    k_high = k_ref[pl.ds(MY - 1, MX, stride=MY), :]
    mid_ref[...] = 1000.0 * (inner_ref[NX:, :] + jnp.where(core == 0, k_high, k_low))
    outer = 1000.0 * (outer_ref[NX:, :] + jnp.where(core == 0, k_low, k_high))
    core_ref[0:8, :] = ra[0]
    core_ref[8:16, :] = ra[1]
    core_ref[16:24, :] = rb[0]
    core_ref[24:32, :] = rb[1]
    core_ref[32:40, :] = pack(my_ref[0:8, :], my_ref[8:16, :])
    core_ref[40:48, :] = pack(my_ref[16:24, :], outer)


def y_segment(rows):
    alpha, beta = unpack(rows[32:40])
    link, joint = unpack(rows[40:48])
    return alpha, beta, link, joint, [rows[0:8], rows[8:16]], [rows[16:24], rows[24:32]]


def merge(first, second, joint):
    a0, b0, h0, outer, ra0, rb0 = first
    a1, b1, h1, _, ra1, rb1 = second
    inv = 1.0 / (h0 + b0 + joint)
    hd, gd = h0 * inv, joint * inv
    alpha = a0 + b0 * hd
    link = h0 * gd
    between = a1 + b0 * gd
    ra = [a + b * hd for a, b in zip(ra0, rb0)]
    rm = [a + b * gd for a, b in zip(ra1, rb0)]
    inv = 1.0 / (link + between + h1)
    hd, gd = link * inv, h1 * inv
    alpha = alpha + between * hd
    beta = b1 + between * gd
    ra = [a + m * hd for a, m in zip(ra, rm)]
    rb = [b + m * gd for b, m in zip(rb1, rm)]
    return alpha, beta, link * gd, outer, ra, rb


def store_segment(ref, segment):
    alpha, beta, link, joint, ra, rb = segment
    ref[...] = jnp.concatenate([*ra, *rb, pack(alpha, beta), pack(link, joint)], 0)


def chip_kernel(own_ref, other_ref, mid_ref, send_ref):
    core = lax.rem(lax.axis_index("gy"), 2)
    own, other = own_ref[...], other_ref[...]
    first = y_segment(jnp.where(core == 0, own, other))
    second = y_segment(jnp.where(core == 0, other, own))
    store_segment(send_ref, merge(first, second, mid_ref[...]))


def y_four_kernel(own_ref, one_ref, two_ref, three_ref, send_ref):
    place = lax.rem(lax.div(lax.axis_index("gy"), 2), 4)
    a, b, c, d = quarter(place, (own_ref, one_ref, two_ref, three_ref), y_segment)
    store_segment(send_ref, merge(merge(a, b, b[3]), merge(c, d, d[3]), c[3]))


def y_sweeps(segments, place, left, left_src, right, right_src):
    for step in range(3):
        d = step
        alpha, beta, link, _, ra, rb = segments[d]
        new, new_src = through(beta, alpha, link, segments[d + 1][3], left, rb, ra, left_src)
        left = jnp.where(d < place, new, left)
        left_src = [jnp.where(d < place, n, o) for n, o in zip(new_src, left_src)]
        d = 3 - step
        alpha, beta, link, joint, ra, rb = segments[d]
        new, new_src = through(alpha, beta, link, joint, right, ra, rb, right_src)
        right = jnp.where(d > place, new, right)
        right_src = [jnp.where(d > place, n, o) for n, o in zip(new_src, right_src)]
    return left, left_src, right, right_src


def y_solve_kernel(
    large0, large1, large2, large3, small0, small1, small2, small3, own_ref, other_ref, mid_ref, rb_ref, gy_ref,
    hy_ref, iy_ref, za_ref, zc_ref, zi_ref, heat_ref, out_ref, second,
):
    at_y = lax.axis_index("gy")
    core, chip = lax.rem(at_y, 2), lax.div(at_y, 2)
    zero = jnp.zeros((MX, NZ), f32)
    large = quarter(lax.div(chip, 4), (large0, large1, large2, large3), y_segment)
    small = quarter(lax.rem(chip, 4), (small0, small1, small2, small3), y_segment)
    state = y_sweeps(large, lax.div(chip, 4), zero, [zero, zero], zero, [zero, zero])
    left, left_src, right, right_src = y_sweeps(small, lax.rem(chip, 4), *state)

    def choose(a, b):
        return jnp.where(core == 0, a, b)

    alpha, beta, link, _, ra, rb = y_segment(other_ref[...])
    near, far = choose(alpha, beta), choose(beta, alpha)
    near_src = [choose(a, b) for a, b in zip(ra, rb)]
    far_src = [choose(b, a) for a, b in zip(ra, rb)]
    leak = choose(right, left)
    src = [choose(r, l) for r, l in zip(right_src, left_src)]
    new, new_src = through(near, far, link, mid_ref[...], leak, near_src, far_src, src)
    left, right = choose(left, new), choose(new, right)
    left_src, right_src = (
        [choose(l, n) for l, n in zip(left_src, new_src)],
        [choose(n, r) for n, r in zip(new_src, right_src)],
    )
    alpha, beta, link, _, ra, rb = y_segment(own_ref[...])
    u_first, u_next = two_nodes(
        alpha + left,
        beta + right,
        link,
        [a + s for a, s in zip(ra, left_src)],
        [b + s for b, s in zip(rb, right_src)],
    )

    def keep(y, u):
        for p in range(2):
            second[y * NX + p * MX : y * NX + (p + 1) * MX, :] = u[p]

    keep(0, u_first)
    keep(NY - 1, u_next)
    for y in range(NY - 2, 0, -1):
        t = y - 1
        gd = gy_ref[t * MX : (t + 1) * MX, :]
        hd = hy_ref[t * MX : (t + 1) * MX, :]
        inv = iy_ref[t * MX : (t + 1) * MX, :]
        b = [rb_ref[t * NX + p * MX : t * NX + (p + 1) * MX, :] for p in range(2)]
        u_next = [(inv * b[p] + hd * u_first[p]) + gd * u_next[p] for p in range(2)]
        keep(y, u_next)

    for n in range(MY):
        cells = [(2 * n + q, p) for q in range(2) for p in range(2)]
        v = [second[y * NX + p * MX : y * NX + (p + 1) * MX, :] for y, p in cells]
        for s in range(7):
            step = 1 << s
            at = s * MX * MY + n * MX
            low, high = za_ref[at : at + MX, :], zc_ref[at : at + MX, :]
            v = [w + (low * pltpu.roll(w, step, 1) + high * pltpu.roll(w, NZ - step, 1)) for w in v]
        inv = zi_ref[n * MX : (n + 1) * MX, :]
        for (y, p), w in zip(cells, v):
            where = pl.ds(p * NY + y, MX, stride=2 * NY)
            out_ref[where, :] = heat_ref[where, :] + inv * w


def call(kernel, ins, outs, scratch=(), outside=False, cost=20000, limit=8 << 20):
    space = pltpu.HBM if outside else pltpu.VMEM
    return pl.pallas_call(
        kernel,
        out_shape=tuple(jax.ShapeDtypeStruct(s, f32) for s in outs),
        in_specs=[pl.BlockSpec(memory_space=space) for _ in ins],
        out_specs=tuple(pl.BlockSpec(memory_space=pltpu.VMEM) for _ in outs),
        scratch_shapes=scratch,
        compiler_params=pltpu.CompilerParams(vmem_limit_bytes=limit),
        cost_estimate=pl.CostEstimate(flops=cost, bytes_accessed=cost, transcendentals=0),
    )(*ins)


def on_device(starting_heat_state, material_zone_ids, zone_diffusivity_lookup):
    heat = starting_heat_state.reshape(NX * NY, NZ)
    ids = material_zone_ids.reshape(MX * MY, NZ // 2)
    nx, ny = lax.axis_size("gx"), lax.axis_size("gy")
    k, inner, outer = call(
        prepare_kernel,
        (ids, zone_diffusivity_lookup, starting_heat_state),
        [(MX * MY, NZ), (NX + MX, NZ), (NX + MX, NZ)],
        scratch=[
            pltpu.VMEM(ids.shape, jnp.int32),
            pltpu.SMEM(zone_diffusivity_lookup.shape, f32),
            pltpu.VMEM((NX, 8, NZ), f32),
            pltpu.VMEM((NX, 8, NZ), f32),
            pltpu.VMEM((MX * MY, NZ), f32),
            pltpu.SemaphoreType.DMA((4,)),
        ],
        outside=True,
        limit=55500 << 10,
    )
    cores = [(i, i ^ 1) for i in range(ny)]
    inner = lax.ppermute(inner, "gy", cores)
    outer = lax.ppermute(outer, "gy", [(i, (i + (1 if i % 2 else -1)) % ny) for i in range(ny)])
    tx, ty = NX - 2, NY - 2
    gx, hx, ix, px, gy, hy, iy, my, za, zc, zi = call(
        matrix_kernel,
        (k,),
        [(tx * MY, NZ)] * 3
        + [(40, NZ)]
        + [(ty * MX, NZ)] * 3
        + [(24, NZ)]
        + [(7 * MX * MY, NZ)] * 2
        + [(MX * MY, NZ)],
        cost=4000000,
    )
    send, rbx = call(
        right_side_kernel,
        (heat, k, inner, outer, gx, hx, px),
        [(XROWS, NZ), (tx * NY, NZ)],
    )
    near = [send] + [lax.ppermute(send, "gx", [(i, i ^ d) for i in range(nx)]) for d in (1, 2, 3)]
    (half,) = call(x_half_kernel, near, [(48, NZ)])
    half = lax.ppermute(half, "gx", [(i, nx - 1 - i) for i in range(nx)])
    own, mid, rby = call(
        x_solve_kernel,
        (*near, half, heat, k, inner, outer, rbx, gx, hx, ix, gy, hy, my),
        [(YROWS, NZ), (MX, NZ), (ty * MX * 2, NZ)],
        scratch=[pltpu.VMEM((NX * NY, NZ), f32)],
    )
    other = lax.ppermute(own, "gy", cores)
    (chip,) = call(chip_kernel, (own, other, mid), [(YROWS, NZ)])
    small = [chip] + [lax.ppermute(chip, "gy", [(i, i ^ (2 * d)) for i in range(ny)]) for d in (1, 2, 3)]
    (four,) = call(y_four_kernel, small, [(YROWS, NZ)])
    large = [four] + [lax.ppermute(four, "gy", [(i, i ^ (8 * d)) for i in range(ny)]) for d in (1, 2, 3)]
    (out,) = call(
        y_solve_kernel,
        (*large, *small, own, other, mid, rby, gy, hy, iy, za, zc, zi, heat),
        [(NX * NY, NZ)],
        scratch=[pltpu.VMEM((NX * NY, NZ), f32)],
    )
    return out.reshape(starting_heat_state.shape)


def solution(mesh):
    return jax.shard_map(
        on_device,
        mesh=mesh,
        in_specs=(P("gx", "gy", None), P("gx", "gy", None), P()),
        out_specs=P("gx", "gy", None),
        check_vma=False,
    )
```

```python
import jax
import jax.numpy as jnp
from jax import lax
from jax.experimental import pallas as pl
from jax.experimental.pallas import tpu as pltpu
from jax.sharding import PartitionSpec as P

NX, NY, NZ = 16, 32, 128
MX, MY = NX // 2, NY // 2
XROWS = 104
YROWS = 48
f32 = jnp.float32


def lanes(shape):
    return lax.broadcasted_iota(jnp.int32, shape, 1)


def rows_of(shape):
    return lax.broadcasted_iota(jnp.int32, shape, 0)


def pack(first, second):
    return jnp.where(lanes(first.shape) % 2 == 0, first, second)


def unpack(both):
    even = lanes(both.shape) % 2 == 0
    first = jnp.where(even, both, pltpu.roll(both, 1, 1))
    second = jnp.where(even, pltpu.roll(both, NZ - 1, 1), both)
    return first, second


def through(near, far, link, beyond, leak, near_src, far_src, src):
    total = far + leak
    q = total + link
    cross = total * link
    f = beyond / ((near + beyond) * q + cross)
    new_leak = f * (near * q + cross)
    new_src = [f * (n * q + (e + s) * link) for n, e, s in zip(near_src, far_src, src)]
    return new_leak, new_src


def two_nodes(first, last, link, first_src, last_src):
    inv = 1.0 / (first * last + link * (first + last))
    low = [((last + link) * a + link * b) * inv for a, b in zip(first_src, last_src)]
    high = [((first + link) * b + link * a) * inv for a, b in zip(first_src, last_src)]
    return low, high


def eliminate(conduct, put):
    alpha = jnp.ones_like(conduct[0])
    beta = jnp.ones_like(conduct[0])
    link = conduct[0]
    for t in range(1, len(conduct)):
        g = conduct[t]
        inv = 1.0 / (link + beta + g)
        hd = link * inv
        gd = g * inv
        put(t - 1, gd, hd, inv)
        alpha = alpha + beta * hd
        link = link * gd
        beta = 1.0 + beta * gd
    return alpha, beta, link


def prepare_kernel(
    ids_hbm, heat_hbm, inner_ref, outer_ref, ids_low, ids_high, heat_low, heat_high, sems
):
    copies = [
        pltpu.make_async_copy(source, place, sems.at[i])
        for i, (source, place) in enumerate(
            (
                (heat_hbm.at[:, 0:8, :], heat_low),
                (heat_hbm.at[:, NY - 8 : NY, :], heat_high),
                (ids_hbm.at[:, 0:8, :], ids_low),
                (ids_hbm.at[:, MY - 8 : MY, :], ids_high),
            )
        )
    ]
    for copy in copies:
        copy.start()
    core = lax.rem(lax.axis_index("gy"), 2)
    inner_ref[NX:, :] = jnp.zeros((MX, NZ), f32)
    outer_ref[NX:, :] = jnp.zeros((MX, NZ), f32)
    for copy in copies:
        copy.wait()
    low, high = heat_low[:, 0, :], heat_high[:, 7, :]
    inner_ref[:NX, :] = jnp.where(core == 0, high, low)
    outer_ref[:NX, :] = jnp.where(core == 0, low, high)
    low, high = ids_low[:, 0, :], ids_high[:, 7, :]
    inner_ref[NX:, : NZ // 2] = jnp.where(core == 0, high, low).astype(f32)
    outer_ref[NX:, : NZ // 2] = jnp.where(core == 0, low, high).astype(f32)


def take(values, index):
    return jnp.take_along_axis(values, index, axis=1, mode="promise_in_bounds")


def chain(k):
    joints = []
    for m in range(len(k)):
        joints.append(2000.0 * k[m])
        if m + 1 < len(k):
            joints.append(1000.0 * (k[m] + k[m + 1]))
    return joints


def x_matrix_kernel(
    ids_ref, table_ref, k_ref, lookup_ref, gx_ref, hx_ref, ix_ref, px_ref, wide
):
    ids = ids_ref[...]
    k = jnp.zeros(ids.shape, f32)
    lookup = jnp.zeros(lookup_ref.shape, f32)
    for region in range(table_ref.shape[0]):
        k = jnp.where(ids == region, table_ref[region], k)
        lookup = jnp.where(lanes(lookup.shape) == region, table_ref[region], lookup)
    lookup_ref[...] = lookup
    wide[...] = jnp.zeros(wide.shape, f32)
    wide[:, : NZ // 2] = k
    k_ref[...] = take(wide[...], lanes(wide.shape) // 2)
    at_x = lax.axis_index("gx")
    last_x = lax.axis_size("gx") - 1
    kx = [k_ref[m * MY : (m + 1) * MY, :] for m in range(MX)]

    def put_x(t, gd, hd, inv):
        gx_ref[t * MY : (t + 1) * MY, :] = gd
        hx_ref[t * MY : (t + 1) * MY, :] = hd
        ix_ref[t * MY : (t + 1) * MY, :] = inv

    alpha, beta, link = eliminate(chain(kx), put_x)
    alpha = alpha + jnp.where(at_x == 0, 1000.0, 0.0) * kx[0]
    beta = beta + jnp.where(at_x == last_x, 1000.0, 0.0) * kx[-1]
    px_ref[0:16, :] = pack(alpha, beta)
    px_ref[16:32, :] = pack(link, kx[0])
    px_ref[32:40, :] = pack(kx[-1][:8], kx[-1][8:])


def yz_matrix_kernel(
    k_ref, beside_ref, gy_ref, hy_ref, iy_ref, my_ref, mid_ref, za_ref, zc_ref, zi_ref, zo_ref
):
    at_y = lax.axis_index("gy")
    last_y = lax.axis_size("gy") - 1
    core = lax.rem(at_y, 2)
    ky = [k_ref[pl.ds(n, MX, stride=MY), :] for n in range(MY)]
    mid_ref[...] = 1000.0 * (beside_ref[:MX, :] + jnp.where(core == 0, ky[-1], ky[0]))
    outer = 1000.0 * (beside_ref[MX:, :] + jnp.where(core == 0, ky[0], ky[-1]))

    def put_y(t, gd, hd, inv):
        gy_ref[t * MX : (t + 1) * MX, :] = gd
        hy_ref[t * MX : (t + 1) * MX, :] = hd
        iy_ref[t * MX : (t + 1) * MX, :] = inv

    alpha, beta, link = eliminate(chain(ky), put_y)
    alpha = alpha + jnp.where(at_y == 0, 1000.0, 0.0) * ky[0]
    beta = beta + jnp.where(at_y == last_y, 1000.0, 0.0) * ky[-1]
    my_ref[0:8, :] = pack(alpha, beta)
    my_ref[8:16, :] = pack(link, outer)

    group = 4
    for start in range(0, MY, group):
        k = jnp.concatenate(ky[start : start + group], 0)
        lane = lanes(k.shape)
        west = 0.25 * (k + jnp.where(lane == 0, 0.0, pltpu.roll(k, 1, 1)))
        east = 0.25 * (k + jnp.where(lane == NZ - 1, 0.0, pltpu.roll(k, NZ - 1, 1)))
        diag = 1.0 + (west + east)
        a = jnp.where(lane == 0, 0.0, west)
        c = jnp.where(lane == NZ - 1, 0.0, east)
        size = MX * group

        def double(coefficient):
            return jnp.where(lane % 2 == 0, coefficient, pltpu.roll(coefficient, 1, 1))

        for s in range(7):
            step = 1 << s
            inv = 1.0 / diag
            if s == 0:
                for i, odd in enumerate((inv, a * inv, c * inv)):
                    at = i * MX * MY + start * MX
                    zo_ref[at : at + size, :] = odd
            low = a * pltpu.roll(inv, step, 1)
            high = c * pltpu.roll(inv, NZ - step, 1)
            at = s * MX * MY + start * MX
            if 2 * step == NZ:
                za_ref[at : at + size, :] = double(low + high)
            else:
                za_ref[at : at + size, :] = double(low)
                zc_ref[at : at + size, :] = double(high)
            diag = diag - (low * pltpu.roll(c, step, 1) + high * pltpu.roll(a, NZ - step, 1))
            a = low * pltpu.roll(a, step, 1)
            c = high * pltpu.roll(c, NZ - step, 1)
        zi_ref[start * MX : start * MX + size, :] = double(1.0 / diag)


def right_side_kernel(
    heat_ref, k_ref, lookup_ref, outer_ref, inner_ref, gx_ref, hx_ref, px_ref, send_ref, rb_ref, beside_ref
):
    at_y = lax.axis_index("gy")
    core = lax.rem(at_y, 2)

    def conduct(ref):
        index = take(ref[NX:, :], lanes((MX, NZ)) // 2).astype(jnp.int32)
        return take(lookup_ref[...], index)

    inner = jnp.concatenate([inner_ref[:NX, :], conduct(inner_ref)], 0)
    outer = jnp.concatenate([outer_ref[:NX, :], conduct(outer_ref)], 0)
    beside_ref[:MX, :] = inner[NX:]
    beside_ref[MX:, :] = outer[NX:]
    low = jnp.where(at_y == 0, 0.0, jnp.where(core == 0, outer, inner))
    high = jnp.where(at_y == lax.axis_size("gy") - 1, 0.0, jnp.where(core == 0, inner, outer))
    shape = (MY, NZ)
    lane, row = lanes(shape), rows_of(shape)
    ra = None
    rb = None
    for m in range(MX):
        k = k_ref[m * MY : (m + 1) * MY, :]
        k_low = low[NX + m : NX + m + 1]
        k_high = high[NX + m : NX + m + 1]
        face_low = 2000.0 * (k + jnp.where(row == 0, k_low, pltpu.roll(k, 1, 0)))
        face_high = 2000.0 * (k + jnp.where(row == MY - 1, k_high, pltpu.roll(k, MY - 1, 0)))
        face_mid = 4000.0 * k
        west = 0.5 * (k + jnp.where(lane == 0, 0.0, pltpu.roll(k, 1, 1)))
        east = 0.5 * (k + jnp.where(lane == NZ - 1, 0.0, pltpu.roll(k, NZ - 1, 1)))
        middle = 2.0 - (west + east)
        west = jnp.where(lane == 0, 0.0, west)
        east = jnp.where(lane == NZ - 1, 0.0, east)
        for x in (2 * m, 2 * m + 1):
            even = heat_ref[pl.ds(x * NY, MY, stride=2), :]
            odd = heat_ref[pl.ds(x * NY + 1, MY, stride=2), :]
            before = jnp.where(row == 0, low[x : x + 1], pltpu.roll(odd, 1, 0))
            after = jnp.where(row == MY - 1, high[x : x + 1], pltpu.roll(even, MY - 1, 0))
            flow = face_mid * (odd - even)
            r = []
            for v, along_y in (
                (even, flow - face_low * (even - before)),
                (odd, face_high * (after - odd) - flow),
            ):
                along_z = west * pltpu.roll(v, 1, 1) + east * pltpu.roll(v, NZ - 1, 1)
                r.append(along_y + (along_z + middle * v))
            if x == 0:
                ra = r
            elif x == 1:
                rb = r
            else:
                t = x - 2
                gd = gx_ref[t * MY : (t + 1) * MY, :]
                hd = hx_ref[t * MY : (t + 1) * MY, :]
                for q in range(2):
                    rb_ref[t * NY + q * MY : t * NY + (q + 1) * MY, :] = rb[q]
                ra = [a + b * hd for a, b in zip(ra, rb)]
                rb = [n + b * gd for n, b in zip(r, rb)]
    send_ref[0:16, :] = ra[0]
    send_ref[16:32, :] = ra[1]
    send_ref[32:48, :] = rb[0]
    send_ref[48:64, :] = rb[1]
    send_ref[64:104, :] = px_ref[...]


def x_segment(rows):
    alpha, beta = unpack(rows[64:80])
    link, k_first = unpack(rows[80:96])
    k_last = jnp.concatenate(unpack(rows[96:104]), 0)
    return alpha, beta, link, k_first, k_last, [rows[0:16], rows[16:32]], [rows[32:48], rows[48:64]]


def quarter(place, refs, segment):
    held = [r[...] for r in refs]
    segments = []
    for d in range(4):
        rows = held[0]
        for j in range(1, 4):
            rows = jnp.where(place == d ^ j, held[j], rows)
        segments.append(segment(rows))
    return segments


def x_half_kernel(own_ref, one_ref, two_ref, three_ref, send_ref):
    at = lax.axis_index("gx")
    upper = at >= 4
    place = lax.rem(at, 4)
    place = jnp.where(upper, 3 - place, place)

    def turn(segment):
        alpha, beta, link, k_first, k_last, ra, rb = segment

        def pick(a, b):
            return jnp.where(upper, a, b)

        near, far = pick(alpha, beta), pick(beta, alpha)
        k_near, k_far = pick(k_first, k_last), pick(k_last, k_first)
        near_src = [pick(a, b) for a, b in zip(ra, rb)]
        far_src = [pick(b, a) for a, b in zip(ra, rb)]
        return near, far, link, k_near, k_far, near_src, far_src

    segments = [turn(g) for g in quarter(place, (own_ref, one_ref, two_ref, three_ref), x_segment)]
    zero = jnp.zeros((MY, NZ), f32)
    leak, src = zero, [zero, zero]
    for d in range(3):
        near, far, link, k_near, _, near_src, far_src = segments[d]
        joint = 1000.0 * (k_near + segments[d + 1][4])
        leak, src = through(near, far, link, joint, leak, near_src, far_src, src)
    near, far, link, k_near, _, near_src, far_src = segments[3]
    total = far + leak
    part = link / (total + link)
    send_ref[0:16, :] = near_src[0] + (far_src[0] + src[0]) * part
    send_ref[16:32, :] = near_src[1] + (far_src[1] + src[1]) * part
    send_ref[32:48, :] = pack(near + total * part, k_near)


def x_solve_kernel(
    own_ref, one_ref, two_ref, three_ref, half_ref, heat_ref, rb_ref, gx_ref, hx_ref, ix_ref, gy_ref, hy_ref,
    my_ref, core_ref, rby_ref, first,
):
    at = lax.axis_index("gx")
    place = lax.rem(at, 4)
    segments = quarter(place, (own_ref, one_ref, two_ref, three_ref), x_segment)
    half_leak, half_k = unpack(half_ref[32:48, :])
    upper = at >= 4
    joint = 1000.0 * (half_k + jnp.where(upper, segments[0][3], segments[3][4]))
    part = joint / (half_leak + joint)
    half_leak = half_leak * part
    half_src = [half_ref[0:16, :] * part, half_ref[16:32, :] * part]
    left = jnp.where(upper, half_leak, 0.0)
    left_src = [jnp.where(upper, v, 0.0) for v in half_src]
    right = jnp.where(upper, 0.0, half_leak)
    right_src = [jnp.where(upper, 0.0, v) for v in half_src]
    joints = [1000.0 * (segments[d][4] + segments[d + 1][3]) for d in range(3)]
    for step in range(3):
        d = step
        alpha, beta, link, _, _, ra, rb = segments[d]
        new, new_src = through(beta, alpha, link, joints[d], left, rb, ra, left_src)
        left = jnp.where(d < place, new, left)
        left_src = [jnp.where(d < place, n, o) for n, o in zip(new_src, left_src)]
        d = 3 - step
        alpha, beta, link, _, _, ra, rb = segments[d]
        new, new_src = through(alpha, beta, link, joints[d - 1], right, ra, rb, right_src)
        right = jnp.where(d > place, new, right)
        right_src = [jnp.where(d > place, n, o) for n, o in zip(new_src, right_src)]
    alpha, beta, link, _, _, ra, rb = x_segment(own_ref[...])
    u_first, u_next = two_nodes(
        alpha + left,
        beta + right,
        link,
        [a + s for a, s in zip(ra, left_src)],
        [b + s for b, s in zip(rb, right_src)],
    )

    def keep(x, u):
        for q in range(2):
            heat = heat_ref[pl.ds(x * NY + q, MY, stride=2), :]
            first[x * NY + q * MY : x * NY + (q + 1) * MY, :] = u[q] - 2.0 * heat

    keep(0, u_first)
    keep(NX - 1, u_next)
    for x in range(NX - 2, 0, -1):
        t = x - 1
        gd = gx_ref[t * MY : (t + 1) * MY, :]
        hd = hx_ref[t * MY : (t + 1) * MY, :]
        inv = ix_ref[t * MY : (t + 1) * MY, :]
        b = [rb_ref[t * NY + q * MY : t * NY + (q + 1) * MY, :] for q in range(2)]
        u_next = [(inv * b[q] + hd * u_first[q]) + gd * u_next[q] for q in range(2)]
        keep(x, u_next)

    def side(y):
        start = (y % 2) * MY + y // 2
        return [first[pl.ds(p * NY + start, MX, stride=2 * NY), :] for p in range(2)]

    ra = side(0)
    rb = side(1)
    for t in range(NY - 2):
        gd = gy_ref[t * MX : (t + 1) * MX, :]
        hd = hy_ref[t * MX : (t + 1) * MX, :]
        for p in range(2):
            rby_ref[t * NX + p * MX : t * NX + (p + 1) * MX, :] = rb[p]
        new = side(t + 2)
        ra = [a + b * hd for a, b in zip(ra, rb)]
        rb = [n + b * gd for n, b in zip(new, rb)]
    core_ref[0:8, :] = ra[0]
    core_ref[8:16, :] = ra[1]
    core_ref[16:24, :] = rb[0]
    core_ref[24:32, :] = rb[1]
    core_ref[32:48, :] = my_ref[...]


def y_segment(rows):
    alpha, beta = unpack(rows[32:40])
    link, joint = unpack(rows[40:48])
    return alpha, beta, link, joint, [rows[0:8], rows[8:16]], [rows[16:24], rows[24:32]]


def merge(first, second, joint):
    a0, b0, h0, outer, ra0, rb0 = first
    a1, b1, h1, _, ra1, rb1 = second
    inv = 1.0 / (h0 + b0 + joint)
    hd, gd = h0 * inv, joint * inv
    alpha = a0 + b0 * hd
    link = h0 * gd
    between = a1 + b0 * gd
    ra = [a + b * hd for a, b in zip(ra0, rb0)]
    rm = [a + b * gd for a, b in zip(ra1, rb0)]
    inv = 1.0 / (link + between + h1)
    hd, gd = link * inv, h1 * inv
    alpha = alpha + between * hd
    beta = b1 + between * gd
    ra = [a + m * hd for a, m in zip(ra, rm)]
    rb = [b + m * gd for b, m in zip(rb1, rm)]
    return alpha, beta, link * gd, outer, ra, rb


def store_segment(ref, segment):
    alpha, beta, link, joint, ra, rb = segment
    ref[...] = jnp.concatenate([*ra, *rb, pack(alpha, beta), pack(link, joint)], 0)


def chip_kernel(own_ref, other_ref, mid_ref, send_ref):
    core = lax.rem(lax.axis_index("gy"), 2)
    own, other = own_ref[...], other_ref[...]
    first = y_segment(jnp.where(core == 0, own, other))
    second = y_segment(jnp.where(core == 0, other, own))
    store_segment(send_ref, merge(first, second, mid_ref[...]))


def y_four_kernel(own_ref, one_ref, two_ref, three_ref, send_ref):
    place = lax.rem(lax.div(lax.axis_index("gy"), 2), 4)
    a, b, c, d = quarter(place, (own_ref, one_ref, two_ref, three_ref), y_segment)
    store_segment(send_ref, merge(merge(a, b, b[3]), merge(c, d, d[3]), c[3]))


def y_sweeps(segments, place, left, left_src, right, right_src):
    for step in range(3):
        d = step
        alpha, beta, link, _, ra, rb = segments[d]
        new, new_src = through(beta, alpha, link, segments[d + 1][3], left, rb, ra, left_src)
        left = jnp.where(d < place, new, left)
        left_src = [jnp.where(d < place, n, o) for n, o in zip(new_src, left_src)]
        d = 3 - step
        alpha, beta, link, joint, ra, rb = segments[d]
        new, new_src = through(alpha, beta, link, joint, right, ra, rb, right_src)
        right = jnp.where(d > place, new, right)
        right_src = [jnp.where(d > place, n, o) for n, o in zip(new_src, right_src)]
    return left, left_src, right, right_src


def y_solve_kernel(
    large0, large1, large2, large3, small0, small1, small2, small3, own_ref, other_ref, mid_ref, rb_ref, gy_ref,
    hy_ref, iy_ref, za_ref, zc_ref, zi_ref, zo_ref, heat_ref, out_ref, second,
):
    at_y = lax.axis_index("gy")
    core, chip = lax.rem(at_y, 2), lax.div(at_y, 2)
    zero = jnp.zeros((MX, NZ), f32)
    large = quarter(lax.div(chip, 4), (large0, large1, large2, large3), y_segment)
    small = quarter(lax.rem(chip, 4), (small0, small1, small2, small3), y_segment)
    state = y_sweeps(large, lax.div(chip, 4), zero, [zero, zero], zero, [zero, zero])
    left, left_src, right, right_src = y_sweeps(small, lax.rem(chip, 4), *state)

    def choose(a, b):
        return jnp.where(core == 0, a, b)

    alpha, beta, link, _, ra, rb = y_segment(other_ref[...])
    near, far = choose(alpha, beta), choose(beta, alpha)
    near_src = [choose(a, b) for a, b in zip(ra, rb)]
    far_src = [choose(b, a) for a, b in zip(ra, rb)]
    leak = choose(right, left)
    src = [choose(r, l) for r, l in zip(right_src, left_src)]
    new, new_src = through(near, far, link, mid_ref[...], leak, near_src, far_src, src)
    left, right = choose(left, new), choose(new, right)
    left_src, right_src = (
        [choose(l, n) for l, n in zip(left_src, new_src)],
        [choose(n, r) for n, r in zip(new_src, right_src)],
    )
    alpha, beta, link, _, ra, rb = y_segment(own_ref[...])
    u_first, u_next = two_nodes(
        alpha + left,
        beta + right,
        link,
        [a + s for a, s in zip(ra, left_src)],
        [b + s for b, s in zip(rb, right_src)],
    )

    def keep(y, u):
        for p in range(2):
            second[y * NX + p * MX : y * NX + (p + 1) * MX, :] = u[p]

    keep(0, u_first)
    keep(NY - 1, u_next)
    for y in range(NY - 2, 0, -1):
        t = y - 1
        gd = gy_ref[t * MX : (t + 1) * MX, :]
        hd = hy_ref[t * MX : (t + 1) * MX, :]
        inv = iy_ref[t * MX : (t + 1) * MX, :]
        b = [rb_ref[t * NX + p * MX : t * NX + (p + 1) * MX, :] for p in range(2)]
        u_next = [(inv * b[p] + hd * u_first[p]) + gd * u_next[p] for p in range(2)]
        keep(y, u_next)

    even = lanes((MX, NZ)) % 2 == 0

    def turned(v, step):
        return pltpu.roll(v, step % NZ, 1)

    for n in range(MY):
        rows = slice(n * MX, (n + 1) * MX)
        inv, odd, odd_low, odd_high = zi_ref[rows, :], *(
            zo_ref[i * MX * MY + n * MX : i * MX * MY + (n + 1) * MX, :] for i in range(3)
        )
        for p in range(2):
            a, b = (second[y * NX + p * MX : y * NX + (p + 1) * MX, :] for y in (2 * n, 2 * n + 1))
            w = jnp.where(even, a, turned(b, 1))
            before = jnp.where(even, turned(a, 1), turned(b, 2))
            after = jnp.where(even, turned(a, -1), b)
            for s in range(7):
                step = 1 << s
                at = slice(s * MX * MY + n * MX, s * MX * MY + (n + 1) * MX)
                if s > 0:
                    before = turned(w, step)
                if 2 * step == NZ:
                    w = w + za_ref[at, :] * before
                else:
                    if s > 0:
                        after = turned(w, -step)
                    w = w + (za_ref[at, :] * before + zc_ref[at, :] * after)
            w = inv * w
            next_w = turned(w, -1)
            a = jnp.where(even, w, odd * a + (odd_low * turned(w, 1) + odd_high * next_w))
            b = jnp.where(even, next_w, odd * b + (odd_low * w + odd_high * turned(w, -2)))
            for y, v in ((2 * n, a), (2 * n + 1, b)):
                where = pl.ds(p * NY + y, MX, stride=2 * NY)
                out_ref[where, :] = heat_ref[where, :] + v


def call(kernel, ins, outs, scratch=(), outside=False, smem=(), cost=20000, limit=8 << 20):
    space = pltpu.HBM if outside else pltpu.VMEM
    return pl.pallas_call(
        kernel,
        out_shape=tuple(jax.ShapeDtypeStruct(s, f32) for s in outs),
        in_specs=[pl.BlockSpec(memory_space=pltpu.SMEM if i in smem else space) for i in range(len(ins))],
        out_specs=tuple(pl.BlockSpec(memory_space=pltpu.VMEM) for _ in outs),
        scratch_shapes=scratch,
        compiler_params=pltpu.CompilerParams(vmem_limit_bytes=limit),
        cost_estimate=pl.CostEstimate(flops=cost, bytes_accessed=cost, transcendentals=0),
    )(*ins)


def on_device(starting_heat_state, material_zone_ids, zone_diffusivity_lookup):
    heat = starting_heat_state.reshape(NX * NY, NZ)
    ids = material_zone_ids.reshape(MX * MY, NZ // 2)
    nx, ny = lax.axis_size("gx"), lax.axis_size("gy")
    inner, outer = call(
        prepare_kernel,
        (material_zone_ids, starting_heat_state),
        [(NX + MX, NZ)] * 2,
        scratch=[
            pltpu.VMEM((MX, 8, NZ // 2), jnp.int32),
            pltpu.VMEM((MX, 8, NZ // 2), jnp.int32),
            pltpu.VMEM((NX, 8, NZ), f32),
            pltpu.VMEM((NX, 8, NZ), f32),
            pltpu.SemaphoreType.DMA((4,)),
        ],
        outside=True,
        limit=55180 << 10,
    )
    cores = [(i, i ^ 1) for i in range(ny)]
    inner = lax.ppermute(inner, "gy", cores)
    outer = lax.ppermute(outer, "gy", [(i, (i + (1 if i % 2 else -1)) % ny) for i in range(ny)])
    tx, ty = NX - 2, NY - 2
    k, lookup, gx, hx, ix, px = call(
        x_matrix_kernel,
        (ids, zone_diffusivity_lookup),
        [(MX * MY, NZ), (8, NZ)] + [(tx * MY, NZ)] * 3 + [(40, NZ)],
        scratch=[pltpu.VMEM((MX * MY, NZ), f32)],
        smem=(1,),
        cost=2000000,
    )
    send, rbx, beside = call(
        right_side_kernel,
        (heat, k, lookup, outer, inner, gx, hx, px),
        [(XROWS, NZ), (tx * NY, NZ), (2 * MX, NZ)],
    )
    near = [send] + [lax.ppermute(send, "gx", [(i, i ^ d) for i in range(nx)]) for d in (1, 2, 3)]
    gy, hy, iy, my, mid, za, zc, zi, zo = call(
        yz_matrix_kernel,
        (k, beside),
        [(ty * MX, NZ)] * 3
        + [(2 * MX, NZ), (MX, NZ)]
        + [(7 * MX * MY, NZ), (6 * MX * MY, NZ), (MX * MY, NZ), (3 * MX * MY, NZ)],
        cost=4000000,
    )
    (half,) = call(x_half_kernel, near, [(48, NZ)])
    half = lax.ppermute(half, "gx", [(i, nx - 1 - i) for i in range(nx)])
    own, rby = call(
        x_solve_kernel,
        (*near, half, heat, rbx, gx, hx, ix, gy, hy, my),
        [(YROWS, NZ), (ty * NX, NZ)],
        scratch=[pltpu.VMEM((NX * NY, NZ), f32)],
    )
    other = lax.ppermute(own, "gy", cores)
    (chip,) = call(chip_kernel, (own, other, mid), [(YROWS, NZ)])
    small = [chip] + [lax.ppermute(chip, "gy", [(i, i ^ (2 * d)) for i in range(ny)]) for d in (1, 2, 3)]
    (four,) = call(y_four_kernel, small, [(YROWS, NZ)])
    large = [four] + [lax.ppermute(four, "gy", [(i, i ^ (8 * d)) for i in range(ny)]) for d in (1, 2, 3)]
    (out,) = call(
        y_solve_kernel,
        (*large, *small, own, other, mid, rby, gy, hy, iy, za, zc, zi, zo, heat),
        [(NX * NY, NZ)],
        scratch=[pltpu.VMEM((NX * NY, NZ), f32)],
    )
    return out.reshape(starting_heat_state.shape)


def solution(mesh):
    return jax.shard_map(
        on_device,
        mesh=mesh,
        in_specs=(P("gx", "gy", None), P("gx", "gy", None), P()),
        out_specs=P("gx", "gy", None),
        check_vma=False,
    )
```

```python
import jax
import jax.numpy as jnp
from jax import lax
from jax.experimental import pallas as pl
from jax.experimental.pallas import tpu as pltpu
from jax.sharding import PartitionSpec as P

NX, NY, NZ = 16, 32, 128
MX, MY = NX // 2, NY // 2
XROWS = 104
YROWS = 48
f32 = jnp.float32


def lanes(shape):
    return lax.broadcasted_iota(jnp.int32, shape, 1)


def rows_of(shape):
    return lax.broadcasted_iota(jnp.int32, shape, 0)


def pack(first, second):
    return jnp.where(lanes(first.shape) % 2 == 0, first, second)


def unpack(both):
    even = lanes(both.shape) % 2 == 0
    first = jnp.where(even, both, pltpu.roll(both, 1, 1))
    second = jnp.where(even, pltpu.roll(both, NZ - 1, 1), both)
    return first, second


def through(near, far, link, beyond, leak, near_src, far_src, src):
    total = far + leak
    q = total + link
    cross = total * link
    f = beyond / ((near + beyond) * q + cross)
    new_leak = f * (near * q + cross)
    new_src = [f * (n * q + (e + s) * link) for n, e, s in zip(near_src, far_src, src)]
    return new_leak, new_src


def two_nodes(first, last, link, first_src, last_src):
    inv = 1.0 / (first * last + link * (first + last))
    low = [((last + link) * a + link * b) * inv for a, b in zip(first_src, last_src)]
    high = [((first + link) * b + link * a) * inv for a, b in zip(first_src, last_src)]
    return low, high


def eliminate(conduct, put):
    alpha = jnp.ones_like(conduct[0])
    beta = jnp.ones_like(conduct[0])
    link = conduct[0]
    for t in range(1, len(conduct)):
        g = conduct[t]
        inv = 1.0 / (link + beta + g)
        hd = link * inv
        gd = g * inv
        put(t - 1, gd, hd, inv)
        alpha = alpha + beta * hd
        link = link * gd
        beta = 1.0 + beta * gd
    return alpha, beta, link


def prepare_kernel(
    ids_hbm, heat_hbm, inner_ref, outer_ref, ids_low, ids_high, heat_low, heat_high, sems
):
    copies = [
        pltpu.make_async_copy(source, place, sems.at[i])
        for i, (source, place) in enumerate(
            (
                (heat_hbm.at[:, 0:8, :], heat_low),
                (heat_hbm.at[:, NY - 8 : NY, :], heat_high),
                (ids_hbm.at[:, 0:8, :], ids_low),
                (ids_hbm.at[:, MY - 8 : MY, :], ids_high),
            )
        )
    ]
    for copy in copies:
        copy.start()
    core = lax.rem(lax.axis_index("gy"), 2)
    inner_ref[NX:, :] = jnp.zeros((MX, NZ), f32)
    outer_ref[NX:, :] = jnp.zeros((MX, NZ), f32)
    for copy in copies:
        copy.wait()
    low, high = heat_low[:, 0, :], heat_high[:, 7, :]
    inner_ref[:NX, :] = jnp.where(core == 0, high, low)
    outer_ref[:NX, :] = jnp.where(core == 0, low, high)
    low, high = ids_low[:, 0, :], ids_high[:, 7, :]
    inner_ref[NX:, : NZ // 2] = jnp.where(core == 0, high, low).astype(f32)
    outer_ref[NX:, : NZ // 2] = jnp.where(core == 0, low, high).astype(f32)


def take(values, index):
    return jnp.take_along_axis(values, index, axis=1, mode="promise_in_bounds")


def chain(k):
    joints = []
    for m in range(len(k)):
        joints.append(2000.0 * k[m])
        if m + 1 < len(k):
            joints.append(1000.0 * (k[m] + k[m + 1]))
    return joints


def x_matrix_kernel(
    ids_ref, table_ref, k_ref, lookup_ref, gx_ref, hx_ref, ix_ref, px_ref, wide
):
    ids = ids_ref[...]
    k = jnp.zeros(ids.shape, f32)
    lookup = jnp.zeros(lookup_ref.shape, f32)
    for region in range(table_ref.shape[0]):
        k = jnp.where(ids == region, table_ref[region], k)
        lookup = jnp.where(lanes(lookup.shape) == region, table_ref[region], lookup)
    lookup_ref[...] = lookup
    wide[...] = jnp.zeros(wide.shape, f32)
    wide[:, : NZ // 2] = k
    k_ref[...] = take(wide[...], lanes(wide.shape) // 2)
    at_x = lax.axis_index("gx")
    last_x = lax.axis_size("gx") - 1
    kx = [k_ref[m * MY : (m + 1) * MY, :] for m in range(MX)]

    def put_x(t, gd, hd, inv):
        gx_ref[t * MY : (t + 1) * MY, :] = gd
        hx_ref[t * MY : (t + 1) * MY, :] = hd
        ix_ref[t * MY : (t + 1) * MY, :] = inv

    alpha, beta, link = eliminate(chain(kx), put_x)
    alpha = alpha + jnp.where(at_x == 0, 1000.0, 0.0) * kx[0]
    beta = beta + jnp.where(at_x == last_x, 1000.0, 0.0) * kx[-1]
    px_ref[0:16, :] = pack(alpha, beta)
    px_ref[16:32, :] = pack(link, kx[0])
    px_ref[32:40, :] = pack(kx[-1][:8], kx[-1][8:])


def y_matrix_kernel(k_ref, beside_ref, gy_ref, hy_ref, iy_ref, my_ref, mid_ref):
    at_y = lax.axis_index("gy")
    last_y = lax.axis_size("gy") - 1
    core = lax.rem(at_y, 2)
    ky = [k_ref[pl.ds(n, MX, stride=MY), :] for n in range(MY)]
    mid_ref[...] = 1000.0 * (beside_ref[:MX, :] + jnp.where(core == 0, ky[-1], ky[0]))
    outer = 1000.0 * (beside_ref[MX:, :] + jnp.where(core == 0, ky[0], ky[-1]))

    def put_y(t, gd, hd, inv):
        gy_ref[t * MX : (t + 1) * MX, :] = gd
        hy_ref[t * MX : (t + 1) * MX, :] = hd
        iy_ref[t * MX : (t + 1) * MX, :] = inv

    alpha, beta, link = eliminate(chain(ky), put_y)
    alpha = alpha + jnp.where(at_y == 0, 1000.0, 0.0) * ky[0]
    beta = beta + jnp.where(at_y == last_y, 1000.0, 0.0) * ky[-1]
    my_ref[0:8, :] = pack(alpha, beta)
    my_ref[8:16, :] = pack(link, outer)


def z_matrix_kernel(k_ref, za_ref, zc_ref, zi_ref, zo_ref):
    ky = [k_ref[pl.ds(n, MX, stride=MY), :] for n in range(MY)]
    group = 16
    for start in range(0, MY, group):
        k = jnp.concatenate(ky[start : start + group], 0)
        lane = lanes(k.shape)
        west = 0.25 * (k + jnp.where(lane == 0, 0.0, pltpu.roll(k, 1, 1)))
        east = 0.25 * (k + jnp.where(lane == NZ - 1, 0.0, pltpu.roll(k, NZ - 1, 1)))
        diag = 1.0 + (west + east)
        a = jnp.where(lane == 0, 0.0, west)
        c = jnp.where(lane == NZ - 1, 0.0, east)
        size = MX * group

        def double(coefficient):
            return jnp.where(lane % 2 == 0, coefficient, pltpu.roll(coefficient, 1, 1))

        for s in range(7):
            step = 1 << s
            inv = 1.0 / diag
            if s == 0:
                for i, odd in enumerate((inv, a * inv, c * inv)):
                    at = i * MX * MY + start * MX
                    zo_ref[at : at + size, :] = odd
            low = a * pltpu.roll(inv, step, 1)
            high = c * pltpu.roll(inv, NZ - step, 1)
            at = s * MX * MY + start * MX
            if 2 * step == NZ:
                za_ref[at : at + size, :] = double(low + high)
            else:
                za_ref[at : at + size, :] = double(low)
                zc_ref[at : at + size, :] = double(high)
            diag = diag - (low * pltpu.roll(c, step, 1) + high * pltpu.roll(a, NZ - step, 1))
            a = low * pltpu.roll(a, step, 1)
            c = high * pltpu.roll(c, NZ - step, 1)
        zi_ref[start * MX : start * MX + size, :] = double(1.0 / diag)


def right_side_kernel(
    heat_ref, k_ref, lookup_ref, outer_ref, inner_ref, gx_ref, hx_ref, px_ref, send_ref, rb_ref, beside_ref
):
    at_y = lax.axis_index("gy")
    core = lax.rem(at_y, 2)

    def conduct(ref):
        index = take(ref[NX:, :], lanes((MX, NZ)) // 2).astype(jnp.int32)
        return take(lookup_ref[...], index)

    inner = jnp.concatenate([inner_ref[:NX, :], conduct(inner_ref)], 0)
    outer = jnp.concatenate([outer_ref[:NX, :], conduct(outer_ref)], 0)
    beside_ref[:MX, :] = inner[NX:]
    beside_ref[MX:, :] = outer[NX:]
    low = jnp.where(at_y == 0, 0.0, jnp.where(core == 0, outer, inner))
    high = jnp.where(at_y == lax.axis_size("gy") - 1, 0.0, jnp.where(core == 0, inner, outer))
    shape = (MY, NZ)
    lane, row = lanes(shape), rows_of(shape)
    ra = None
    rb = None
    for m in range(MX):
        k = k_ref[m * MY : (m + 1) * MY, :]
        k_low = low[NX + m : NX + m + 1]
        k_high = high[NX + m : NX + m + 1]
        face_low = 2000.0 * (k + jnp.where(row == 0, k_low, pltpu.roll(k, 1, 0)))
        face_high = 2000.0 * (k + jnp.where(row == MY - 1, k_high, pltpu.roll(k, MY - 1, 0)))
        face_mid = 4000.0 * k
        west = 0.5 * (k + jnp.where(lane == 0, 0.0, pltpu.roll(k, 1, 1)))
        east = 0.5 * (k + jnp.where(lane == NZ - 1, 0.0, pltpu.roll(k, NZ - 1, 1)))
        middle = 2.0 - (west + east)
        west = jnp.where(lane == 0, 0.0, west)
        east = jnp.where(lane == NZ - 1, 0.0, east)
        for x in (2 * m, 2 * m + 1):
            even = heat_ref[pl.ds(x * NY, MY, stride=2), :]
            odd = heat_ref[pl.ds(x * NY + 1, MY, stride=2), :]
            before = jnp.where(row == 0, low[x : x + 1], pltpu.roll(odd, 1, 0))
            after = jnp.where(row == MY - 1, high[x : x + 1], pltpu.roll(even, MY - 1, 0))
            flow = face_mid * (odd - even)
            r = []
            for v, along_y in (
                (even, flow - face_low * (even - before)),
                (odd, face_high * (after - odd) - flow),
            ):
                along_z = west * pltpu.roll(v, 1, 1) + east * pltpu.roll(v, NZ - 1, 1)
                r.append(along_y + (along_z + middle * v))
            if x == 0:
                ra = r
            elif x == 1:
                rb = r
            else:
                t = x - 2
                gd = gx_ref[t * MY : (t + 1) * MY, :]
                hd = hx_ref[t * MY : (t + 1) * MY, :]
                for q in range(2):
                    rb_ref[t * NY + q * MY : t * NY + (q + 1) * MY, :] = rb[q]
                ra = [a + b * hd for a, b in zip(ra, rb)]
                rb = [n + b * gd for n, b in zip(r, rb)]
    send_ref[0:16, :] = ra[0]
    send_ref[16:32, :] = ra[1]
    send_ref[32:48, :] = rb[0]
    send_ref[48:64, :] = rb[1]
    send_ref[64:104, :] = px_ref[...]


def x_segment(rows):
    alpha, beta = unpack(rows[64:80])
    link, k_first = unpack(rows[80:96])
    k_last = jnp.concatenate(unpack(rows[96:104]), 0)
    return alpha, beta, link, k_first, k_last, [rows[0:16], rows[16:32]], [rows[32:48], rows[48:64]]


def quarter(place, refs, segment):
    held = [r[...] for r in refs]
    segments = []
    for d in range(4):
        rows = held[0]
        for j in range(1, 4):
            rows = jnp.where(place == d ^ j, held[j], rows)
        segments.append(segment(rows))
    return segments


def x_half_kernel(own_ref, one_ref, two_ref, three_ref, send_ref):
    at = lax.axis_index("gx")
    upper = at >= 4
    place = lax.rem(at, 4)
    place = jnp.where(upper, 3 - place, place)

    def turn(segment):
        alpha, beta, link, k_first, k_last, ra, rb = segment

        def pick(a, b):
            return jnp.where(upper, a, b)

        near, far = pick(alpha, beta), pick(beta, alpha)
        k_near, k_far = pick(k_first, k_last), pick(k_last, k_first)
        near_src = [pick(a, b) for a, b in zip(ra, rb)]
        far_src = [pick(b, a) for a, b in zip(ra, rb)]
        return near, far, link, k_near, k_far, near_src, far_src

    segments = [turn(g) for g in quarter(place, (own_ref, one_ref, two_ref, three_ref), x_segment)]
    zero = jnp.zeros((MY, NZ), f32)
    leak, src = zero, [zero, zero]
    for d in range(3):
        near, far, link, k_near, _, near_src, far_src = segments[d]
        joint = 1000.0 * (k_near + segments[d + 1][4])
        leak, src = through(near, far, link, joint, leak, near_src, far_src, src)
    near, far, link, k_near, _, near_src, far_src = segments[3]
    total = far + leak
    part = link / (total + link)
    send_ref[0:16, :] = near_src[0] + (far_src[0] + src[0]) * part
    send_ref[16:32, :] = near_src[1] + (far_src[1] + src[1]) * part
    send_ref[32:48, :] = pack(near + total * part, k_near)


def x_solve_kernel(
    own_ref, one_ref, two_ref, three_ref, half_ref, heat_ref, rb_ref, gx_ref, hx_ref, ix_ref, gy_ref, hy_ref,
    my_ref, core_ref, rby_ref, first,
):
    at = lax.axis_index("gx")
    place = lax.rem(at, 4)
    segments = quarter(place, (own_ref, one_ref, two_ref, three_ref), x_segment)
    half_leak, half_k = unpack(half_ref[32:48, :])
    upper = at >= 4
    joint = 1000.0 * (half_k + jnp.where(upper, segments[0][3], segments[3][4]))
    part = joint / (half_leak + joint)
    half_leak = half_leak * part
    half_src = [half_ref[0:16, :] * part, half_ref[16:32, :] * part]
    left = jnp.where(upper, half_leak, 0.0)
    left_src = [jnp.where(upper, v, 0.0) for v in half_src]
    right = jnp.where(upper, 0.0, half_leak)
    right_src = [jnp.where(upper, 0.0, v) for v in half_src]
    joints = [1000.0 * (segments[d][4] + segments[d + 1][3]) for d in range(3)]
    for step in range(3):
        d = step
        alpha, beta, link, _, _, ra, rb = segments[d]
        new, new_src = through(beta, alpha, link, joints[d], left, rb, ra, left_src)
        left = jnp.where(d < place, new, left)
        left_src = [jnp.where(d < place, n, o) for n, o in zip(new_src, left_src)]
        d = 3 - step
        alpha, beta, link, _, _, ra, rb = segments[d]
        new, new_src = through(alpha, beta, link, joints[d - 1], right, ra, rb, right_src)
        right = jnp.where(d > place, new, right)
        right_src = [jnp.where(d > place, n, o) for n, o in zip(new_src, right_src)]
    alpha, beta, link, _, _, ra, rb = x_segment(own_ref[...])
    u_first, u_next = two_nodes(
        alpha + left,
        beta + right,
        link,
        [a + s for a, s in zip(ra, left_src)],
        [b + s for b, s in zip(rb, right_src)],
    )

    def keep(x, u):
        for q in range(2):
            heat = heat_ref[pl.ds(x * NY + q, MY, stride=2), :]
            first[x * NY + q * MY : x * NY + (q + 1) * MY, :] = u[q] - 2.0 * heat

    keep(0, u_first)
    keep(NX - 1, u_next)
    for x in range(NX - 2, 0, -1):
        t = x - 1
        gd = gx_ref[t * MY : (t + 1) * MY, :]
        hd = hx_ref[t * MY : (t + 1) * MY, :]
        inv = ix_ref[t * MY : (t + 1) * MY, :]
        b = [rb_ref[t * NY + q * MY : t * NY + (q + 1) * MY, :] for q in range(2)]
        u_next = [(inv * b[q] + hd * u_first[q]) + gd * u_next[q] for q in range(2)]
        keep(x, u_next)

    def side(y):
        start = (y % 2) * MY + y // 2
        return [first[pl.ds(p * NY + start, MX, stride=2 * NY), :] for p in range(2)]

    ra = side(0)
    rb = side(1)
    for t in range(NY - 2):
        gd = gy_ref[t * MX : (t + 1) * MX, :]
        hd = hy_ref[t * MX : (t + 1) * MX, :]
        for p in range(2):
            rby_ref[t * NX + p * MX : t * NX + (p + 1) * MX, :] = rb[p]
        new = side(t + 2)
        ra = [a + b * hd for a, b in zip(ra, rb)]
        rb = [n + b * gd for n, b in zip(new, rb)]
    core_ref[0:8, :] = ra[0]
    core_ref[8:16, :] = ra[1]
    core_ref[16:24, :] = rb[0]
    core_ref[24:32, :] = rb[1]
    core_ref[32:48, :] = my_ref[...]


def y_segment(rows):
    alpha, beta = unpack(rows[32:40])
    link, joint = unpack(rows[40:48])
    return alpha, beta, link, joint, [rows[0:8], rows[8:16]], [rows[16:24], rows[24:32]]


def merge(first, second, joint):
    a0, b0, h0, outer, ra0, rb0 = first
    a1, b1, h1, _, ra1, rb1 = second
    inv = 1.0 / (h0 + b0 + joint)
    hd, gd = h0 * inv, joint * inv
    alpha = a0 + b0 * hd
    link = h0 * gd
    between = a1 + b0 * gd
    ra = [a + b * hd for a, b in zip(ra0, rb0)]
    rm = [a + b * gd for a, b in zip(ra1, rb0)]
    inv = 1.0 / (link + between + h1)
    hd, gd = link * inv, h1 * inv
    alpha = alpha + between * hd
    beta = b1 + between * gd
    ra = [a + m * hd for a, m in zip(ra, rm)]
    rb = [b + m * gd for b, m in zip(rb1, rm)]
    return alpha, beta, link * gd, outer, ra, rb


def store_segment(ref, segment):
    alpha, beta, link, joint, ra, rb = segment
    ref[...] = jnp.concatenate([*ra, *rb, pack(alpha, beta), pack(link, joint)], 0)


def chip_kernel(own_ref, other_ref, mid_ref, send_ref):
    core = lax.rem(lax.axis_index("gy"), 2)
    own, other = own_ref[...], other_ref[...]
    first = y_segment(jnp.where(core == 0, own, other))
    second = y_segment(jnp.where(core == 0, other, own))
    store_segment(send_ref, merge(first, second, mid_ref[...]))


def y_four_kernel(own_ref, one_ref, two_ref, three_ref, send_ref):
    place = lax.rem(lax.div(lax.axis_index("gy"), 2), 4)
    a, b, c, d = quarter(place, (own_ref, one_ref, two_ref, three_ref), y_segment)
    store_segment(send_ref, merge(merge(a, b, b[3]), merge(c, d, d[3]), c[3]))


def y_sweeps(segments, place, left, left_src, right, right_src):
    for step in range(3):
        d = step
        alpha, beta, link, _, ra, rb = segments[d]
        new, new_src = through(beta, alpha, link, segments[d + 1][3], left, rb, ra, left_src)
        left = jnp.where(d < place, new, left)
        left_src = [jnp.where(d < place, n, o) for n, o in zip(new_src, left_src)]
        d = 3 - step
        alpha, beta, link, joint, ra, rb = segments[d]
        new, new_src = through(alpha, beta, link, joint, right, ra, rb, right_src)
        right = jnp.where(d > place, new, right)
        right_src = [jnp.where(d > place, n, o) for n, o in zip(new_src, right_src)]
    return left, left_src, right, right_src


def y_solve_kernel(
    large0, large1, large2, large3, small0, small1, small2, small3, own_ref, other_ref, mid_ref, rb_ref, gy_ref,
    hy_ref, iy_ref, za_ref, zc_ref, zi_ref, zo_ref, heat_ref, out_ref, second,
):
    at_y = lax.axis_index("gy")
    core, chip = lax.rem(at_y, 2), lax.div(at_y, 2)
    zero = jnp.zeros((MX, NZ), f32)
    large = quarter(lax.div(chip, 4), (large0, large1, large2, large3), y_segment)
    small = quarter(lax.rem(chip, 4), (small0, small1, small2, small3), y_segment)
    state = y_sweeps(large, lax.div(chip, 4), zero, [zero, zero], zero, [zero, zero])
    left, left_src, right, right_src = y_sweeps(small, lax.rem(chip, 4), *state)

    def choose(a, b):
        return jnp.where(core == 0, a, b)

    alpha, beta, link, _, ra, rb = y_segment(other_ref[...])
    near, far = choose(alpha, beta), choose(beta, alpha)
    near_src = [choose(a, b) for a, b in zip(ra, rb)]
    far_src = [choose(b, a) for a, b in zip(ra, rb)]
    leak = choose(right, left)
    src = [choose(r, l) for r, l in zip(right_src, left_src)]
    new, new_src = through(near, far, link, mid_ref[...], leak, near_src, far_src, src)
    left, right = choose(left, new), choose(new, right)
    left_src, right_src = (
        [choose(l, n) for l, n in zip(left_src, new_src)],
        [choose(n, r) for n, r in zip(new_src, right_src)],
    )
    alpha, beta, link, _, ra, rb = y_segment(own_ref[...])
    u_first, u_next = two_nodes(
        alpha + left,
        beta + right,
        link,
        [a + s for a, s in zip(ra, left_src)],
        [b + s for b, s in zip(rb, right_src)],
    )

    def keep(y, u):
        for p in range(2):
            second[y * NX + p * MX : y * NX + (p + 1) * MX, :] = u[p]

    keep(0, u_first)
    keep(NY - 1, u_next)
    for y in range(NY - 2, 0, -1):
        t = y - 1
        gd = gy_ref[t * MX : (t + 1) * MX, :]
        hd = hy_ref[t * MX : (t + 1) * MX, :]
        inv = iy_ref[t * MX : (t + 1) * MX, :]
        b = [rb_ref[t * NX + p * MX : t * NX + (p + 1) * MX, :] for p in range(2)]
        u_next = [(inv * b[p] + hd * u_first[p]) + gd * u_next[p] for p in range(2)]
        keep(y, u_next)

    even = lanes((MX, NZ)) % 2 == 0

    def turned(v, step):
        return pltpu.roll(v, step % NZ, 1)

    for n in range(MY):
        rows = slice(n * MX, (n + 1) * MX)
        inv, odd, odd_low, odd_high = zi_ref[rows, :], *(
            zo_ref[i * MX * MY + n * MX : i * MX * MY + (n + 1) * MX, :] for i in range(3)
        )
        for p in range(2):
            a, b = (second[y * NX + p * MX : y * NX + (p + 1) * MX, :] for y in (2 * n, 2 * n + 1))
            w = jnp.where(even, a, turned(b, 1))
            before = jnp.where(even, turned(a, 1), turned(b, 2))
            after = jnp.where(even, turned(a, -1), b)
            for s in range(7):
                step = 1 << s
                at = slice(s * MX * MY + n * MX, s * MX * MY + (n + 1) * MX)
                if s > 0:
                    before = turned(w, step)
                if 2 * step == NZ:
                    w = w + za_ref[at, :] * before
                else:
                    if s > 0:
                        after = turned(w, -step)
                    w = w + (za_ref[at, :] * before + zc_ref[at, :] * after)
            w = inv * w
            next_w = turned(w, -1)
            a = jnp.where(even, w, odd * a + (odd_low * turned(w, 1) + odd_high * next_w))
            b = jnp.where(even, next_w, odd * b + (odd_low * w + odd_high * turned(w, -2)))
            for y, v in ((2 * n, a), (2 * n + 1, b)):
                where = pl.ds(p * NY + y, MX, stride=2 * NY)
                out_ref[where, :] = heat_ref[where, :] + v


def call(kernel, ins, outs, scratch=(), outside=False, smem=(), cost=20000, limit=8 << 20):
    space = pltpu.HBM if outside else pltpu.VMEM
    return pl.pallas_call(
        kernel,
        out_shape=tuple(jax.ShapeDtypeStruct(s, f32) for s in outs),
        in_specs=[pl.BlockSpec(memory_space=pltpu.SMEM if i in smem else space) for i in range(len(ins))],
        out_specs=tuple(pl.BlockSpec(memory_space=pltpu.VMEM) for _ in outs),
        scratch_shapes=scratch,
        compiler_params=pltpu.CompilerParams(vmem_limit_bytes=limit),
        cost_estimate=pl.CostEstimate(flops=cost, bytes_accessed=cost, transcendentals=0),
    )(*ins)


def on_device(starting_heat_state, material_zone_ids, zone_diffusivity_lookup):
    heat = starting_heat_state.reshape(NX * NY, NZ)
    ids = material_zone_ids.reshape(MX * MY, NZ // 2)
    nx, ny = lax.axis_size("gx"), lax.axis_size("gy")
    inner, outer = call(
        prepare_kernel,
        (material_zone_ids, starting_heat_state),
        [(NX + MX, NZ)] * 2,
        scratch=[
            pltpu.VMEM((MX, 8, NZ // 2), jnp.int32),
            pltpu.VMEM((MX, 8, NZ // 2), jnp.int32),
            pltpu.VMEM((NX, 8, NZ), f32),
            pltpu.VMEM((NX, 8, NZ), f32),
            pltpu.SemaphoreType.DMA((4,)),
        ],
        outside=True,
        limit=55180 << 10,
    )
    cores = [(i, i ^ 1) for i in range(ny)]
    inner = lax.ppermute(inner, "gy", cores)
    outer = lax.ppermute(outer, "gy", [(i, (i + (1 if i % 2 else -1)) % ny) for i in range(ny)])
    tx, ty = NX - 2, NY - 2
    k, lookup, gx, hx, ix, px = call(
        x_matrix_kernel,
        (ids, zone_diffusivity_lookup),
        [(MX * MY, NZ), (8, NZ)] + [(tx * MY, NZ)] * 3 + [(40, NZ)],
        scratch=[pltpu.VMEM((MX * MY, NZ), f32)],
        smem=(1,),
        cost=2000000,
    )
    send, rbx, beside = call(
        right_side_kernel,
        (heat, k, lookup, outer, inner, gx, hx, px),
        [(XROWS, NZ), (tx * NY, NZ), (2 * MX, NZ)],
    )
    near = [send] + [lax.ppermute(send, "gx", [(i, i ^ d) for i in range(nx)]) for d in (1, 2, 3)]
    gy, hy, iy, my, mid = call(
        y_matrix_kernel,
        (k, beside),
        [(ty * MX, NZ)] * 3 + [(2 * MX, NZ), (MX, NZ)],
        cost=2000000,
    )
    (half,) = call(x_half_kernel, near, [(48, NZ)])
    half = lax.ppermute(half, "gx", [(i, nx - 1 - i) for i in range(nx)])
    own, rby = call(
        x_solve_kernel,
        (*near, half, heat, rbx, gx, hx, ix, gy, hy, my),
        [(YROWS, NZ), (ty * NX, NZ)],
        scratch=[pltpu.VMEM((NX * NY, NZ), f32)],
    )
    other = lax.ppermute(own, "gy", cores)
    (chip,) = call(chip_kernel, (own, other, mid), [(YROWS, NZ)])
    chip, k = lax.optimization_barrier((chip, k))
    za, zc, zi, zo = call(
        z_matrix_kernel,
        (k,),
        [(7 * MX * MY, NZ), (6 * MX * MY, NZ), (MX * MY, NZ), (3 * MX * MY, NZ)],
        cost=4000000,
    )
    small = [chip] + [lax.ppermute(chip, "gy", [(i, i ^ (2 * d)) for i in range(ny)]) for d in (1, 2, 3)]
    (four,) = call(y_four_kernel, small, [(YROWS, NZ)])
    large = [four] + [lax.ppermute(four, "gy", [(i, i ^ (8 * d)) for i in range(ny)]) for d in (1, 2, 3)]
    (out,) = call(
        y_solve_kernel,
        (*large, *small, own, other, mid, rby, gy, hy, iy, za, zc, zi, zo, heat),
        [(NX * NY, NZ)],
        scratch=[pltpu.VMEM((NX * NY, NZ), f32)],
    )
    return out.reshape(starting_heat_state.shape)


def solution(mesh):
    return jax.shard_map(
        on_device,
        mesh=mesh,
        in_specs=(P("gx", "gy", None), P("gx", "gy", None), P()),
        out_specs=P("gx", "gy", None),
        check_vma=False,
    )
```

```python
import jax
import jax.numpy as jnp
from jax import lax
from jax.experimental import pallas as pl
from jax.experimental.pallas import tpu as pltpu
from jax.sharding import PartitionSpec as P

NX, NY, NZ = 16, 32, 128
MX, MY = NX // 2, NY // 2
XROWS = 104
YROWS = 48
f32 = jnp.float32


def lanes(shape):
    return lax.broadcasted_iota(jnp.int32, shape, 1)


def rows_of(shape):
    return lax.broadcasted_iota(jnp.int32, shape, 0)


def pack(first, second):
    return jnp.where(lanes(first.shape) % 2 == 0, first, second)


def unpack(both):
    even = lanes(both.shape) % 2 == 0
    first = jnp.where(even, both, pltpu.roll(both, 1, 1))
    second = jnp.where(even, pltpu.roll(both, NZ - 1, 1), both)
    return first, second


def through(near, far, link, beyond, leak, near_src, far_src, src):
    total = far + leak
    q = total + link
    cross = total * link
    f = beyond / ((near + beyond) * q + cross)
    new_leak = f * (near * q + cross)
    new_src = [f * (n * q + (e + s) * link) for n, e, s in zip(near_src, far_src, src)]
    return new_leak, new_src


def two_nodes(first, last, link, first_src, last_src):
    inv = 1.0 / (first * last + link * (first + last))
    low = [((last + link) * a + link * b) * inv for a, b in zip(first_src, last_src)]
    high = [((first + link) * b + link * a) * inv for a, b in zip(first_src, last_src)]
    return low, high


def eliminate(conduct, put):
    alpha = jnp.ones_like(conduct[0])
    beta = jnp.ones_like(conduct[0])
    link = conduct[0]
    for t in range(1, len(conduct)):
        g = conduct[t]
        inv = 1.0 / (link + beta + g)
        hd = link * inv
        gd = g * inv
        put(t - 1, gd, hd, inv)
        alpha = alpha + beta * hd
        link = link * gd
        beta = 1.0 + beta * gd
    return alpha, beta, link


def prepare_kernel(
    ids_hbm, heat_hbm, inner_ref, outer_ref, ids_low, ids_high, heat_low, heat_high, sems
):
    copies = [
        pltpu.make_async_copy(source, place, sems.at[i])
        for i, (source, place) in enumerate(
            (
                (heat_hbm.at[:, 0:1, :], heat_low),
                (heat_hbm.at[:, NY - 1 : NY, :], heat_high),
                (ids_hbm.at[:, 0:1, :], ids_low),
                (ids_hbm.at[:, MY - 1 : MY, :], ids_high),
            )
        )
    ]
    for copy in copies:
        copy.start()
    core = lax.rem(lax.axis_index("gy"), 2)
    inner_ref[NX:, :] = jnp.zeros((MX, NZ), f32)
    outer_ref[NX:, :] = jnp.zeros((MX, NZ), f32)
    for copy in copies:
        copy.wait()
    low, high = heat_low[:, 0, :], heat_high[:, 0, :]
    inner_ref[:NX, :] = jnp.where(core == 0, high, low)
    outer_ref[:NX, :] = jnp.where(core == 0, low, high)
    low, high = ids_low[:, 0, :], ids_high[:, 0, :]
    inner_ref[NX:, : NZ // 2] = jnp.where(core == 0, high, low).astype(f32)
    outer_ref[NX:, : NZ // 2] = jnp.where(core == 0, low, high).astype(f32)


def take(values, index):
    return jnp.take_along_axis(values, index, axis=1, mode="promise_in_bounds")


def chain(k):
    joints = []
    for m in range(len(k)):
        joints.append(2000.0 * k[m])
        if m + 1 < len(k):
            joints.append(1000.0 * (k[m] + k[m + 1]))
    return joints


def x_matrix_kernel(
    ids_ref, table_ref, k_ref, lookup_ref, gx_ref, hx_ref, ix_ref, px_ref, wide
):
    ids = ids_ref[...]
    k = jnp.zeros(ids.shape, f32)
    lookup = jnp.zeros(lookup_ref.shape, f32)
    for region in range(table_ref.shape[0]):
        k = jnp.where(ids == region, table_ref[region], k)
        lookup = jnp.where(lanes(lookup.shape) == region, table_ref[region], lookup)
    lookup_ref[...] = lookup
    wide[...] = jnp.zeros(wide.shape, f32)
    wide[:, : NZ // 2] = k
    k_ref[...] = take(wide[...], lanes(wide.shape) // 2)
    at_x = lax.axis_index("gx")
    last_x = lax.axis_size("gx") - 1
    kx = [k_ref[m * MY : (m + 1) * MY, :] for m in range(MX)]

    def put_x(t, gd, hd, inv):
        gx_ref[t * MY : (t + 1) * MY, :] = gd
        hx_ref[t * MY : (t + 1) * MY, :] = hd
        ix_ref[t * MY : (t + 1) * MY, :] = inv

    alpha, beta, link = eliminate(chain(kx), put_x)
    alpha = alpha + jnp.where(at_x == 0, 1000.0, 0.0) * kx[0]
    beta = beta + jnp.where(at_x == last_x, 1000.0, 0.0) * kx[-1]
    px_ref[0:16, :] = pack(alpha, beta)
    px_ref[16:32, :] = pack(link, kx[0])
    px_ref[32:40, :] = pack(kx[-1][:8], kx[-1][8:])


def y_matrix_kernel(k_ref, beside_ref, gy_ref, hy_ref, iy_ref, my_ref, mid_ref):
    at_y = lax.axis_index("gy")
    last_y = lax.axis_size("gy") - 1
    core = lax.rem(at_y, 2)
    ky = [k_ref[pl.ds(n, MX, stride=MY), :] for n in range(MY)]
    mid_ref[...] = 1000.0 * (beside_ref[:MX, :] + jnp.where(core == 0, ky[-1], ky[0]))
    outer = 1000.0 * (beside_ref[MX:, :] + jnp.where(core == 0, ky[0], ky[-1]))

    def put_y(t, gd, hd, inv):
        gy_ref[t * MX : (t + 1) * MX, :] = gd
        hy_ref[t * MX : (t + 1) * MX, :] = hd
        iy_ref[t * MX : (t + 1) * MX, :] = inv

    alpha, beta, link = eliminate(chain(ky), put_y)
    alpha = alpha + jnp.where(at_y == 0, 1000.0, 0.0) * ky[0]
    beta = beta + jnp.where(at_y == last_y, 1000.0, 0.0) * ky[-1]
    my_ref[0:8, :] = pack(alpha, beta)
    my_ref[8:16, :] = pack(link, outer)


def z_matrix_kernel(k_ref, heat_ref, za_ref, zc_ref, zi_ref, zo_ref, turned_ref):
    for y in range(NY):
        for p in range(2):
            turned_ref[y * NX + p * MX : y * NX + (p + 1) * MX, :] = heat_ref[
                pl.ds(p * NY + y, MX, stride=2 * NY), :
            ]
    ky = [k_ref[pl.ds(n, MX, stride=MY), :] for n in range(MY)]
    group = 16
    for start in range(0, MY, group):
        k = jnp.concatenate(ky[start : start + group], 0)
        lane = lanes(k.shape)
        west = 0.25 * (k + jnp.where(lane == 0, 0.0, pltpu.roll(k, 1, 1)))
        east = 0.25 * (k + jnp.where(lane == NZ - 1, 0.0, pltpu.roll(k, NZ - 1, 1)))
        diag = 1.0 + (west + east)
        a = jnp.where(lane == 0, 0.0, west)
        c = jnp.where(lane == NZ - 1, 0.0, east)
        size = MX * group

        def double(coefficient):
            return jnp.where(lane % 2 == 0, coefficient, pltpu.roll(coefficient, 1, 1))

        for s in range(7):
            step = 1 << s
            inv = 1.0 / diag
            if s == 0:
                for i, odd in enumerate((inv, a * inv, c * inv)):
                    at = i * MX * MY + start * MX
                    zo_ref[at : at + size, :] = odd
            low = a * pltpu.roll(inv, step, 1)
            high = c * pltpu.roll(inv, NZ - step, 1)
            at = s * MX * MY + start * MX
            if 2 * step == NZ:
                za_ref[at : at + size, :] = double(low + high)
            else:
                za_ref[at : at + size, :] = double(low)
                zc_ref[at : at + size, :] = double(high)
            diag = diag - (low * pltpu.roll(c, step, 1) + high * pltpu.roll(a, NZ - step, 1))
            a = low * pltpu.roll(a, step, 1)
            c = high * pltpu.roll(c, NZ - step, 1)
        zi_ref[start * MX : start * MX + size, :] = double(1.0 / diag)


def right_side_kernel(
    heat_ref, k_ref, lookup_ref, outer_ref, inner_ref, gx_ref, hx_ref, px_ref, send_ref, rb_ref, beside_ref
):
    at_y = lax.axis_index("gy")
    core = lax.rem(at_y, 2)

    def conduct(ref):
        index = take(ref[NX:, :], lanes((MX, NZ)) // 2).astype(jnp.int32)
        return take(lookup_ref[...], index)

    inner = jnp.concatenate([inner_ref[:NX, :], conduct(inner_ref)], 0)
    outer = jnp.concatenate([outer_ref[:NX, :], conduct(outer_ref)], 0)
    beside_ref[:MX, :] = inner[NX:]
    beside_ref[MX:, :] = outer[NX:]
    low = jnp.where(at_y == 0, 0.0, jnp.where(core == 0, outer, inner))
    high = jnp.where(at_y == lax.axis_size("gy") - 1, 0.0, jnp.where(core == 0, inner, outer))
    shape = (MY, NZ)
    lane, row = lanes(shape), rows_of(shape)
    ra = None
    rb = None
    for m in range(MX):
        k = k_ref[m * MY : (m + 1) * MY, :]
        k_low = low[NX + m : NX + m + 1]
        k_high = high[NX + m : NX + m + 1]
        face_low = 2000.0 * (k + jnp.where(row == 0, k_low, pltpu.roll(k, 1, 0)))
        face_high = 2000.0 * (k + jnp.where(row == MY - 1, k_high, pltpu.roll(k, MY - 1, 0)))
        face_mid = 4000.0 * k
        west = 0.5 * (k + jnp.where(lane == 0, 0.0, pltpu.roll(k, 1, 1)))
        east = 0.5 * (k + jnp.where(lane == NZ - 1, 0.0, pltpu.roll(k, NZ - 1, 1)))
        middle = 2.0 - (west + east)
        west = jnp.where(lane == 0, 0.0, west)
        east = jnp.where(lane == NZ - 1, 0.0, east)
        for x in (2 * m, 2 * m + 1):
            even = heat_ref[pl.ds(x * NY, MY, stride=2), :]
            odd = heat_ref[pl.ds(x * NY + 1, MY, stride=2), :]
            before = jnp.where(row == 0, low[x : x + 1], pltpu.roll(odd, 1, 0))
            after = jnp.where(row == MY - 1, high[x : x + 1], pltpu.roll(even, MY - 1, 0))
            flow = face_mid * (odd - even)
            r = []
            for v, along_y in (
                (even, flow - face_low * (even - before)),
                (odd, face_high * (after - odd) - flow),
            ):
                along_z = west * pltpu.roll(v, 1, 1) + east * pltpu.roll(v, NZ - 1, 1)
                r.append(along_y + (along_z + middle * v))
            if x == 0:
                ra = r
            elif x == 1:
                rb = r
            else:
                t = x - 2
                gd = gx_ref[t * MY : (t + 1) * MY, :]
                hd = hx_ref[t * MY : (t + 1) * MY, :]
                for q in range(2):
                    rb_ref[t * NY + q * MY : t * NY + (q + 1) * MY, :] = rb[q]
                ra = [a + b * hd for a, b in zip(ra, rb)]
                rb = [n + b * gd for n, b in zip(r, rb)]
    send_ref[0:16, :] = ra[0]
    send_ref[16:32, :] = ra[1]
    send_ref[32:48, :] = rb[0]
    send_ref[48:64, :] = rb[1]
    send_ref[64:104, :] = px_ref[...]


def x_segment(rows):
    alpha, beta = unpack(rows[64:80])
    link, k_first = unpack(rows[80:96])
    k_last = jnp.concatenate(unpack(rows[96:104]), 0)
    return alpha, beta, link, k_first, k_last, [rows[0:16], rows[16:32]], [rows[32:48], rows[48:64]]


def quarter(place, refs, segment):
    held = [r[...] for r in refs]
    segments = []
    for d in range(4):
        rows = held[0]
        for j in range(1, 4):
            rows = jnp.where(place == d ^ j, held[j], rows)
        segments.append(segment(rows))
    return segments


def x_half_kernel(own_ref, one_ref, two_ref, three_ref, send_ref):
    at = lax.axis_index("gx")
    upper = at >= 4
    place = lax.rem(at, 4)
    place = jnp.where(upper, 3 - place, place)

    def turn(segment):
        alpha, beta, link, k_first, k_last, ra, rb = segment

        def pick(a, b):
            return jnp.where(upper, a, b)

        near, far = pick(alpha, beta), pick(beta, alpha)
        k_near, k_far = pick(k_first, k_last), pick(k_last, k_first)
        near_src = [pick(a, b) for a, b in zip(ra, rb)]
        far_src = [pick(b, a) for a, b in zip(ra, rb)]
        return near, far, link, k_near, k_far, near_src, far_src

    segments = [turn(g) for g in quarter(place, (own_ref, one_ref, two_ref, three_ref), x_segment)]
    zero = jnp.zeros((MY, NZ), f32)
    leak, src = zero, [zero, zero]
    for d in range(3):
        near, far, link, k_near, _, near_src, far_src = segments[d]
        joint = 1000.0 * (k_near + segments[d + 1][4])
        leak, src = through(near, far, link, joint, leak, near_src, far_src, src)
    near, far, link, k_near, _, near_src, far_src = segments[3]
    total = far + leak
    part = link / (total + link)
    send_ref[0:16, :] = near_src[0] + (far_src[0] + src[0]) * part
    send_ref[16:32, :] = near_src[1] + (far_src[1] + src[1]) * part
    send_ref[32:48, :] = pack(near + total * part, k_near)


def x_solve_kernel(
    own_ref, one_ref, two_ref, three_ref, half_ref, heat_ref, rb_ref, gx_ref, hx_ref, ix_ref, gy_ref, hy_ref,
    my_ref, core_ref, rby_ref, first,
):
    at = lax.axis_index("gx")
    place = lax.rem(at, 4)
    segments = quarter(place, (own_ref, one_ref, two_ref, three_ref), x_segment)
    half_leak, half_k = unpack(half_ref[32:48, :])
    upper = at >= 4
    joint = 1000.0 * (half_k + jnp.where(upper, segments[0][3], segments[3][4]))
    part = joint / (half_leak + joint)
    half_leak = half_leak * part
    half_src = [half_ref[0:16, :] * part, half_ref[16:32, :] * part]
    left = jnp.where(upper, half_leak, 0.0)
    left_src = [jnp.where(upper, v, 0.0) for v in half_src]
    right = jnp.where(upper, 0.0, half_leak)
    right_src = [jnp.where(upper, 0.0, v) for v in half_src]
    joints = [1000.0 * (segments[d][4] + segments[d + 1][3]) for d in range(3)]
    for step in range(3):
        d = step
        alpha, beta, link, _, _, ra, rb = segments[d]
        new, new_src = through(beta, alpha, link, joints[d], left, rb, ra, left_src)
        left = jnp.where(d < place, new, left)
        left_src = [jnp.where(d < place, n, o) for n, o in zip(new_src, left_src)]
        d = 3 - step
        alpha, beta, link, _, _, ra, rb = segments[d]
        new, new_src = through(alpha, beta, link, joints[d - 1], right, ra, rb, right_src)
        right = jnp.where(d > place, new, right)
        right_src = [jnp.where(d > place, n, o) for n, o in zip(new_src, right_src)]
    alpha, beta, link, _, _, ra, rb = x_segment(own_ref[...])
    u_first, u_next = two_nodes(
        alpha + left,
        beta + right,
        link,
        [a + s for a, s in zip(ra, left_src)],
        [b + s for b, s in zip(rb, right_src)],
    )

    def keep(x, u):
        for q in range(2):
            heat = heat_ref[pl.ds(x * NY + q, MY, stride=2), :]
            first[x * NY + q * MY : x * NY + (q + 1) * MY, :] = u[q] - 2.0 * heat

    keep(0, u_first)
    keep(NX - 1, u_next)
    for x in range(NX - 2, 0, -1):
        t = x - 1
        gd = gx_ref[t * MY : (t + 1) * MY, :]
        hd = hx_ref[t * MY : (t + 1) * MY, :]
        inv = ix_ref[t * MY : (t + 1) * MY, :]
        b = [rb_ref[t * NY + q * MY : t * NY + (q + 1) * MY, :] for q in range(2)]
        u_next = [(inv * b[q] + hd * u_first[q]) + gd * u_next[q] for q in range(2)]
        keep(x, u_next)

    def side(y):
        start = (y % 2) * MY + y // 2
        return [first[pl.ds(p * NY + start, MX, stride=2 * NY), :] for p in range(2)]

    ra = side(0)
    rb = side(1)
    for t in range(NY - 2):
        gd = gy_ref[t * MX : (t + 1) * MX, :]
        hd = hy_ref[t * MX : (t + 1) * MX, :]
        for p in range(2):
            rby_ref[t * NX + p * MX : t * NX + (p + 1) * MX, :] = rb[p]
        new = side(t + 2)
        ra = [a + b * hd for a, b in zip(ra, rb)]
        rb = [n + b * gd for n, b in zip(new, rb)]
    core_ref[0:8, :] = ra[0]
    core_ref[8:16, :] = ra[1]
    core_ref[16:24, :] = rb[0]
    core_ref[24:32, :] = rb[1]
    core_ref[32:48, :] = my_ref[...]


def y_segment(rows):
    alpha, beta = unpack(rows[32:40])
    link, joint = unpack(rows[40:48])
    return alpha, beta, link, joint, [rows[0:8], rows[8:16]], [rows[16:24], rows[24:32]]


def merge(first, second, joint):
    a0, b0, h0, outer, ra0, rb0 = first
    a1, b1, h1, _, ra1, rb1 = second
    inv = 1.0 / (h0 + b0 + joint)
    hd, gd = h0 * inv, joint * inv
    alpha = a0 + b0 * hd
    link = h0 * gd
    between = a1 + b0 * gd
    ra = [a + b * hd for a, b in zip(ra0, rb0)]
    rm = [a + b * gd for a, b in zip(ra1, rb0)]
    inv = 1.0 / (link + between + h1)
    hd, gd = link * inv, h1 * inv
    alpha = alpha + between * hd
    beta = b1 + between * gd
    ra = [a + m * hd for a, m in zip(ra, rm)]
    rb = [b + m * gd for b, m in zip(rb1, rm)]
    return alpha, beta, link * gd, outer, ra, rb


def store_segment(ref, segment):
    alpha, beta, link, joint, ra, rb = segment
    ref[...] = jnp.concatenate([*ra, *rb, pack(alpha, beta), pack(link, joint)], 0)


def chip_kernel(own_ref, other_ref, mid_ref, send_ref):
    core = lax.rem(lax.axis_index("gy"), 2)
    own, other = own_ref[...], other_ref[...]
    first = y_segment(jnp.where(core == 0, own, other))
    second = y_segment(jnp.where(core == 0, other, own))
    store_segment(send_ref, merge(first, second, mid_ref[...]))


def y_four_kernel(own_ref, one_ref, two_ref, three_ref, send_ref):
    place = lax.rem(lax.div(lax.axis_index("gy"), 2), 4)
    a, b, c, d = quarter(place, (own_ref, one_ref, two_ref, three_ref), y_segment)
    store_segment(send_ref, merge(merge(a, b, b[3]), merge(c, d, d[3]), c[3]))


def y_sweeps(segments, place, left, left_src, right, right_src):
    for step in range(3):
        d = step
        alpha, beta, link, _, ra, rb = segments[d]
        new, new_src = through(beta, alpha, link, segments[d + 1][3], left, rb, ra, left_src)
        left = jnp.where(d < place, new, left)
        left_src = [jnp.where(d < place, n, o) for n, o in zip(new_src, left_src)]
        d = 3 - step
        alpha, beta, link, joint, ra, rb = segments[d]
        new, new_src = through(alpha, beta, link, joint, right, ra, rb, right_src)
        right = jnp.where(d > place, new, right)
        right_src = [jnp.where(d > place, n, o) for n, o in zip(new_src, right_src)]
    return left, left_src, right, right_src


def y_solve_kernel(
    large0, large1, large2, large3, small0, small1, small2, small3, own_ref, other_ref, mid_ref, rb_ref, gy_ref,
    hy_ref, iy_ref, za_ref, zc_ref, zi_ref, zo_ref, heat_ref, out_ref, second,
):
    at_y = lax.axis_index("gy")
    core, chip = lax.rem(at_y, 2), lax.div(at_y, 2)
    zero = jnp.zeros((MX, NZ), f32)
    large = quarter(lax.div(chip, 4), (large0, large1, large2, large3), y_segment)
    small = quarter(lax.rem(chip, 4), (small0, small1, small2, small3), y_segment)
    state = y_sweeps(large, lax.div(chip, 4), zero, [zero, zero], zero, [zero, zero])
    left, left_src, right, right_src = y_sweeps(small, lax.rem(chip, 4), *state)

    def choose(a, b):
        return jnp.where(core == 0, a, b)

    alpha, beta, link, _, ra, rb = y_segment(other_ref[...])
    near, far = choose(alpha, beta), choose(beta, alpha)
    near_src = [choose(a, b) for a, b in zip(ra, rb)]
    far_src = [choose(b, a) for a, b in zip(ra, rb)]
    leak = choose(right, left)
    src = [choose(r, l) for r, l in zip(right_src, left_src)]
    new, new_src = through(near, far, link, mid_ref[...], leak, near_src, far_src, src)
    left, right = choose(left, new), choose(new, right)
    left_src, right_src = (
        [choose(l, n) for l, n in zip(left_src, new_src)],
        [choose(n, r) for n, r in zip(new_src, right_src)],
    )
    alpha, beta, link, _, ra, rb = y_segment(own_ref[...])
    u_first, u_next = two_nodes(
        alpha + left,
        beta + right,
        link,
        [a + s for a, s in zip(ra, left_src)],
        [b + s for b, s in zip(rb, right_src)],
    )

    def keep(y, u):
        for p in range(2):
            second[y * NX + p * MX : y * NX + (p + 1) * MX, :] = u[p]

    keep(0, u_first)
    keep(NY - 1, u_next)
    for y in range(NY - 2, 0, -1):
        t = y - 1
        gd = gy_ref[t * MX : (t + 1) * MX, :]
        hd = hy_ref[t * MX : (t + 1) * MX, :]
        inv = iy_ref[t * MX : (t + 1) * MX, :]
        b = [rb_ref[t * NX + p * MX : t * NX + (p + 1) * MX, :] for p in range(2)]
        u_next = [(inv * b[p] + hd * u_first[p]) + gd * u_next[p] for p in range(2)]
        keep(y, u_next)

    even = lanes((MX, NZ)) % 2 == 0

    def turned(v, step):
        return pltpu.roll(v, step % NZ, 1)

    for n in range(MY):
        rows = slice(n * MX, (n + 1) * MX)
        inv, odd, odd_low, odd_high = zi_ref[rows, :], *(
            zo_ref[i * MX * MY + n * MX : i * MX * MY + (n + 1) * MX, :] for i in range(3)
        )
        for p in range(2):
            a, b = (second[y * NX + p * MX : y * NX + (p + 1) * MX, :] for y in (2 * n, 2 * n + 1))
            w = jnp.where(even, a, turned(b, 1))
            before = jnp.where(even, turned(a, 1), turned(b, 2))
            after = jnp.where(even, turned(a, -1), b)
            for s in range(7):
                step = 1 << s
                at = slice(s * MX * MY + n * MX, s * MX * MY + (n + 1) * MX)
                if s > 0:
                    before = turned(w, step)
                if 2 * step == NZ:
                    w = w + za_ref[at, :] * before
                else:
                    if s > 0:
                        after = turned(w, -step)
                    w = w + (za_ref[at, :] * before + zc_ref[at, :] * after)
            w = inv * w
            next_w = turned(w, -1)
            a = jnp.where(even, w, odd * a + (odd_low * turned(w, 1) + odd_high * next_w))
            b = jnp.where(even, next_w, odd * b + (odd_low * w + odd_high * turned(w, -2)))
            for y, v in ((2 * n, a), (2 * n + 1, b)):
                where = pl.ds(p * NY + y, MX, stride=2 * NY)
                out_ref[where, :] = heat_ref[y * NX + p * MX : y * NX + (p + 1) * MX, :] + v


def call(kernel, ins, outs, scratch=(), outside=False, smem=(), cost=20000, limit=8 << 20):
    space = pltpu.HBM if outside else pltpu.VMEM
    return pl.pallas_call(
        kernel,
        out_shape=tuple(jax.ShapeDtypeStruct(s, f32) for s in outs),
        in_specs=[pl.BlockSpec(memory_space=pltpu.SMEM if i in smem else space) for i in range(len(ins))],
        out_specs=tuple(pl.BlockSpec(memory_space=pltpu.VMEM) for _ in outs),
        scratch_shapes=scratch,
        compiler_params=pltpu.CompilerParams(vmem_limit_bytes=limit),
        cost_estimate=pl.CostEstimate(flops=cost, bytes_accessed=cost, transcendentals=0),
    )(*ins)


def on_device(starting_heat_state, material_zone_ids, zone_diffusivity_lookup):
    heat = starting_heat_state.reshape(NX * NY, NZ)
    ids = material_zone_ids.reshape(MX * MY, NZ // 2)
    nx, ny = lax.axis_size("gx"), lax.axis_size("gy")
    inner, outer = call(
        prepare_kernel,
        (material_zone_ids, starting_heat_state),
        [(NX + MX, NZ)] * 2,
        scratch=[
            pltpu.VMEM((MX, 1, NZ // 2), jnp.int32),
            pltpu.VMEM((MX, 1, NZ // 2), jnp.int32),
            pltpu.VMEM((NX, 1, NZ), f32),
            pltpu.VMEM((NX, 1, NZ), f32),
            pltpu.SemaphoreType.DMA((4,)),
        ],
        outside=True,
        limit=55180 << 10,
    )
    cores = [(i, i ^ 1) for i in range(ny)]
    inner = lax.ppermute(inner, "gy", cores)
    outer = lax.ppermute(outer, "gy", [(i, (i + (1 if i % 2 else -1)) % ny) for i in range(ny)])
    tx, ty = NX - 2, NY - 2
    k, lookup, gx, hx, ix, px = call(
        x_matrix_kernel,
        (ids, zone_diffusivity_lookup),
        [(MX * MY, NZ), (8, NZ)] + [(tx * MY, NZ)] * 3 + [(40, NZ)],
        scratch=[pltpu.VMEM((MX * MY, NZ), f32)],
        smem=(1,),
        cost=2000000,
    )
    send, rbx, beside = call(
        right_side_kernel,
        (heat, k, lookup, outer, inner, gx, hx, px),
        [(XROWS, NZ), (tx * NY, NZ), (2 * MX, NZ)],
    )
    near = [send] + [lax.ppermute(send, "gx", [(i, i ^ d) for i in range(nx)]) for d in (1, 2, 3)]
    gy, hy, iy, my, mid = call(
        y_matrix_kernel,
        (k, beside),
        [(ty * MX, NZ)] * 3 + [(2 * MX, NZ), (MX, NZ)],
        cost=2000000,
    )
    (half,) = call(x_half_kernel, near, [(48, NZ)])
    half = lax.ppermute(half, "gx", [(i, nx - 1 - i) for i in range(nx)])
    own, rby = call(
        x_solve_kernel,
        (*near, half, heat, rbx, gx, hx, ix, gy, hy, my),
        [(YROWS, NZ), (ty * NX, NZ)],
        scratch=[pltpu.VMEM((NX * NY, NZ), f32)],
    )
    other = lax.ppermute(own, "gy", cores)
    (chip,) = call(chip_kernel, (own, other, mid), [(YROWS, NZ)])
    chip, k = lax.optimization_barrier((chip, k))
    za, zc, zi, zo, turned = call(
        z_matrix_kernel,
        (k, heat),
        [(7 * MX * MY, NZ), (6 * MX * MY, NZ), (MX * MY, NZ), (3 * MX * MY, NZ), (NX * NY, NZ)],
        cost=4000000,
    )
    small = [chip] + [lax.ppermute(chip, "gy", [(i, i ^ (2 * d)) for i in range(ny)]) for d in (1, 2, 3)]
    (four,) = call(y_four_kernel, small, [(YROWS, NZ)])
    large = [four] + [lax.ppermute(four, "gy", [(i, i ^ (8 * d)) for i in range(ny)]) for d in (1, 2, 3)]
    (out,) = call(
        y_solve_kernel,
        (*large, *small, own, other, mid, rby, gy, hy, iy, za, zc, zi, zo, turned),
        [(NX * NY, NZ)],
        scratch=[pltpu.VMEM((NX * NY, NZ), f32)],
    )
    return out.reshape(starting_heat_state.shape)


def solution(mesh):
    return jax.shard_map(
        on_device,
        mesh=mesh,
        in_specs=(P("gx", "gy", None), P("gx", "gy", None), P()),
        out_specs=P("gx", "gy", None),
        check_vma=False,
    )
```

```python
import jax
import jax.numpy as jnp
from jax import lax
from jax.experimental import pallas as pl
from jax.experimental.pallas import tpu as pltpu
from jax.sharding import PartitionSpec as P

NX, NY, NZ = 16, 32, 128
MX, MY = NX // 2, NY // 2
XROWS = 104
YROWS = 48
f32 = jnp.float32


def lanes(shape):
    return lax.broadcasted_iota(jnp.int32, shape, 1)


def rows_of(shape):
    return lax.broadcasted_iota(jnp.int32, shape, 0)


def pack(first, second):
    return jnp.where(lanes(first.shape) % 2 == 0, first, second)


def unpack(both):
    even = lanes(both.shape) % 2 == 0
    first = jnp.where(even, both, pltpu.roll(both, 1, 1))
    second = jnp.where(even, pltpu.roll(both, NZ - 1, 1), both)
    return first, second


def through(near, far, link, beyond, leak, near_src, far_src, src):
    total = far + leak
    q = total + link
    cross = total * link
    f = beyond / ((near + beyond) * q + cross)
    new_leak = f * (near * q + cross)
    new_src = [f * (n * q + (e + s) * link) for n, e, s in zip(near_src, far_src, src)]
    return new_leak, new_src


def two_nodes(first, last, link, first_src, last_src):
    inv = 1.0 / (first * last + link * (first + last))
    low = [((last + link) * a + link * b) * inv for a, b in zip(first_src, last_src)]
    high = [((first + link) * b + link * a) * inv for a, b in zip(first_src, last_src)]
    return low, high


def eliminate(conduct, put):
    alpha = jnp.ones_like(conduct[0])
    beta = jnp.ones_like(conduct[0])
    link = conduct[0]
    for t in range(1, len(conduct)):
        g = conduct[t]
        inv = 1.0 / (link + beta + g)
        hd = link * inv
        gd = g * inv
        put(t - 1, gd, hd, inv)
        alpha = alpha + beta * hd
        link = link * gd
        beta = 1.0 + beta * gd
    return alpha, beta, link


def prepare_kernel(
    ids_hbm, heat_hbm, inner_ref, outer_ref, ids_low, ids_high, heat_low, heat_high, sems
):
    copies = [
        pltpu.make_async_copy(source, place, sems.at[i])
        for i, (source, place) in enumerate(
            (
                (heat_hbm.at[:, 0:8, :], heat_low),
                (heat_hbm.at[:, NY - 8 : NY, :], heat_high),
                (ids_hbm.at[:, 0:8, :], ids_low),
                (ids_hbm.at[:, MY - 8 : MY, :], ids_high),
            )
        )
    ]
    for copy in copies:
        copy.start()
    core = lax.rem(lax.axis_index("gy"), 2)
    inner_ref[NX:, :] = jnp.zeros((MX, NZ), f32)
    outer_ref[NX:, :] = jnp.zeros((MX, NZ), f32)
    for copy in copies:
        copy.wait()
    low, high = heat_low[:, 0, :], heat_high[:, 7, :]
    inner_ref[:NX, :] = jnp.where(core == 0, high, low)
    outer_ref[:NX, :] = jnp.where(core == 0, low, high)
    low, high = ids_low[:, 0, :], ids_high[:, 7, :]
    inner_ref[NX:, : NZ // 2] = jnp.where(core == 0, high, low).astype(f32)
    outer_ref[NX:, : NZ // 2] = jnp.where(core == 0, low, high).astype(f32)


def take(values, index):
    return jnp.take_along_axis(values, index, axis=1, mode="promise_in_bounds")


def chain(k):
    joints = []
    for m in range(len(k)):
        joints.append(2000.0 * k[m])
        if m + 1 < len(k):
            joints.append(1000.0 * (k[m] + k[m + 1]))
    return joints


def x_matrix_kernel(
    ids_ref, table_ref, k_ref, lookup_ref, gx_ref, hx_ref, ix_ref, px_ref, wide
):
    ids = ids_ref[...]
    k = jnp.zeros(ids.shape, f32)
    lookup = jnp.zeros(lookup_ref.shape, f32)
    for region in range(table_ref.shape[0]):
        k = jnp.where(ids == region, table_ref[region], k)
        lookup = jnp.where(lanes(lookup.shape) == region, table_ref[region], lookup)
    lookup_ref[...] = lookup
    wide[...] = jnp.zeros(wide.shape, f32)
    wide[:, : NZ // 2] = k
    k_ref[...] = take(wide[...], lanes(wide.shape) // 2)
    at_x = lax.axis_index("gx")
    last_x = lax.axis_size("gx") - 1
    kx = [k_ref[m * MY : (m + 1) * MY, :] for m in range(MX)]

    def put_x(t, gd, hd, inv):
        gx_ref[t * MY : (t + 1) * MY, :] = gd
        hx_ref[t * MY : (t + 1) * MY, :] = hd
        ix_ref[t * MY : (t + 1) * MY, :] = inv

    alpha, beta, link = eliminate(chain(kx), put_x)
    alpha = alpha + jnp.where(at_x == 0, 1000.0, 0.0) * kx[0]
    beta = beta + jnp.where(at_x == last_x, 1000.0, 0.0) * kx[-1]
    px_ref[0:16, :] = pack(alpha, beta)
    px_ref[16:32, :] = pack(link, kx[0])
    px_ref[32:40, :] = pack(kx[-1][:8], kx[-1][8:])


def y_matrix_kernel(k_ref, beside_ref, gy_ref, hy_ref, iy_ref, my_ref, mid_ref):
    at_y = lax.axis_index("gy")
    last_y = lax.axis_size("gy") - 1
    core = lax.rem(at_y, 2)
    ky = [k_ref[pl.ds(n, MX, stride=MY), :] for n in range(MY)]
    mid_ref[...] = 1000.0 * (beside_ref[:MX, :] + jnp.where(core == 0, ky[-1], ky[0]))
    outer = 1000.0 * (beside_ref[MX:, :] + jnp.where(core == 0, ky[0], ky[-1]))

    def put_y(t, gd, hd, inv):
        gy_ref[t * MX : (t + 1) * MX, :] = gd
        hy_ref[t * MX : (t + 1) * MX, :] = hd
        iy_ref[t * MX : (t + 1) * MX, :] = inv

    alpha, beta, link = eliminate(chain(ky), put_y)
    alpha = alpha + jnp.where(at_y == 0, 1000.0, 0.0) * ky[0]
    beta = beta + jnp.where(at_y == last_y, 1000.0, 0.0) * ky[-1]
    my_ref[0:8, :] = pack(alpha, beta)
    my_ref[8:16, :] = pack(link, outer)


def z_matrix_kernel(k_ref, heat_ref, za_ref, zc_ref, zi_ref, zo_ref, turned_ref):
    for y in range(NY):
        for p in range(2):
            turned_ref[y * NX + p * MX : y * NX + (p + 1) * MX, :] = heat_ref[
                pl.ds(p * NY + y, MX, stride=2 * NY), :
            ]
    ky = [k_ref[pl.ds(n, MX, stride=MY), :] for n in range(MY)]
    group = 16
    for start in range(0, MY, group):
        k = jnp.concatenate(ky[start : start + group], 0)
        lane = lanes(k.shape)
        west = 0.25 * (k + jnp.where(lane == 0, 0.0, pltpu.roll(k, 1, 1)))
        east = 0.25 * (k + jnp.where(lane == NZ - 1, 0.0, pltpu.roll(k, NZ - 1, 1)))
        diag = 1.0 + (west + east)
        a = jnp.where(lane == 0, 0.0, west)
        c = jnp.where(lane == NZ - 1, 0.0, east)
        size = MX * group

        def double(coefficient):
            return jnp.where(lane % 2 == 0, coefficient, pltpu.roll(coefficient, 1, 1))

        for s in range(7):
            step = 1 << s
            inv = 1.0 / diag
            if s == 0:
                for i, odd in enumerate((inv, a * inv, c * inv)):
                    at = i * MX * MY + start * MX
                    zo_ref[at : at + size, :] = odd
            low = a * pltpu.roll(inv, step, 1)
            high = c * pltpu.roll(inv, NZ - step, 1)
            at = s * MX * MY + start * MX
            if 2 * step == NZ:
                za_ref[at : at + size, :] = double(low + high)
            else:
                za_ref[at : at + size, :] = double(low)
                zc_ref[at : at + size, :] = double(high)
            diag = diag - (low * pltpu.roll(c, step, 1) + high * pltpu.roll(a, NZ - step, 1))
            a = low * pltpu.roll(a, step, 1)
            c = high * pltpu.roll(c, NZ - step, 1)
        zi_ref[start * MX : start * MX + size, :] = double(1.0 / diag)


def right_side_kernel(
    heat_ref, k_ref, lookup_ref, outer_ref, inner_ref, gx_ref, hx_ref, px_ref, send_ref, rb_ref, beside_ref
):
    at_y = lax.axis_index("gy")
    core = lax.rem(at_y, 2)

    def conduct(ref):
        index = take(ref[NX:, :], lanes((MX, NZ)) // 2).astype(jnp.int32)
        return take(lookup_ref[...], index)

    inner = jnp.concatenate([inner_ref[:NX, :], conduct(inner_ref)], 0)
    outer = jnp.concatenate([outer_ref[:NX, :], conduct(outer_ref)], 0)
    beside_ref[:MX, :] = inner[NX:]
    beside_ref[MX:, :] = outer[NX:]
    low = jnp.where(at_y == 0, 0.0, jnp.where(core == 0, outer, inner))
    high = jnp.where(at_y == lax.axis_size("gy") - 1, 0.0, jnp.where(core == 0, inner, outer))
    shape = (MY, NZ)
    lane, row = lanes(shape), rows_of(shape)
    ra = None
    rb = None
    for m in range(MX):
        k = k_ref[m * MY : (m + 1) * MY, :]
        k_low = low[NX + m : NX + m + 1]
        k_high = high[NX + m : NX + m + 1]
        face_low = 2000.0 * (k + jnp.where(row == 0, k_low, pltpu.roll(k, 1, 0)))
        face_high = 2000.0 * (k + jnp.where(row == MY - 1, k_high, pltpu.roll(k, MY - 1, 0)))
        face_mid = 4000.0 * k
        west = 0.5 * (k + jnp.where(lane == 0, 0.0, pltpu.roll(k, 1, 1)))
        east = 0.5 * (k + jnp.where(lane == NZ - 1, 0.0, pltpu.roll(k, NZ - 1, 1)))
        middle = 2.0 - (west + east)
        west = jnp.where(lane == 0, 0.0, west)
        east = jnp.where(lane == NZ - 1, 0.0, east)
        for x in (2 * m, 2 * m + 1):
            even = heat_ref[pl.ds(x * NY, MY, stride=2), :]
            odd = heat_ref[pl.ds(x * NY + 1, MY, stride=2), :]
            before = jnp.where(row == 0, low[x : x + 1], pltpu.roll(odd, 1, 0))
            after = jnp.where(row == MY - 1, high[x : x + 1], pltpu.roll(even, MY - 1, 0))
            flow = face_mid * (odd - even)
            r = []
            for v, along_y in (
                (even, flow - face_low * (even - before)),
                (odd, face_high * (after - odd) - flow),
            ):
                along_z = west * pltpu.roll(v, 1, 1) + east * pltpu.roll(v, NZ - 1, 1)
                r.append(along_y + (along_z + middle * v))
            if x == 0:
                ra = r
            elif x == 1:
                rb = r
            else:
                t = x - 2
                gd = gx_ref[t * MY : (t + 1) * MY, :]
                hd = hx_ref[t * MY : (t + 1) * MY, :]
                for q in range(2):
                    rb_ref[t * NY + q * MY : t * NY + (q + 1) * MY, :] = rb[q]
                ra = [a + b * hd for a, b in zip(ra, rb)]
                rb = [n + b * gd for n, b in zip(r, rb)]
    send_ref[0:16, :] = ra[0]
    send_ref[16:32, :] = ra[1]
    send_ref[32:48, :] = rb[0]
    send_ref[48:64, :] = rb[1]
    send_ref[64:104, :] = px_ref[...]


def x_segment(rows):
    alpha, beta = unpack(rows[64:80])
    link, k_first = unpack(rows[80:96])
    k_last = jnp.concatenate(unpack(rows[96:104]), 0)
    return alpha, beta, link, k_first, k_last, [rows[0:16], rows[16:32]], [rows[32:48], rows[48:64]]


def quarter(place, refs, segment):
    held = [r[...] for r in refs]
    segments = []
    for d in range(4):
        rows = held[0]
        for j in range(1, 4):
            rows = jnp.where(place == d ^ j, held[j], rows)
        segments.append(segment(rows))
    return segments


def x_half_kernel(own_ref, one_ref, two_ref, three_ref, send_ref):
    at = lax.axis_index("gx")
    upper = at >= 4
    place = lax.rem(at, 4)
    place = jnp.where(upper, 3 - place, place)

    def turn(segment):
        alpha, beta, link, k_first, k_last, ra, rb = segment

        def pick(a, b):
            return jnp.where(upper, a, b)

        near, far = pick(alpha, beta), pick(beta, alpha)
        k_near, k_far = pick(k_first, k_last), pick(k_last, k_first)
        near_src = [pick(a, b) for a, b in zip(ra, rb)]
        far_src = [pick(b, a) for a, b in zip(ra, rb)]
        return near, far, link, k_near, k_far, near_src, far_src

    segments = [turn(g) for g in quarter(place, (own_ref, one_ref, two_ref, three_ref), x_segment)]
    zero = jnp.zeros((MY, NZ), f32)
    leak, src = zero, [zero, zero]
    for d in range(3):
        near, far, link, k_near, _, near_src, far_src = segments[d]
        joint = 1000.0 * (k_near + segments[d + 1][4])
        leak, src = through(near, far, link, joint, leak, near_src, far_src, src)
    near, far, link, k_near, _, near_src, far_src = segments[3]
    total = far + leak
    part = link / (total + link)
    send_ref[0:16, :] = near_src[0] + (far_src[0] + src[0]) * part
    send_ref[16:32, :] = near_src[1] + (far_src[1] + src[1]) * part
    send_ref[32:48, :] = pack(near + total * part, k_near)


def x_solve_kernel(
    own_ref, one_ref, two_ref, three_ref, half_ref, heat_ref, rb_ref, gx_ref, hx_ref, ix_ref, gy_ref, hy_ref,
    my_ref, core_ref, rby_ref, first,
):
    at = lax.axis_index("gx")
    place = lax.rem(at, 4)
    segments = quarter(place, (own_ref, one_ref, two_ref, three_ref), x_segment)
    half_leak, half_k = unpack(half_ref[32:48, :])
    upper = at >= 4
    joint = 1000.0 * (half_k + jnp.where(upper, segments[0][3], segments[3][4]))
    part = joint / (half_leak + joint)
    half_leak = half_leak * part
    half_src = [half_ref[0:16, :] * part, half_ref[16:32, :] * part]
    left = jnp.where(upper, half_leak, 0.0)
    left_src = [jnp.where(upper, v, 0.0) for v in half_src]
    right = jnp.where(upper, 0.0, half_leak)
    right_src = [jnp.where(upper, 0.0, v) for v in half_src]
    joints = [1000.0 * (segments[d][4] + segments[d + 1][3]) for d in range(3)]
    for step in range(3):
        d = step
        alpha, beta, link, _, _, ra, rb = segments[d]
        new, new_src = through(beta, alpha, link, joints[d], left, rb, ra, left_src)
        left = jnp.where(d < place, new, left)
        left_src = [jnp.where(d < place, n, o) for n, o in zip(new_src, left_src)]
        d = 3 - step
        alpha, beta, link, _, _, ra, rb = segments[d]
        new, new_src = through(alpha, beta, link, joints[d - 1], right, ra, rb, right_src)
        right = jnp.where(d > place, new, right)
        right_src = [jnp.where(d > place, n, o) for n, o in zip(new_src, right_src)]
    alpha, beta, link, _, _, ra, rb = x_segment(own_ref[...])
    u_first, u_next = two_nodes(
        alpha + left,
        beta + right,
        link,
        [a + s for a, s in zip(ra, left_src)],
        [b + s for b, s in zip(rb, right_src)],
    )

    def keep(x, u):
        for q in range(2):
            heat = heat_ref[pl.ds(x * NY + q, MY, stride=2), :]
            first[x * NY + q * MY : x * NY + (q + 1) * MY, :] = u[q] - 2.0 * heat

    keep(0, u_first)
    keep(NX - 1, u_next)
    for x in range(NX - 2, 0, -1):
        t = x - 1
        gd = gx_ref[t * MY : (t + 1) * MY, :]
        hd = hx_ref[t * MY : (t + 1) * MY, :]
        inv = ix_ref[t * MY : (t + 1) * MY, :]
        b = [rb_ref[t * NY + q * MY : t * NY + (q + 1) * MY, :] for q in range(2)]
        u_next = [(inv * b[q] + hd * u_first[q]) + gd * u_next[q] for q in range(2)]
        keep(x, u_next)

    def side(y):
        start = (y % 2) * MY + y // 2
        return [first[pl.ds(p * NY + start, MX, stride=2 * NY), :] for p in range(2)]

    ra = side(0)
    rb = side(1)
    for t in range(NY - 2):
        gd = gy_ref[t * MX : (t + 1) * MX, :]
        hd = hy_ref[t * MX : (t + 1) * MX, :]
        for p in range(2):
            rby_ref[t * NX + p * MX : t * NX + (p + 1) * MX, :] = rb[p]
        new = side(t + 2)
        ra = [a + b * hd for a, b in zip(ra, rb)]
        rb = [n + b * gd for n, b in zip(new, rb)]
    core_ref[0:8, :] = ra[0]
    core_ref[8:16, :] = ra[1]
    core_ref[16:24, :] = rb[0]
    core_ref[24:32, :] = rb[1]
    core_ref[32:48, :] = my_ref[...]


def y_segment(rows):
    alpha, beta = unpack(rows[32:40])
    link, joint = unpack(rows[40:48])
    return alpha, beta, link, joint, [rows[0:8], rows[8:16]], [rows[16:24], rows[24:32]]


def merge(first, second, joint):
    a0, b0, h0, outer, ra0, rb0 = first
    a1, b1, h1, _, ra1, rb1 = second
    inv = 1.0 / (h0 + b0 + joint)
    hd, gd = h0 * inv, joint * inv
    alpha = a0 + b0 * hd
    link = h0 * gd
    between = a1 + b0 * gd
    ra = [a + b * hd for a, b in zip(ra0, rb0)]
    rm = [a + b * gd for a, b in zip(ra1, rb0)]
    inv = 1.0 / (link + between + h1)
    hd, gd = link * inv, h1 * inv
    alpha = alpha + between * hd
    beta = b1 + between * gd
    ra = [a + m * hd for a, m in zip(ra, rm)]
    rb = [b + m * gd for b, m in zip(rb1, rm)]
    return alpha, beta, link * gd, outer, ra, rb


def store_segment(ref, segment):
    alpha, beta, link, joint, ra, rb = segment
    ref[...] = jnp.concatenate([*ra, *rb, pack(alpha, beta), pack(link, joint)], 0)


def chip_kernel(own_ref, other_ref, mid_ref, send_ref):
    core = lax.rem(lax.axis_index("gy"), 2)
    own, other = own_ref[...], other_ref[...]
    first = y_segment(jnp.where(core == 0, own, other))
    second = y_segment(jnp.where(core == 0, other, own))
    store_segment(send_ref, merge(first, second, mid_ref[...]))


def y_four_kernel(own_ref, one_ref, two_ref, three_ref, send_ref):
    place = lax.rem(lax.div(lax.axis_index("gy"), 2), 4)
    a, b, c, d = quarter(place, (own_ref, one_ref, two_ref, three_ref), y_segment)
    store_segment(send_ref, merge(merge(a, b, b[3]), merge(c, d, d[3]), c[3]))


def y_sweeps(segments, place, left, left_src, right, right_src):
    for step in range(3):
        d = step
        alpha, beta, link, _, ra, rb = segments[d]
        new, new_src = through(beta, alpha, link, segments[d + 1][3], left, rb, ra, left_src)
        left = jnp.where(d < place, new, left)
        left_src = [jnp.where(d < place, n, o) for n, o in zip(new_src, left_src)]
        d = 3 - step
        alpha, beta, link, joint, ra, rb = segments[d]
        new, new_src = through(alpha, beta, link, joint, right, ra, rb, right_src)
        right = jnp.where(d > place, new, right)
        right_src = [jnp.where(d > place, n, o) for n, o in zip(new_src, right_src)]
    return left, left_src, right, right_src


def y_solve_kernel(
    large0, large1, large2, large3, small0, small1, small2, small3, own_ref, other_ref, mid_ref, rb_ref, gy_ref,
    hy_ref, iy_ref, za_ref, zc_ref, zi_ref, zo_ref, heat_ref, out_ref, second,
):
    at_y = lax.axis_index("gy")
    core, chip = lax.rem(at_y, 2), lax.div(at_y, 2)
    zero = jnp.zeros((MX, NZ), f32)
    large = quarter(lax.div(chip, 4), (large0, large1, large2, large3), y_segment)
    small = quarter(lax.rem(chip, 4), (small0, small1, small2, small3), y_segment)
    state = y_sweeps(large, lax.div(chip, 4), zero, [zero, zero], zero, [zero, zero])
    left, left_src, right, right_src = y_sweeps(small, lax.rem(chip, 4), *state)

    def choose(a, b):
        return jnp.where(core == 0, a, b)

    alpha, beta, link, _, ra, rb = y_segment(other_ref[...])
    near, far = choose(alpha, beta), choose(beta, alpha)
    near_src = [choose(a, b) for a, b in zip(ra, rb)]
    far_src = [choose(b, a) for a, b in zip(ra, rb)]
    leak = choose(right, left)
    src = [choose(r, l) for r, l in zip(right_src, left_src)]
    new, new_src = through(near, far, link, mid_ref[...], leak, near_src, far_src, src)
    left, right = choose(left, new), choose(new, right)
    left_src, right_src = (
        [choose(l, n) for l, n in zip(left_src, new_src)],
        [choose(n, r) for n, r in zip(new_src, right_src)],
    )
    alpha, beta, link, _, ra, rb = y_segment(own_ref[...])
    u_first, u_next = two_nodes(
        alpha + left,
        beta + right,
        link,
        [a + s for a, s in zip(ra, left_src)],
        [b + s for b, s in zip(rb, right_src)],
    )

    def keep(y, u):
        for p in range(2):
            second[y * NX + p * MX : y * NX + (p + 1) * MX, :] = u[p]

    keep(0, u_first)
    keep(NY - 1, u_next)
    for y in range(NY - 2, 0, -1):
        t = y - 1
        gd = gy_ref[t * MX : (t + 1) * MX, :]
        hd = hy_ref[t * MX : (t + 1) * MX, :]
        inv = iy_ref[t * MX : (t + 1) * MX, :]
        b = [rb_ref[t * NX + p * MX : t * NX + (p + 1) * MX, :] for p in range(2)]
        u_next = [(inv * b[p] + hd * u_first[p]) + gd * u_next[p] for p in range(2)]
        keep(y, u_next)

    even = lanes((MX, NZ)) % 2 == 0

    def turned(v, step):
        return pltpu.roll(v, step % NZ, 1)

    for n in range(MY):
        rows = slice(n * MX, (n + 1) * MX)
        inv, odd, odd_low, odd_high = zi_ref[rows, :], *(
            zo_ref[i * MX * MY + n * MX : i * MX * MY + (n + 1) * MX, :] for i in range(3)
        )
        for p in range(2):
            a, b = (second[y * NX + p * MX : y * NX + (p + 1) * MX, :] for y in (2 * n, 2 * n + 1))
            w = jnp.where(even, a, turned(b, 1))
            before = jnp.where(even, turned(a, 1), turned(b, 2))
            after = jnp.where(even, turned(a, -1), b)
            for s in range(7):
                step = 1 << s
                at = slice(s * MX * MY + n * MX, s * MX * MY + (n + 1) * MX)
                if s > 0:
                    before = turned(w, step)
                if 2 * step == NZ:
                    w = w + za_ref[at, :] * before
                else:
                    if s > 0:
                        after = turned(w, -step)
                    w = w + (za_ref[at, :] * before + zc_ref[at, :] * after)
            w = inv * w
            next_w = turned(w, -1)
            a = jnp.where(even, w, odd * a + (odd_low * turned(w, 1) + odd_high * next_w))
            b = jnp.where(even, next_w, odd * b + (odd_low * w + odd_high * turned(w, -2)))
            for y, v in ((2 * n, a), (2 * n + 1, b)):
                where = pl.ds(p * NY + y, MX, stride=2 * NY)
                out_ref[where, :] = heat_ref[y * NX + p * MX : y * NX + (p + 1) * MX, :] + v


def call(kernel, ins, outs, scratch=(), outside=False, smem=(), cost=20000, limit=8 << 20):
    space = pltpu.HBM if outside else pltpu.VMEM
    return pl.pallas_call(
        kernel,
        out_shape=tuple(jax.ShapeDtypeStruct(s, f32) for s in outs),
        in_specs=[pl.BlockSpec(memory_space=pltpu.SMEM if i in smem else space) for i in range(len(ins))],
        out_specs=tuple(pl.BlockSpec(memory_space=pltpu.VMEM) for _ in outs),
        scratch_shapes=scratch,
        compiler_params=pltpu.CompilerParams(vmem_limit_bytes=limit),
        cost_estimate=pl.CostEstimate(flops=cost, bytes_accessed=cost, transcendentals=0),
    )(*ins)


def on_device(starting_heat_state, material_zone_ids, zone_diffusivity_lookup):
    heat = starting_heat_state.reshape(NX * NY, NZ)
    ids = material_zone_ids.reshape(MX * MY, NZ // 2)
    nx, ny = lax.axis_size("gx"), lax.axis_size("gy")
    inner, outer = call(
        prepare_kernel,
        (material_zone_ids, starting_heat_state),
        [(NX + MX, NZ)] * 2,
        scratch=[
            pltpu.VMEM((MX, 8, NZ // 2), jnp.int32),
            pltpu.VMEM((MX, 8, NZ // 2), jnp.int32),
            pltpu.VMEM((NX, 8, NZ), f32),
            pltpu.VMEM((NX, 8, NZ), f32),
            pltpu.SemaphoreType.DMA((4,)),
        ],
        outside=True,
        limit=55180 << 10,
    )
    cores = [(i, i ^ 1) for i in range(ny)]
    inner = lax.ppermute(inner, "gy", cores)
    outer = lax.ppermute(outer, "gy", [(i, (i + (1 if i % 2 else -1)) % ny) for i in range(ny)])
    tx, ty = NX - 2, NY - 2
    k, lookup, gx, hx, ix, px = call(
        x_matrix_kernel,
        (ids, zone_diffusivity_lookup),
        [(MX * MY, NZ), (8, NZ)] + [(tx * MY, NZ)] * 3 + [(40, NZ)],
        scratch=[pltpu.VMEM((MX * MY, NZ), f32)],
        smem=(1,),
        cost=2000000,
    )
    send, rbx, beside = call(
        right_side_kernel,
        (heat, k, lookup, outer, inner, gx, hx, px),
        [(XROWS, NZ), (tx * NY, NZ), (2 * MX, NZ)],
    )
    near = [send] + [lax.ppermute(send, "gx", [(i, i ^ d) for i in range(nx)]) for d in (1, 2, 3)]
    gy, hy, iy, my, mid = call(
        y_matrix_kernel,
        (k, beside),
        [(ty * MX, NZ)] * 3 + [(2 * MX, NZ), (MX, NZ)],
        cost=2000000,
    )
    (half,) = call(x_half_kernel, near, [(48, NZ)])
    half = lax.ppermute(half, "gx", [(i, nx - 1 - i) for i in range(nx)])
    own, rby = call(
        x_solve_kernel,
        (*near, half, heat, rbx, gx, hx, ix, gy, hy, my),
        [(YROWS, NZ), (ty * NX, NZ)],
        scratch=[pltpu.VMEM((NX * NY, NZ), f32)],
    )
    other = lax.ppermute(own, "gy", cores)
    (chip,) = call(chip_kernel, (own, other, mid), [(YROWS, NZ)])
    chip, k = lax.optimization_barrier((chip, k))
    za, zc, zi, zo, turned = call(
        z_matrix_kernel,
        (k, heat),
        [(7 * MX * MY, NZ), (6 * MX * MY, NZ), (MX * MY, NZ), (3 * MX * MY, NZ), (NX * NY, NZ)],
        cost=4000000,
    )
    small = [chip] + [lax.ppermute(chip, "gy", [(i, i ^ (2 * d)) for i in range(ny)]) for d in (1, 2, 3)]
    (four,) = call(y_four_kernel, small, [(YROWS, NZ)])
    large = [four] + [lax.ppermute(four, "gy", [(i, i ^ (8 * d)) for i in range(ny)]) for d in (1, 2, 3)]
    (out,) = call(
        y_solve_kernel,
        (*large, *small, own, other, mid, rby, gy, hy, iy, za, zc, zi, zo, turned),
        [(NX * NY, NZ)],
        scratch=[pltpu.VMEM((NX * NY, NZ), f32)],
    )
    return out.reshape(starting_heat_state.shape)


def solution(mesh):
    return jax.shard_map(
        on_device,
        mesh=mesh,
        in_specs=(P("gx", "gy", None), P("gx", "gy", None), P()),
        out_specs=P("gx", "gy", None),
        check_vma=False,
    )
```
